32 devices in a mesh: batch: 4 (over y, x), fsdp: 8 (over z, core).
Axes of the slice: x: 2, y: 2, z: 4, core: 2. Of those that a mesh axis runs over, the one named last changes fastest.
Arguments:
- x_small: bfloat16 [64, 10, 10, 256], P(('batch', 'fsdp')), may hold values from -6 to 6
- x_mid: bfloat16 [64, 14, 14, 256], P(('batch', 'fsdp')), may hold values from -6 to 6
- x_large: bfloat16 [64, 18, 18, 256], P(('batch', 'fsdp')), may hold values from -6 to 6
- cot_small: bfloat16 [64, 5, 5, 512], P(('batch', 'fsdp')), may hold values from -6 to 6
- cot_mid: bfloat16 [64, 7, 7, 512], P(('batch', 'fsdp')), may hold values from -6 to 6
- cot_large: bfloat16 [64, 9, 9, 512], P(('batch', 'fsdp')), may hold values from -6 to 6
- counts: int32 [32, 3], P(('batch', 'fsdp')), may hold values from 1 to 2, as said below
- w_first: bfloat16 [3, 3, 256, 512], P(None, None, None, 'fsdp'), may hold values from -0.125 to 0.125
- gain_first: bfloat16 [512], P('fsdp'), may hold values from 0.5 to 1.5
- shift_first: bfloat16 [512], P('fsdp'), may hold values from -3 to 3
- w_second: bfloat16 [3, 3, 512, 512], P(None, None, None, 'fsdp'), may hold values from -0.09375 to 0.09375
- gain_second: bfloat16 [512], P('fsdp'), may hold values from 0.5 to 1.5
- shift_second: bfloat16 [512], P('fsdp'), may hold values from -3 to 3
- w_short: bfloat16 [256, 512], P(None, 'fsdp'), may hold values from -0.375 to 0.375
- gain_short: bfloat16 [512], P('fsdp'), may hold values from 0.5 to 1.5
- shift_short: bfloat16 [512], P('fsdp'), may hold values from -3 to 3
Outputs:
- out_small: bfloat16 [64, 5, 5, 512], P(('batch', 'fsdp'))
- out_mid: bfloat16 [64, 7, 7, 512], P(('batch', 'fsdp'))
- out_large: bfloat16 [64, 9, 9, 512], P(('batch', 'fsdp'))
- dx_small: bfloat16 [64, 10, 10, 256], P(('batch', 'fsdp'))
- dx_mid: bfloat16 [64, 14, 14, 256], P(('batch', 'fsdp'))
- dx_large: bfloat16 [64, 18, 18, 256], P(('batch', 'fsdp'))
- grad_w_first: float32 [3, 3, 256, 512], P(None, None, None, 'fsdp')
- grad_gain_first: float32 [512], P('fsdp')
- grad_shift_first: float32 [512], P('fsdp')
- grad_w_second: float32 [3, 3, 512, 512], P(None, None, None, 'fsdp')
- grad_gain_second: float32 [512], P('fsdp')
- grad_shift_second: float32 [512], P('fsdp')
- grad_w_short: float32 [256, 512], P(None, 'fsdp')
- grad_gain_short: float32 [512], P('fsdp')
- grad_shift_short: float32 [512], P('fsdp')
The draws below stay inside these ranges and needn't reach their ends.
Inputs may be any that keep to these rules, and one draw needn't show every extreme that they name: counts[d, g] live slots of device d in group g come first among its 2 slots; some device has 2 in some group and another 1.
All inputs are finite; a program needn't handle non-finite values.
Results may differ from the reference program's by a relative error of at most 0.0095.
Values may be sent and summed in bfloat16 or wider, within the bound.
No kernel may reach another device: no remote copies, remote signals or barrier semaphores. Data moves between devices by JAX's collectives and lax.ppermute only.
A program may use at most 128 MiB of HBM per device.

```python
import jax
import jax.numpy as jnp
from jax import lax

C_IN = 256
C_OUT = 512
SLOTS = 2
HS = 10
HM = 14
HL = 18
OS = 5
OM = 7
OL = 9
IMAGES = 64


def draw_counts(key, part):
    key = jax.random.fold_in(key, 7)
    device_count = IMAGES // SLOTS
    fewest = max(1, SLOTS // 2)
    key_base, key_full, key_other, key_group = jax.random.split(key, 4)
    drawn = jax.random.randint(key_base, (device_count, 3), fewest, SLOTS + 1, dtype=jnp.int32)
    full_device = jax.random.randint(key_full, (), 0, device_count, dtype=jnp.int32)
    other_device = (full_device + 1 + jax.random.randint(key_other, (), 0, device_count - 1, dtype=jnp.int32)) % device_count
    chosen_group = jax.random.randint(key_group, (), 0, 3, dtype=jnp.int32)
    row_index = jnp.arange(device_count, dtype=jnp.int32)[:, None]
    col_index = jnp.arange(3, dtype=jnp.int32)[None, :]
    drawn = jnp.where((row_index == full_device) & (col_index == chosen_group), SLOTS, drawn)
    drawn = jnp.where((row_index == other_device) & (col_index == chosen_group), fewest, drawn)
    return drawn.astype(jnp.int32)


def levels(stream_key, shape, cuts, low, top_value):
    loudness, own = 1.0, jax.random.fold_in(stream_key, 6)
    for dim, shards_of in cuts:
        steps = jnp.exp(jax.random.uniform(jax.random.fold_in(own, dim), (shards_of,), jnp.float32, low / len(cuts), top_value / len(cuts)))
        loudness = loudness * jnp.repeat(steps, shape[dim] // shards_of).reshape([-1 if axis == dim else 1 for axis in range(len(shape))])
    return loudness


def gaussian(own_key, extent, scale, limit, cuts=(), kind=jnp.bfloat16):
    array = scale * jax.random.normal(own_key, extent, jnp.float32)
    if cuts:
        array = array * levels(own_key, extent, cuts, -0.22, 0.18)
    return jnp.clip(array, -limit, limit).astype(kind)


def setup_inputs(seed: int = 0) -> dict:
    splits = jax.random.split(jax.random.key(seed), 17)
    x_small = gaussian(splits[0], (IMAGES, HS, HS, C_IN), 1.0, 6.0, ((0, 32),))
    x_mid = gaussian(splits[1], (IMAGES, HM, HM, C_IN), 1.0, 6.0, ((0, 32),))
    x_large = gaussian(splits[2], (IMAGES, HL, HL, C_IN), 1.0, 6.0, ((0, 32),))
    cot_small = gaussian(splits[3], (IMAGES, OS, OS, C_OUT), 1.0, 6.0, ((0, 32),))
    cot_mid = gaussian(splits[4], (IMAGES, OM, OM, C_OUT), 1.0, 6.0, ((0, 32),))
    cot_large = gaussian(splits[5], (IMAGES, OL, OL, C_OUT), 1.0, 6.0, ((0, 32),))
    counts = draw_counts(jax.random.fold_in(splits[16], 71), 0)
    w_first = gaussian(splits[7], (3, 3, C_IN, C_OUT), (9 * C_IN) ** -0.5, 0.125, ((3, 8),))
    gain_first = jnp.clip(1.0 + 0.1 * jax.random.normal(splits[8], (C_OUT,), jnp.float32), 0.5, 1.5).astype(jnp.bfloat16)
    shift_first = gaussian(splits[9], (C_OUT,), 0.5, 3.0, ((0, 8),))
    w_second = gaussian(splits[10], (3, 3, C_OUT, C_OUT), (9 * C_OUT) ** -0.5, 0.09375, ((3, 8),))
    gain_second = jnp.clip(1.0 + 0.1 * jax.random.normal(splits[11], (C_OUT,), jnp.float32), 0.5, 1.5).astype(jnp.bfloat16)
    shift_second = gaussian(splits[12], (C_OUT,), 0.5, 3.0, ((0, 8),))
    w_short = gaussian(splits[13], (C_IN, C_OUT), C_IN ** -0.5, 0.375, ((1, 8),))
    gain_short = jnp.clip(1.0 + 0.1 * jax.random.normal(splits[14], (C_OUT,), jnp.float32), 0.5, 1.5).astype(jnp.bfloat16)
    shift_short = gaussian(splits[15], (C_OUT,), 0.5, 3.0, ((0, 8),))
    return dict(x_small=x_small, x_mid=x_mid, x_large=x_large, cot_small=cot_small, cot_mid=cot_mid, cot_large=cot_large, counts=counts, w_first=w_first, gain_first=gain_first, shift_first=shift_first, w_second=w_second, gain_second=gain_second, shift_second=shift_second, w_short=w_short, gain_short=gain_short, shift_short=shift_short)


EPSILON = 1e-05

@jax.custom_vjp
def low(v):
    return lax.optimization_barrier(v.astype(jnp.bfloat16)).astype(jnp.float32)

@jax.custom_vjp
def low_back(v):
    return v

def low_keep(v):
    return (low(v), None)

def low_pass(kept, grad):
    return (grad,)

def back_keep(v):
    return (v, None)

def back_low(kept, grad):
    return (low(grad),)
low.defvjp(low_keep, low_pass)
low_back.defvjp(back_keep, back_low)

def convolve(field, kernel, stride, margin):
    return lax.conv_general_dilated(field, kernel, (stride, stride), ((margin, margin), (margin, margin)), dimension_numbers=('NHWC', 'HWIO', 'NHWC'), precision=lax.Precision.HIGHEST)

def slot_live(counts, group, images):
    index = jnp.arange(images, dtype=jnp.int32)
    owner = index // SLOTS
    return (index % SLOTS < counts[owner, group]).astype(jnp.float32)

def normalize(parts, masks, total, gain, shift):
    first = sum((lax.optimization_barrier(jnp.sum(mask_one[:, None, None, None] * value, axis=(0, 1, 2))) for value, mask_one in zip(parts, masks)))
    second = sum((lax.optimization_barrier(jnp.sum(mask_one[:, None, None, None] * value * value, axis=(0, 1, 2))) for value, mask_one in zip(parts, masks)))
    center = first / total
    spread = second / total - center * center
    factor = lax.rsqrt(spread + EPSILON)
    return [(value - center) * factor * gain + shift for value in parts]

def reference(x_small, x_mid, x_large, cot_small, cot_mid, cot_large, counts, w_first, gain_first, shift_first, w_second, gain_second, shift_second, w_short, gain_short, shift_short):
    images = x_small.shape[0]
    masks = [slot_live(counts, group, images) for group in range(3)]
    fields = tuple((value.astype(jnp.float32) for value in (x_small, x_mid, x_large)))
    total = sum((jnp.sum(mask_one) * float(((value.shape[1] + 1) // 2) ** 2) for value, mask_one in zip(fields, masks)))
    params = tuple((value.astype(jnp.float32) for value in (w_first, gain_first, shift_first, w_second, gain_second, shift_second, w_short, gain_short, shift_short)))

    def forward(inputs, weights):
        short_kernel = weights[6].reshape(1, 1, weights[6].shape[0], weights[6].shape[1])
        first = [low_back(convolve(value, weights[0], 2, 1)) for value in inputs]
        short = [low_back(convolve(value, short_kernel, 2, 0)) for value in inputs]
        hidden = [low(jax.nn.silu(value)) for value in normalize(first, masks, total, weights[1], weights[2])]
        second = [low_back(convolve(value, weights[3], 1, 1)) for value in hidden]
        main_path = normalize(second, masks, total, weights[4], weights[5])
        side_path = normalize(short, masks, total, weights[7], weights[8])
        return tuple((jax.nn.silu(left + right) * mask_one[:, None, None, None] for left, right, mask_one in zip(main_path, side_path, masks)))
    outputs, pullback = jax.vjp(forward, fields, params)
    cotangent = tuple((value.astype(jnp.float32) for value in (cot_small, cot_mid, cot_large)))
    grad_fields, grad_params = pullback(cotangent)
    return (outputs[0].astype(jnp.bfloat16), outputs[1].astype(jnp.bfloat16), outputs[2].astype(jnp.bfloat16), grad_fields[0].astype(jnp.bfloat16), grad_fields[1].astype(jnp.bfloat16), grad_fields[2].astype(jnp.bfloat16), grad_params[0], grad_params[1], grad_params[2], grad_params[3], grad_params[4], grad_params[5], grad_params[6], grad_params[7], grad_params[8])
```

```python
import functools

import jax
import jax.numpy as jnp
import numpy as np
from jax import lax
from jax.experimental import pallas as pl
from jax.experimental.pallas import tpu as pltpu
from jax.sharding import PartitionSpec as P

EPSILON = 1e-05
F32 = jnp.float32
BF16 = jnp.bfloat16
ROWS = 16
VMEM_LIMIT = 56 * 2**20


def up(value, step):
    return -(-value // step) * step


class Plan:
    def __init__(self, sides, slots):
        self.sides, self.slots = sides, slots
        self.starts, self.sizes, row = [], [], 0
        for index, side in enumerate(sides):
            width = side + 1
            after = sides[index + 1] + 1 if index + 1 < len(sides) else 0
            size = up(slots * (width * width + max(0, width + 1 - after)), ROWS)
            self.starts.append(row)
            self.sizes.append(size)
            row += size
        self.rows = row
        self.margin = up(slots * (max(sides) + 2), ROWS)
        self.span = self.rows + 2 * self.margin

    def segments(self):
        return list(zip(self.starts, self.sizes, [side + 1 for side in self.sides]))


def cells(plan, group, value):
    slots, side = value.shape[0], value.shape[1]
    value = jnp.pad(jnp.transpose(value, (1, 2, 0, 3)), ((1, 0), (1, 0), (0, 0), (0, 0)))
    value = value.reshape((side + 1) * (side + 1) * slots, value.shape[3])
    return jnp.pad(value, ((0, plan.sizes[group] - value.shape[0]), (0, 0)))


def images(plan, group, rows):
    side, slots = plan.sides[group], plan.slots
    start, count = plan.starts[group], (side + 1) * (side + 1) * slots
    value = rows[start : start + count].reshape(side + 1, side + 1, slots, rows.shape[1])
    return jnp.transpose(value[1:, 1:], (2, 0, 1, 3))


def nn(left, right):
    return lax.dot_general(left, right, (((1,), (0,)), ((), ())), preferred_element_type=F32)


def nt(left, right):
    return lax.dot_general(left, right, (((1,), (1,)), ((), ())), preferred_element_type=F32)


def column(value):
    return jnp.sum(value, axis=0, keepdims=True)


def wide(mask_ref, channels):
    return jnp.concatenate([mask_ref[...]] * (channels // mask_ref.shape[1]), axis=1)


def silu_slope(value):
    gate = jax.nn.sigmoid(value)
    return gate * (1.0 + value * (1.0 - gate))


def norm(value, sums, row, total):
    center = sums[row : row + 1] / total
    spread = sums[row + 1 : row + 2] / total - center * center
    factor = lax.rsqrt(spread + EPSILON)
    return (value - center) * factor, factor


def put_rows(ref, rows):
    for index, row in enumerate(rows):
        ref[index : index + 1, :] = row
    ref[len(rows) :, :] = jnp.zeros((ref.shape[0] - len(rows), ref.shape[1]), F32)


def offsets(plan, width):
    return [plan.slots * (dy * width + dx) for dy in (-1, 0, 1) for dx in (-1, 0, 1)]


def unfold(plan, padded_ref, out_ref, sign):
    channels = padded_ref.shape[1]
    for start, size, width in plan.segments():
        for tap, offset in enumerate(offsets(plan, width)):
            first = plan.margin + start + sign * offset
            out_ref[start : start + size, tap * channels : (tap + 1) * channels] = padded_ref[
                first : first + size, :
            ].astype(BF16)


def fill(plan, padded_ref, value):
    edge = jnp.zeros((plan.margin, padded_ref.shape[1]), F32)
    padded_ref[: plan.margin, :] = edge
    padded_ref[plan.margin : plan.margin + plan.rows, :] = value
    padded_ref[plan.margin + plan.rows :, :] = edge


def patches_kernel(plan, planes_ref, out_ref, held_ref):
    channels = planes_ref.shape[2]
    held_ref[...] = planes_ref[...].astype(F32)
    for start, size, width in plan.segments():
        for ky in range(3):
            for kx in range(3):
                tap = ky * 3 + kx
                shift = plan.slots * (width * (ky == 0) + (kx == 0))
                first = plan.margin + start - shift
                out_ref[start : start + size, tap * channels : (tap + 1) * channels] = held_ref[
                    2 * (ky != 1) + (kx != 1), first : first + size, :
                ].astype(BF16)


def first_kernel(patches_ref, weights_ref, mask_ref, first_ref, side_ref, sums_ref):
    cin = weights_ref.shape[2]
    cout = weights_ref.shape[1]
    total = nt(patches_ref[:, :cin], weights_ref[0])
    for tap in range(1, 9):
        total += nt(patches_ref[:, tap * cin : (tap + 1) * cin], weights_ref[tap])
    side = nt(patches_ref[:, 4 * cin : 5 * cin], weights_ref[9])
    first_ref[...] = total
    side_ref[...] = side
    mask = wide(mask_ref, cout)
    put_rows(
        sums_ref,
        [
            column(mask * total),
            column(mask * total * total),
            column(mask * side),
            column(mask * side * side),
            column(mask),
        ],
    )


def second_kernel(plan, sums_ref, first_ref, mask_ref, vec_ref, weights_ref, second_ref, patches_ref, out_ref, held_ref):
    cout = first_ref.shape[1]
    mask = wide(mask_ref, cout)
    sums = sums_ref[...]
    normed, _ = norm(first_ref[...], sums, 0, sums[4:5])
    pre = normed * vec_ref[0:1] + vec_ref[1:2]
    fill(plan, held_ref, jax.nn.silu(pre) * mask)
    unfold(plan, held_ref, patches_ref, 1)
    total = nt(patches_ref[:, :cout], weights_ref[0])
    for tap in range(1, 9):
        total += nt(patches_ref[:, tap * cout : (tap + 1) * cout], weights_ref[tap])
    second_ref[...] = total
    put_rows(out_ref, [column(mask * total), column(mask * total * total)])


def output_kernel(sums_ref, sums_two_ref, second_ref, side_ref, cot_ref, mask_ref, vec_ref, out_ref, dz_ref, sums_out_ref):
    cout = second_ref.shape[1]
    mask = wide(mask_ref, cout)
    sums = sums_ref[...]
    total = sums[4:5]
    normed_two, _ = norm(second_ref[...], sums_two_ref[...], 0, total)
    normed_side, _ = norm(side_ref[...], sums, 2, total)
    value = (normed_two * vec_ref[2:3] + vec_ref[3:4]) + (normed_side * vec_ref[4:5] + vec_ref[5:6])
    gate = jax.nn.sigmoid(value)
    out_ref[...] = (value * gate * mask).astype(BF16)
    grad = cot_ref[...].astype(F32) * mask * (gate * (1.0 + value * (1.0 - gate)))
    dz_ref[...] = grad
    put_rows(sums_out_ref, [column(grad), column(grad * normed_two), column(grad * normed_side)])


def back_second_kernel(
    plan, sums_ref, sums_two_ref, sums_z_ref, first_ref, second_ref, side_ref, dz_ref, mask_ref, vec_ref, weights_ref,
    grad_two_ref, grad_side_ref, dy_ref, out_ref, held_ref, patches_ref,
):
    cout = first_ref.shape[1]
    mask = wide(mask_ref, cout)
    sums, sums_z = sums_ref[...], sums_z_ref[...]
    total = sums[4:5]
    grad = dz_ref[...]
    normed, factor = norm(second_ref[...], sums_two_ref[...], 0, total)
    two = vec_ref[2:3] * factor * (grad - mask * (sums_z[0:1] + normed * sums_z[1:2]) / total)
    normed, factor = norm(side_ref[...], sums, 2, total)
    side = vec_ref[4:5] * factor * (grad - mask * (sums_z[0:1] + normed * sums_z[2:3]) / total)
    grad_side_ref[...] = side.astype(BF16)
    grad_two_ref[...] = two.astype(BF16)
    fill(plan, held_ref, two)
    unfold(plan, held_ref, patches_ref, -1)
    back = nn(patches_ref[:, :cout], weights_ref[0])
    for tap in range(1, 9):
        back += nn(patches_ref[:, tap * cout : (tap + 1) * cout], weights_ref[tap])
    normed, _ = norm(first_ref[...], sums, 0, total)
    pre = normed * vec_ref[0:1] + vec_ref[1:2]
    grad = back * silu_slope(pre) * mask
    dy_ref[...] = grad
    put_rows(out_ref, [column(grad), column(grad * normed)])


def back_first_kernel(sums_ref, sums_y_ref, first_ref, dy_ref, mask_ref, vec_ref, grad_ref):
    cout = first_ref.shape[1]
    mask = wide(mask_ref, cout)
    sums, sums_y = sums_ref[...], sums_y_ref[...]
    total = sums[4:5]
    normed, factor = norm(first_ref[...], sums, 0, total)
    grad = vec_ref[0:1] * factor * (dy_ref[...] - mask * (sums_y[0:1] + normed * sums_y[1:2]) / total)
    grad_ref[...] = grad.astype(BF16)


class Order:
    def __init__(self, batch, fsdp, owned):
        self.zs, self.quarter, self.owned = fsdp // 2, owned // batch, owned
        half = self.zs // 2
        self.parts = []
        for core in range(2):
            self.parts.append([(core, b, z) for b in (0, 2, 1, 3) for z in range(half)])
            self.parts.append([(core, b, z) for b in (0, 1, 2, 3) for z in range(half, self.zs)])

    def starts(self, place_ref):
        core, b, z = place_ref[0], place_ref[1], place_ref[2]
        for part in self.parts:
            for rel_core, rel_b, rel_z in part:
                row = ((z ^ rel_z) * 2 + (core ^ rel_core)) * self.owned + (b ^ rel_b) * self.quarter
                yield pl.multiple_of(row, self.quarter)


def correlate(order, place_ref, grads, patch_refs, out_refs, turned_ref, lhs_ref):
    quarter = order.quarter
    for index, grad in enumerate(grads):
        turned_ref[...] = grad.T
        for block, start in enumerate(order.starts(place_ref)):
            lhs_ref[block * quarter : (block + 1) * quarter, :] = turned_ref[pl.ds(start, quarter), :]
        left = lhs_ref[...]
        for tap, (ref, first, size) in patch_refs[index]:
            value = nn(left, ref[:, first : first + size]).astype(BF16)
            begin = 0
            for out_ref in out_refs:
                count = out_ref.shape[0]
                out_ref[:, tap] = value[begin : begin + count * quarter].reshape(count, quarter, size)
                begin += count * quarter


def weight_second_kernel(order, place_ref, grad_ref, patches_ref, *refs):
    outs, (turned_ref, lhs_ref) = refs[:-2], refs[-2:]
    cout = grad_ref.shape[1]
    taps = [(tap, (patches_ref, tap * cout, cout)) for tap in range(9)]
    correlate(order, place_ref, [grad_ref[...]], [taps], outs, turned_ref, lhs_ref)


def weight_first_kernel(order, place_ref, grad_ref, side_ref, patches_ref, *refs):
    outs, (turned_ref, lhs_ref) = refs[:-2], refs[-2:]
    cin = patches_ref.shape[1] // 9
    taps = [(tap, (patches_ref, tap * cin, cin)) for tap in range(9)]
    center = [(9, (patches_ref, 4 * cin, cin))]
    correlate(order, place_ref, [grad_ref[...], side_ref[...]], [taps, center], outs, turned_ref, lhs_ref)


def plain_weight_kernel(taps, grad_ref, patches_ref, out_ref):
    turned = grad_ref[...].T
    channels = out_ref.shape[2]
    for index, tap in enumerate(taps):
        out_ref[index] = nn(turned, patches_ref[:, tap * channels : (tap + 1) * channels]).astype(BF16)


def input_kernel(plan, grad_ref, side_ref, weights_ref, out_ref, held_ref, moved_ref):
    rows = plan.rows
    fill(plan, held_ref, grad_ref[...].astype(F32))
    for index, (down, right) in enumerate(((0, 0), (0, 1), (1, 0), (1, 1))):
        for start, size, width in plan.segments():
            first = plan.margin + start + plan.slots * (down * width + right)
            moved_ref[index, start : start + size, :] = held_ref[first : first + size, :].astype(BF16)
    for py in range(2):
        for px in range(2):
            total = None
            for ky in (0, 2) if py else (1,):
                for kx in (0, 2) if px else (1,):
                    index = 2 * (ky == 0) + (kx == 0)
                    term = nn(moved_ref[index], weights_ref[ky * 3 + kx])
                    total = term if total is None else total + term
            if py + px == 0:
                total += nn(side_ref[...], weights_ref[9])
            out_ref[2 * py + px] = total.astype(BF16)


def finish_kernel(order, place_ref, *refs):
    parts, outs = refs[:4], refs[4:]
    b, quarter = place_ref[1], order.quarter
    taps = outs[0].shape[0]
    for rel, ref in enumerate(parts):
        rows = pl.ds(pl.multiple_of((b ^ rel) * quarter, quarter), quarter)
        outs[0][:, rows, :] = ref[:taps].astype(F32)
        if len(outs) > 1:
            outs[1][rows, :] = ref[taps].astype(F32)


def call(body, out_shapes, *args, scratch=(), scalars=0, flops=0):
    vmem = pl.BlockSpec(memory_space=pltpu.VMEM)
    specs = [pl.BlockSpec(memory_space=pltpu.SMEM)] * scalars + [vmem] * (len(args) - scalars)
    many = isinstance(out_shapes, (list, tuple))
    moved = sum(arg.size * arg.dtype.itemsize for arg in args)
    return pl.pallas_call(
        body,
        in_specs=specs,
        out_specs=[vmem] * len(out_shapes) if many else vmem,
        out_shape=list(out_shapes) if many else out_shapes,
        scratch_shapes=list(scratch),
        compiler_params=pltpu.CompilerParams(vmem_limit_bytes=VMEM_LIMIT),
        cost_estimate=pl.CostEstimate(flops=flops, bytes_accessed=moved, transcendentals=0),
    )(*args)


def shape(dims, dtype=F32):
    return jax.ShapeDtypeStruct(tuple(dims), dtype)


def exchange(value, axis, count, bit):
    return lax.ppermute(value, axis, [(index, index ^ bit) for index in range(count)])


def bits(count):
    return [1 << index for index in range(count.bit_length() - 1)]


def sum_over(value, axes):
    for axis, count in axes:
        if count & (count - 1):
            value = lax.psum(value, axis)
            continue
        for bit in bits(count):
            value = value + exchange(value, axis, count, bit)
    return value


def reduce_in_plane(parts, core, batch):
    keep_p, keep_q, send_p, send_q = parts
    half_p = keep_p + exchange(send_p, "fsdp", core, 1)
    half_q = keep_q + exchange(send_q, "fsdp", core, 1)
    n_p, n_q = half_p.shape[0] // 4, half_q.shape[0] // 4
    got_p = exchange(half_p[2 * n_p :], "batch", batch, 1)
    got_q = exchange(half_q[2 * n_q :], "batch", batch, 2)
    half_p = half_p[: 2 * n_p] + got_p
    half_q = half_q[: 2 * n_q] + got_q
    got_p = exchange(half_p[n_p:], "batch", batch, 2)
    got_q = exchange(half_q[n_q:], "batch", batch, 1)
    return half_p[:n_p] + got_p, half_q[:n_q] + got_q


def reduce_weights(order, place, parts, batch, fsdp, outs):
    low, high = reduce_in_plane(parts, fsdp, batch)
    pieces = [low[index] for index in range(low.shape[0])] + [high[index] for index in range(high.shape[0])]
    total = pieces[0].astype(F32)
    for rel in range(1, len(pieces)):
        total = total + exchange(pieces[rel], "fsdp", fsdp, 2 * rel).astype(F32)
    mine = total.astype(BF16)
    spread = [mine] + [exchange(mine, "batch", batch, rel) for rel in (1, 2, 3)]
    return call(functools.partial(finish_kernel, order), outs, place, *spread, scalars=1)


def local(
    x_small,
    x_mid,
    x_large,
    cot_small,
    cot_mid,
    cot_large,
    counts,
    w_first,
    gain_first,
    shift_first,
    w_second,
    gain_second,
    shift_second,
    w_short,
    gain_short,
    shift_short,
    *,
    batch,
    fsdp,
):
    fields = (x_small, x_mid, x_large)
    cots = (cot_small, cot_mid, cot_large)
    slots, cin, owned = x_small.shape[0], x_small.shape[3], gain_first.shape[0]
    cout = owned * fsdp
    plan = Plan([cot.shape[1] for cot in cots], slots)
    rows, span = plan.rows, plan.span
    everywhere = (("fsdp", fsdp), ("batch", batch))
    me = lax.axis_index("fsdp")
    fast = batch == 4 and fsdp >= 4 and fsdp & (fsdp - 1) == 0 and owned % (ROWS * batch) == 0
    order = Order(batch, fsdp, owned) if fast else None
    place = jnp.stack([me % 2, lax.axis_index("batch"), me // 2]).astype(jnp.int32)

    own_first = jnp.transpose(w_first, (0, 1, 3, 2)).reshape(9, owned, cin)
    own_second = jnp.transpose(w_second, (0, 1, 3, 2)).reshape(9, owned, cout)
    own_side = jnp.transpose(w_short).reshape(1, owned, cin)
    kern_first = lax.all_gather(jnp.concatenate([own_first, own_side]), "fsdp", axis=1, tiled=True)
    kern_second = lax.all_gather(own_second, "fsdp", axis=1, tiled=True)
    vectors = jnp.stack([gain_first, shift_first, gain_second, shift_second, gain_short, shift_short]).astype(F32)
    vec = lax.dynamic_update_slice(jnp.zeros((8, cout), F32), vectors, (0, me * owned))
    vec = sum_over(vec, (("fsdp", fsdp),))

    planes = []
    for group, field in enumerate(fields):
        side = plan.sides[group]
        split = field.reshape(slots, side, 2, side, 2, cin)
        planes.append(
            jnp.stack([cells(plan, group, split[:, :, py, :, px]) for py in range(2) for px in range(2)])
        )
    planes = jnp.pad(jnp.concatenate(planes, axis=1), ((0, 0), (plan.margin, 0), (0, 0)))
    cot_rows = jnp.concatenate([cells(plan, group, cot) for group, cot in enumerate(cots)])
    mask = []
    for group, side in enumerate(plan.sides):
        valid = np.zeros((side + 1, side + 1, slots), bool)
        valid[1:, 1:] = True
        valid = np.pad(valid.reshape(-1), (0, plan.sizes[group] - valid.size))
        slot = np.arange(plan.sizes[group]) % slots
        mask.append(jnp.asarray(valid) & (jnp.asarray(slot, jnp.int32) < counts[0, group]))
    mask = jnp.broadcast_to(jnp.concatenate(mask).astype(F32)[:, None], (rows, 128))

    patches = call(
        functools.partial(patches_kernel, plan),
        shape((rows, 9 * cin), BF16),
        planes,
        scratch=[pltpu.VMEM((4, plan.margin + rows, cin), F32)],
    )
    flops = 2 * rows * cout * cin * 9
    first, side, sums = call(
        first_kernel,
        [shape((rows, cout)), shape((rows, cout)), shape((8, cout))],
        patches,
        kern_first,
        mask,
        flops=flops,
    )
    sums = sum_over(sums, everywhere)
    second, patches_two, sums_two = call(
        functools.partial(second_kernel, plan),
        [shape((rows, cout)), shape((rows, 9 * cout), BF16), shape((8, cout))],
        sums,
        first,
        mask,
        vec,
        kern_second,
        scratch=[pltpu.VMEM((span, cout), F32)],
        flops=2 * flops,
    )
    sums_two = sum_over(sums_two, everywhere)
    out, dz, sums_z = call(
        output_kernel,
        [shape((rows, cout), BF16), shape((rows, cout)), shape((8, cout))],
        sums,
        sums_two,
        second,
        side,
        cot_rows,
        mask,
        vec,
        flops=50 * rows * cout,
    )
    sums_z = sum_over(sums_z, everywhere)
    grad_two, grad_side, dy, sums_y = call(
        functools.partial(back_second_kernel, plan),
        [shape((rows, cout), BF16), shape((rows, cout), BF16), shape((rows, cout)), shape((8, cout))],
        sums,
        sums_two,
        sums_z,
        first,
        second,
        side,
        dz,
        mask,
        vec,
        kern_second,
        scratch=[pltpu.VMEM((span, cout), F32), pltpu.VMEM((rows, 9 * cout), BF16)],
        flops=2 * flops,
    )
    sums_y = sum_over(sums_y, everywhere)
    if fast:
        turned = [pltpu.VMEM((cout, rows), BF16), pltpu.VMEM((cout, rows), BF16)]
        parts_two = call(
            functools.partial(weight_second_kernel, order),
            [shape((len(part), 9, order.quarter, cout), BF16) for part in order.parts],
            place,
            grad_two,
            patches_two,
            scratch=turned,
            scalars=1,
            flops=2 * flops,
        )
        dw_second = reduce_weights(order, place, parts_two, batch, fsdp, [shape((9, owned, cout))])[0]
    grad_one = call(
        back_first_kernel, shape((rows, cout), BF16), sums, sums_y, first, dy, mask, vec, flops=20 * rows * cout
    )
    if fast:
        parts_one = call(
            functools.partial(weight_first_kernel, order),
            [shape((len(part), 10, order.quarter, cin), BF16) for part in order.parts],
            place,
            grad_one,
            grad_side,
            patches,
            scratch=turned,
            scalars=1,
            flops=flops,
        )
        dw_first, dw_side = reduce_weights(
            order, place, parts_one, batch, fsdp, [shape((9, owned, cin)), shape((owned, cin))]
        )
    else:
        taps = tuple(range(9))
        whole = [
            call(functools.partial(plain_weight_kernel, taps), shape((9, cout, cout), BF16), grad_two, patches_two),
            call(functools.partial(plain_weight_kernel, taps), shape((9, cout, cin), BF16), grad_one, patches),
            call(functools.partial(plain_weight_kernel, (4,)), shape((1, cout, cin), BF16), grad_side, patches),
        ]
        dw_second, dw_first, dw_side = [
            lax.psum(lax.psum_scatter(value, "fsdp", scatter_dimension=1, tiled=True), "batch").astype(F32)
            for value in whole
        ]
        dw_side = dw_side[0]
    dx = call(
        functools.partial(input_kernel, plan),
        shape((4, rows, cin), BF16),
        grad_one,
        grad_side,
        kern_first,
        scratch=[pltpu.VMEM((span, cout), F32), pltpu.VMEM((4, rows, cout), BF16)],
        flops=flops,
    )
    outputs = [images(plan, group, out) for group in range(3)]
    input_grads = []
    for group, side_length in enumerate(plan.sides):
        quarter = [images(plan, group, dx[index]) for index in range(4)]
        whole_rows = [jnp.stack(quarter[2 * py : 2 * py + 2], axis=3) for py in range(2)]
        value = jnp.stack(whole_rows, axis=2)
        input_grads.append(value.reshape(slots, 2 * side_length, 2 * side_length, cin))

    def mine(sums, row):
        return lax.dynamic_slice(sums, (row, me * owned), (1, owned))[0]

    def as_weight(value):
        return jnp.transpose(value.reshape(3, 3, owned, value.shape[2]), (0, 1, 3, 2))

    return (
        outputs[0],
        outputs[1],
        outputs[2],
        input_grads[0],
        input_grads[1],
        input_grads[2],
        as_weight(dw_first),
        mine(sums_y, 1),
        mine(sums_y, 0),
        as_weight(dw_second),
        mine(sums_z, 1),
        mine(sums_z, 0),
        jnp.transpose(dw_side),
        mine(sums_z, 2),
        mine(sums_z, 0),
    )


def solution(mesh):
    split = ("batch", "fsdp")
    image = P(split, None, None, None)
    kernel = P(None, None, None, "fsdp")
    vector = P("fsdp")
    in_specs = (image,) * 6 + (
        P(split, None),
        kernel,
        vector,
        vector,
        kernel,
        vector,
        vector,
        P(None, "fsdp"),
        vector,
        vector,
    )
    out_specs = (image,) * 6 + (
        kernel,
        vector,
        vector,
        kernel,
        vector,
        vector,
        P(None, "fsdp"),
        vector,
        vector,
    )
    body = functools.partial(local, batch=mesh.shape["batch"], fsdp=mesh.shape["fsdp"])
    return jax.shard_map(body, mesh=mesh, in_specs=in_specs, out_specs=out_specs, check_vma=False)
```

```python
import functools

import jax
import jax.numpy as jnp
import numpy as np
from jax import lax
from jax.experimental import pallas as pl
from jax.experimental.pallas import tpu as pltpu
from jax.sharding import PartitionSpec as P

EPSILON = 1e-05
F32 = jnp.float32
BF16 = jnp.bfloat16
ROWS = 16
VMEM_LIMIT = 20 * 2**20


def up(value, step):
    return -(-value // step) * step


class Plan:
    def __init__(self, sides, slots):
        self.sides, self.slots = sides, slots
        self.starts, self.sizes, row = [], [], 0
        for index, side in enumerate(sides):
            width = side + 1
            after = sides[index + 1] + 1 if index + 1 < len(sides) else 0
            size = up(slots * (width * width + max(0, width + 1 - after)), ROWS)
            self.starts.append(row)
            self.sizes.append(size)
            row += size
        self.rows = row
        self.margin = up(slots * (max(sides) + 2), ROWS)
        self.span = self.rows + 2 * self.margin

    def segments(self):
        return list(zip(self.starts, self.sizes, [side + 1 for side in self.sides]))


    def cells(self):
        for group, (start, side) in enumerate(zip(self.starts, self.sides)):
            for down in range(side):
                for right in range(side):
                    yield group, down, right, start + self.slots * ((down + 1) * (side + 1) + right + 1)


def nn(left, right):
    return lax.dot_general(left, right, (((1,), (0,)), ((), ())), preferred_element_type=F32)


def nt(left, right):
    return lax.dot_general(left, right, (((1,), (1,)), ((), ())), preferred_element_type=F32)


def column(value):
    return jnp.sum(value, axis=0, keepdims=True)


def wide(mask_ref, channels):
    return jnp.concatenate([mask_ref[...]] * (channels // mask_ref.shape[1]), axis=1)


def silu_slope(value):
    gate = jax.nn.sigmoid(value)
    return gate * (1.0 + value * (1.0 - gate))


def norm(value, sums, row, total):
    center = sums[row : row + 1] / total
    spread = sums[row + 1 : row + 2] / total - center * center
    factor = lax.rsqrt(spread + EPSILON)
    return (value - center) * factor, factor


def put_rows(ref, rows):
    for index, row in enumerate(rows):
        ref[index : index + 1, :] = row
    ref[len(rows) :, :] = jnp.zeros((ref.shape[0] - len(rows), ref.shape[1]), F32)


def offsets(plan, width):
    return [plan.slots * (dy * width + dx) for dy in (-1, 0, 1) for dx in (-1, 0, 1)]


def unfold(plan, padded_ref, out_ref, sign):
    channels = padded_ref.shape[1]
    for start, size, width in plan.segments():
        for tap, offset in enumerate(offsets(plan, width)):
            first = plan.margin + start + sign * offset
            out_ref[start : start + size, tap * channels : (tap + 1) * channels] = padded_ref[
                first : first + size, :
            ].astype(BF16)


def fill(plan, padded_ref, value):
    edge = jnp.zeros((plan.margin, padded_ref.shape[1]), F32)
    padded_ref[: plan.margin, :] = edge
    padded_ref[plan.margin : plan.margin + plan.rows, :] = value
    padded_ref[plan.margin + plan.rows :, :] = edge


def prepare_kernel(plan, counts_ref, *refs):
    fields, cots, (patches_ref, cot_ref, mask_ref, held_ref) = refs[:3], refs[3:6], refs[6:]
    slots, channels = plan.slots, fields[0].shape[3]
    held_ref[...] = jnp.zeros(held_ref.shape, F32)
    cot_ref[...] = jnp.zeros(cot_ref.shape, F32)
    mask_ref[...] = jnp.zeros(mask_ref.shape, F32)
    slot = lax.broadcasted_iota(jnp.int32, (slots, mask_ref.shape[1]), 0)
    live = [(slot < counts_ref[0, group]).astype(F32) for group in range(3)]
    for group, down, right, row in plan.cells():
        mask_ref[row : row + slots, :] = live[group]
        cot_ref[row : row + slots, :] = cots[group][down, right].astype(F32)
        for py in range(2):
            for px in range(2):
                first = plan.margin + row
                held_ref[2 * py + px, first : first + slots, :] = fields[group][2 * down + py, 2 * right + px].astype(F32)
    for start, size, width in plan.segments():
        for ky in range(3):
            for kx in range(3):
                tap = ky * 3 + kx
                shift = plan.slots * (width * (ky == 0) + (kx == 0))
                first = plan.margin + start - shift
                patches_ref[start : start + size, tap * channels : (tap + 1) * channels] = held_ref[
                    2 * (ky != 1) + (kx != 1), first : first + size, :
                ].astype(BF16)


def output_rows_kernel(plan, rows_ref, *outs):
    for group, down, right, row in plan.cells():
        outs[group][down, right] = rows_ref[row : row + plan.slots, :].astype(BF16)


def first_kernel(patches_ref, mask_ref, vec_ref, weights_ref, ready, first_ref, side_ref, sums_ref):
    ready()
    cin = weights_ref.shape[2]
    cout = weights_ref.shape[1]
    total = nt(patches_ref[:, :cin], weights_ref[0])
    for tap in range(1, 9):
        total += nt(patches_ref[:, tap * cin : (tap + 1) * cin], weights_ref[tap])
    side = nt(patches_ref[:, 4 * cin : 5 * cin], weights_ref[9])
    first_ref[...] = total
    side_ref[...] = side
    mask = wide(mask_ref, cout)
    put_rows(
        sums_ref,
        [
            column(mask * total),
            column(mask * total * total),
            column(mask * side),
            column(mask * side * side),
            column(mask),
            vec_ref[0:1],
            vec_ref[1:2],
        ],
    )


def second_kernel(
    plan, sums_ref, got_ref, first_ref, mask_ref, vec_ref, weights_ref, ready, second_ref, patches_ref, out_ref, held_ref
):
    cout = first_ref.shape[1]
    mask = wide(mask_ref, cout)
    sums = sums_ref[...] + got_ref[...]
    normed, _ = norm(first_ref[...], sums, 0, sums[4:5])
    pre = normed * sums[5:6] + sums[6:7]
    fill(plan, held_ref, jax.nn.silu(pre) * mask)
    unfold(plan, held_ref, patches_ref, 1)
    ready()
    total = nt(patches_ref[:, :cout], weights_ref[0])
    for tap in range(1, 9):
        total += nt(patches_ref[:, tap * cout : (tap + 1) * cout], weights_ref[tap])
    second_ref[...] = total
    put_rows(
        out_ref, [column(mask * total), column(mask * total * total)] + [vec_ref[row : row + 1] for row in range(2, 6)]
    )


def output_kernel(
    sums_ref, got_ref, sums_two_ref, got_two_ref, second_ref, side_ref, cot_ref, mask_ref, out_ref, dz_ref, sums_out_ref
):
    cout = second_ref.shape[1]
    mask = wide(mask_ref, cout)
    sums, sums_two = sums_ref[...] + got_ref[...], sums_two_ref[...] + got_two_ref[...]
    total = sums[4:5]
    normed_two, _ = norm(second_ref[...], sums_two, 0, total)
    normed_side, _ = norm(side_ref[...], sums, 2, total)
    value = (normed_two * sums_two[2:3] + sums_two[3:4]) + (normed_side * sums_two[4:5] + sums_two[5:6])
    gate = jax.nn.sigmoid(value)
    out_ref[...] = value * gate * mask
    grad = cot_ref[...] * mask * (gate * (1.0 + value * (1.0 - gate)))
    dz_ref[...] = grad
    total = column(grad)
    put_rows(sums_out_ref, [total, column(grad * normed_two), column(grad * normed_side), total])


def back_second_kernel(
    plan, sums_ref, got_ref, sums_two_ref, got_two_ref, sums_z_ref, got_z_ref,
    first_ref, second_ref, side_ref, dz_ref, mask_ref, weights_ref, ready,
    grad_two_ref, grad_side_ref, dy_ref, out_ref, held_ref, patches_ref,
):
    cout = first_ref.shape[1]
    mask = wide(mask_ref, cout)
    sums, sums_two = sums_ref[...] + got_ref[...], sums_two_ref[...] + got_two_ref[...]
    sums_z = sums_z_ref[...] + got_z_ref[...]
    total = sums[4:5]
    grad = dz_ref[...]
    normed, factor = norm(second_ref[...], sums_two, 0, total)
    two = sums_two[2:3] * factor * (grad - mask * (sums_z[0:1] + normed * sums_z[1:2]) / total)
    normed, factor = norm(side_ref[...], sums, 2, total)
    side = sums_two[4:5] * factor * (grad - mask * (sums_z[0:1] + normed * sums_z[2:3]) / total)
    grad_side_ref[...] = side.astype(BF16)
    grad_two_ref[...] = two.astype(BF16)
    fill(plan, held_ref, two)
    unfold(plan, held_ref, patches_ref, -1)
    ready()
    back = nn(patches_ref[:, :cout], weights_ref[0])
    for tap in range(1, 9):
        back += nn(patches_ref[:, tap * cout : (tap + 1) * cout], weights_ref[tap])
    normed, _ = norm(first_ref[...], sums, 0, total)
    pre = normed * sums[5:6] + sums[6:7]
    grad = back * silu_slope(pre) * mask
    dy_ref[...] = grad
    put_rows(out_ref, [column(grad), column(grad * normed)])


def back_first(sums_ref, got_ref, sums_y_ref, got_y_ref, first_ref, dy_ref, mask_ref, grad_ref):
    cout = first_ref.shape[1]
    mask = wide(mask_ref, cout)
    sums, sums_y = sums_ref[...] + got_ref[...], sums_y_ref[...] + got_y_ref[...]
    total = sums[4:5]
    normed, factor = norm(first_ref[...], sums, 0, total)
    grad = sums[5:6] * factor * (dy_ref[...] - mask * (sums_y[0:1] + normed * sums_y[1:2]) / total)
    grad_ref[...] = grad.astype(BF16)


class Order:
    def __init__(self, batch, fsdp, owned):
        self.zs, self.quarter, self.owned = fsdp // 2, owned // batch, owned
        half = self.zs // 2
        self.parts = []
        for core in range(2):
            self.parts.append([(core, b, z) for b in (0, 2, 1, 3) for z in range(half)])
            self.parts.append([(core, b, z) for b in (0, 1, 2, 3) for z in range(half, self.zs)])

    def starts(self, place_ref):
        core, b, z = place_ref[0], place_ref[1], place_ref[2]
        for part in self.parts:
            for rel_core, rel_b, rel_z in part:
                row = ((z ^ rel_z) * 2 + (core ^ rel_core)) * self.owned + (b ^ rel_b) * self.quarter
                yield pl.multiple_of(row, self.quarter)


def correlate(order, place_ref, grads, patch_refs, out_refs, turned_ref, lhs_ref):
    quarter = order.quarter
    for index, grad in enumerate(grads):
        turned_ref[...] = grad.T
        for block, start in enumerate(order.starts(place_ref)):
            lhs_ref[block * quarter : (block + 1) * quarter, :] = turned_ref[pl.ds(start, quarter), :]
        left = lhs_ref[...]
        for tap, (ref, first, size) in patch_refs[index]:
            value = nn(left, ref[:, first : first + size]).astype(BF16)
            begin = 0
            for out_ref in out_refs:
                count = out_ref.shape[0]
                out_ref[:, tap] = value[begin : begin + count * quarter].reshape(count, quarter, size)
                begin += count * quarter


def weight_second_kernel(order, place_ref, grad_ref, patches_ref, *refs):
    outs, (turned_ref, lhs_ref) = refs[:-2], refs[-2:]
    cout = grad_ref.shape[1]
    taps = [(tap, (patches_ref, tap * cout, cout)) for tap in range(9)]
    correlate(order, place_ref, [grad_ref[...]], [taps], outs, turned_ref, lhs_ref)


def weight_first_kernel(
    order, place_ref, sums_ref, got_ref, sums_y_ref, got_y_ref, first_ref, dy_ref, mask_ref, side_ref, patches_ref, *refs
):
    grad_ref, outs, (turned_ref, lhs_ref) = refs[0], refs[1:-2], refs[-2:]
    back_first(sums_ref, got_ref, sums_y_ref, got_y_ref, first_ref, dy_ref, mask_ref, grad_ref)
    cin = patches_ref.shape[1] // 9
    taps = [(tap, (patches_ref, tap * cin, cin)) for tap in range(9)]
    center = [(9, (patches_ref, 4 * cin, cin))]
    correlate(order, place_ref, [grad_ref[...], side_ref[...]], [taps, center], outs, turned_ref, lhs_ref)


def plain_weight_kernel(taps, grad_ref, patches_ref, out_ref):
    turned = grad_ref[...].T
    channels = out_ref.shape[2]
    for index, tap in enumerate(taps):
        out_ref[index] = nn(turned, patches_ref[:, tap * channels : (tap + 1) * channels]).astype(BF16)


def input_kernel(plan, grad_ref, side_ref, weights_ref, ready, *refs):
    outs, (held_ref, moved_ref, total_ref) = refs[:3], refs[3:]
    ready()
    rows = plan.rows
    fill(plan, held_ref, grad_ref[...].astype(F32))
    for index, (down, right) in enumerate(((0, 0), (0, 1), (1, 0), (1, 1))):
        for start, size, width in plan.segments():
            first = plan.margin + start + plan.slots * (down * width + right)
            moved_ref[index, start : start + size, :] = held_ref[first : first + size, :].astype(BF16)
    for py in range(2):
        for px in range(2):
            total = None
            for ky in (0, 2) if py else (1,):
                for kx in (0, 2) if px else (1,):
                    index = 2 * (ky == 0) + (kx == 0)
                    term = nn(moved_ref[index], weights_ref[ky * 3 + kx])
                    total = term if total is None else total + term
            if py + px == 0:
                total += nn(side_ref[...], weights_ref[9])
            total_ref[...] = total
            for group, down, right, row in plan.cells():
                outs[group][2 * down + py, 2 * right + px] = total_ref[row : row + plan.slots, :].astype(BF16)


def finish_kernel(order, place_ref, *refs):
    parts, outs = refs[:4], refs[4:]
    b, quarter = place_ref[1], order.quarter
    taps = outs[0].shape[0]
    for rel, ref in enumerate(parts):
        rows = pl.ds(pl.multiple_of((b ^ rel) * quarter, quarter), quarter)
        outs[0][:, rows, :] = ref[:taps].astype(F32)
        if len(outs) > 1:
            outs[1][rows, :] = ref[taps].astype(F32)


class Gathered:
    def __init__(self, arrays, place=None, order=None):
        self.arrays, self.place, self.order = arrays, place, order

    def dims(self):
        if self.order is None:
            return self.arrays[0].shape
        zs, taps, quarter, channels = self.arrays[0].shape
        return taps, 2 * zs * self.order.owned, channels

    def wrap(self, body, scalars, count):
        if self.order is None:
            return lambda *refs: body(*refs[: count + 1], lambda: None, *refs[count + 1 :])
        order, many = self.order, len(self.arrays)

        def whole(place_ref, *refs):
            inputs, bundles, rest = refs[:count], refs[count : count + many], refs[count + many :]
            outs, (weights_ref, semaphores) = rest[:-2], rest[-2:]
            core, b, z = place_ref[0], place_ref[1], place_ref[2]
            copies = []
            for index, bundle in enumerate(bundles):
                for rel_z in range(order.zs):
                    row = ((z ^ rel_z) * 2 + (core ^ (index // 4))) * order.owned + (b ^ (index % 4)) * order.quarter
                    rows = pl.ds(pl.multiple_of(row, order.quarter), order.quarter)
                    copies.append(
                        pltpu.make_async_copy(
                            bundle.at[rel_z], weights_ref.at[:, rows, :], semaphores.at[index * order.zs + rel_z]
                        )
                    )
            for copy in copies:
                copy.start()

            def ready():
                for copy in copies:
                    copy.wait()

            body(*inputs, weights_ref, ready, *outs)

        return whole


def call(body, out_shapes, *args, scratch=(), scalars=0, flops=0, weights=None):
    vmem = pl.BlockSpec(memory_space=pltpu.VMEM)
    specs = [pl.BlockSpec(memory_space=pltpu.SMEM)] * scalars + [vmem] * (len(args) - scalars)
    if weights is not None:
        body = weights.wrap(body, scalars, len(args))
        scratch = list(scratch)
        if weights.order is None:
            args = args + tuple(weights.arrays)
            specs = specs + [vmem]
        else:
            args = (weights.place,) + args + tuple(weights.arrays)
            specs = [pl.BlockSpec(memory_space=pltpu.SMEM)] + specs + [pl.BlockSpec(memory_space=pl.ANY)] * len(weights.arrays)
            scratch += [
                pltpu.VMEM(weights.dims(), BF16),
                pltpu.SemaphoreType.DMA((len(weights.arrays) * weights.order.zs,)),
            ]
    many = isinstance(out_shapes, (list, tuple))
    moved = sum(arg.size * arg.dtype.itemsize for arg in args)
    return pl.pallas_call(
        body,
        in_specs=specs,
        out_specs=[vmem] * len(out_shapes) if many else vmem,
        out_shape=list(out_shapes) if many else out_shapes,
        scratch_shapes=list(scratch),
        compiler_params=pltpu.CompilerParams(vmem_limit_bytes=VMEM_LIMIT),
        cost_estimate=pl.CostEstimate(flops=flops, bytes_accessed=moved, transcendentals=0),
    )(*args)


def shape(dims, dtype=F32):
    return jax.ShapeDtypeStruct(tuple(dims), dtype)


def exchange(value, axis, count, bit):
    return lax.ppermute(value, axis, [(index, index ^ bit) for index in range(count)])


def bits(count):
    return [1 << index for index in range(count.bit_length() - 1)]


def after(value, *others):
    return lax.optimization_barrier((value, *others))[0]


def sum_over(value, axes, hooks=()):
    steps = []
    for axis, count in axes:
        if count & (count - 1):
            value = lax.psum(value, axis)
        else:
            steps += [(axis, count, bit) for bit in bits(count)]
    got = jnp.zeros_like(value)
    for index, (axis, count, bit) in enumerate(steps):
        if index:
            value = value + got
        if index < len(hooks) and hooks[index] is not None:
            value = after(value, *hooks[index]())
        got = exchange(value, axis, count, bit)
    return value, got


def piece_kernel(order, place_ref, first_ref, side_ref, second_ref, first_out_ref, second_out_ref):
    rows = pl.ds(pl.multiple_of(place_ref[1] * order.quarter, order.quarter), order.quarter)
    first_out_ref[:9] = first_ref[:, rows, :]
    first_out_ref[9] = side_ref[rows, :]
    second_out_ref[...] = second_ref[:, rows, :]


def spread_line(order, piece, fsdp):
    return [piece] + [exchange(piece, "fsdp", fsdp, 2 * rel) for rel in range(1, order.zs)]


def spread_plane(pieces, batch):
    bundle = jnp.stack(pieces)
    return [bundle] + [exchange(bundle, "batch", batch, rel) for rel in (1, 2, 3)]


def spread_cores(bundles, fsdp):
    return bundles + [exchange(value, "fsdp", fsdp, 1) for value in bundles]


def reduce_cores(parts, fsdp):
    keep_p, keep_q, send_p, send_q = parts
    return keep_p + exchange(send_p, "fsdp", fsdp, 1), keep_q + exchange(send_q, "fsdp", fsdp, 1)


def finish_weights(order, place, halves, batch, fsdp, outs):
    half_p, half_q = halves
    n_p, n_q = half_p.shape[0] // 4, half_q.shape[0] // 4
    got_p = exchange(half_p[2 * n_p :], "batch", batch, 1)
    got_q = exchange(half_q[2 * n_q :], "batch", batch, 2)
    half_p = half_p[: 2 * n_p] + got_p
    half_q = half_q[: 2 * n_q] + got_q
    got_p = exchange(half_p[n_p:], "batch", batch, 2)
    got_q = exchange(half_q[n_q:], "batch", batch, 1)
    low, high = half_p[:n_p] + got_p, half_q[:n_q] + got_q
    pieces = [low[index] for index in range(n_p)] + [high[index] for index in range(n_q)]
    total = pieces[0].astype(F32)
    for rel in range(1, len(pieces)):
        total = total + exchange(pieces[rel], "fsdp", fsdp, 2 * rel).astype(F32)
    mine = total.astype(BF16)
    spread = [mine] + [exchange(mine, "batch", batch, rel) for rel in (1, 2, 3)]
    return call(functools.partial(finish_kernel, order), outs, place, *spread, scalars=1)


def local(
    x_small,
    x_mid,
    x_large,
    cot_small,
    cot_mid,
    cot_large,
    counts,
    w_first,
    gain_first,
    shift_first,
    w_second,
    gain_second,
    shift_second,
    w_short,
    gain_short,
    shift_short,
    *,
    batch,
    fsdp,
):
    fields = (x_small, x_mid, x_large)
    cots = (cot_small, cot_mid, cot_large)
    slots, cin, owned = x_small.shape[0], x_small.shape[3], gain_first.shape[0]
    cout = owned * fsdp
    plan = Plan([cot.shape[1] for cot in cots], slots)
    rows, span = plan.rows, plan.span
    everywhere = (("fsdp", fsdp), ("batch", batch))
    me = lax.axis_index("fsdp")
    fast = batch == 4 and fsdp >= 4 and fsdp & (fsdp - 1) == 0 and owned % (ROWS * batch) == 0
    order = Order(batch, fsdp, owned) if fast else None
    place = jnp.stack([me % 2, lax.axis_index("batch"), me // 2]).astype(jnp.int32)

    own_first = jnp.transpose(w_first, (0, 1, 3, 2)).reshape(9, owned, cin)
    own_second = jnp.transpose(w_second, (0, 1, 3, 2)).reshape(9, owned, cout)
    own_side = jnp.transpose(w_short)
    if fast:
        piece_first, piece_second = call(
            functools.partial(piece_kernel, order),
            [shape((10, order.quarter, cin), BF16), shape((9, order.quarter, cout), BF16)],
            place,
            own_first,
            own_side,
            own_second,
            scalars=1,
        )
        along_first = spread_line(order, piece_first, fsdp)
        plane_first = spread_plane(along_first, batch)
        along_second = spread_line(order, after(piece_second, *along_first), fsdp)
        plane_second = spread_plane(along_second, batch)
        kern_first = Gathered(spread_cores(plane_first, fsdp), place, order)
    else:
        kern_first = Gathered([lax.all_gather(jnp.concatenate([own_first, own_side[None]]), "fsdp", axis=1, tiled=True)])
        kern_second = Gathered([lax.all_gather(own_second, "fsdp", axis=1, tiled=True)])
    vectors = jnp.stack([gain_first, shift_first, gain_second, shift_second, gain_short, shift_short]).astype(F32)
    vectors = jnp.where(lax.axis_index("batch") == 0, vectors, 0.0)
    vec = lax.dynamic_update_slice(jnp.zeros((8, cout), F32), vectors, (0, me * owned))

    patches, cot_rows, mask = call(
        functools.partial(prepare_kernel, plan),
        [shape((rows, 9 * cin), BF16), shape((rows, cout)), shape((rows, 128))],
        counts,
        *[jnp.transpose(value, (1, 2, 0, 3)) for value in fields + cots],
        scratch=[pltpu.VMEM((4, plan.margin + rows, cin), F32)],
        scalars=1,
    )
    flops = 2 * rows * cout * cin * 9
    first, side, sums = call(
        first_kernel,
        [shape((rows, cout)), shape((rows, cout)), shape((8, cout))],
        patches,
        mask,
        vec,
        flops=flops,
        weights=kern_first,
    )
    sums = sum_over(sums, everywhere)
    if fast:
        kern_second = Gathered(spread_cores([after(value, *sums) for value in plane_second], fsdp), place, order)
    second, patches_two, sums_two = call(
        functools.partial(second_kernel, plan),
        [shape((rows, cout)), shape((rows, 9 * cout), BF16), shape((8, cout))],
        *sums,
        first,
        mask,
        vec,
        scratch=[pltpu.VMEM((span, cout), F32)],
        flops=2 * flops,
        weights=kern_second,
    )
    sums_two = sum_over(sums_two, everywhere)
    out_rows, dz, sums_z = call(
        output_kernel,
        [shape((rows, cout)), shape((rows, cout)), shape((8, cout))],
        *sums,
        *sums_two,
        second,
        side,
        cot_rows,
        mask,
        flops=50 * rows * cout,
    )
    sums_z = sum_over(sums_z, everywhere)
    grad_two, grad_side, dy, sums_y = call(
        functools.partial(back_second_kernel, plan),
        [shape((rows, cout), BF16), shape((rows, cout), BF16), shape((rows, cout)), shape((8, cout))],
        *sums,
        *sums_two,
        *sums_z,
        first,
        second,
        side,
        dz,
        mask,
        scratch=[pltpu.VMEM((span, cout), F32), pltpu.VMEM((rows, 9 * cout), BF16)],
        flops=2 * flops,
        weights=kern_second,
    )
    hooks = ()
    if fast:
        turned = [pltpu.VMEM((cout, rows), BF16), pltpu.VMEM((cout, rows), BF16)]
        parts_two = call(
            functools.partial(weight_second_kernel, order),
            [shape((len(part), 9, order.quarter, cout), BF16) for part in order.parts],
            place,
            grad_two,
            patches_two,
            scratch=turned,
            scalars=1,
            flops=2 * flops,
        )
        halves_two = reduce_cores(parts_two, fsdp)
        hooks = (None, None, lambda: parts_two, None, lambda: halves_two)
    sums_y = sum_over(sums_y, everywhere, hooks)
    if fast:
        grad_one, *parts_one = call(
            functools.partial(weight_first_kernel, order),
            [shape((rows, cout), BF16)] + [shape((len(part), 10, order.quarter, cin), BF16) for part in order.parts],
            place,
            *sums,
            *sums_y,
            first,
            dy,
            mask,
            grad_side,
            patches,
            scratch=turned,
            scalars=1,
            flops=flops,
        )
        halves_one = reduce_cores(parts_one, fsdp)
        dw_first, dw_side = finish_weights(
            order, place, halves_one, batch, fsdp, [shape((9, owned, cin)), shape((owned, cin))]
        )
        dw_second = finish_weights(order, place, halves_two, batch, fsdp, [shape((9, owned, cout))])[0]
        grad_late, out_rows = after(grad_one, *halves_one), after(out_rows, *halves_one)
    else:
        grad_one = call(back_first, shape((rows, cout), BF16), *sums, *sums_y, first, dy, mask)
        taps = tuple(range(9))
        whole = [
            call(functools.partial(plain_weight_kernel, taps), shape((9, cout, cout), BF16), grad_two, patches_two),
            call(functools.partial(plain_weight_kernel, taps), shape((9, cout, cin), BF16), grad_one, patches),
            call(functools.partial(plain_weight_kernel, (4,)), shape((1, cout, cin), BF16), grad_side, patches),
        ]
        dw_second, dw_first, dw_side = [
            lax.psum(lax.psum_scatter(value, "fsdp", scatter_dimension=1, tiled=True), "batch").astype(F32)
            for value in whole
        ]
        dw_side = dw_side[0]
        grad_late = grad_one
    input_grads = call(
        functools.partial(input_kernel, plan),
        [shape((2 * length, 2 * length, slots, cin), BF16) for length in plan.sides],
        grad_late,
        grad_side,
        scratch=[pltpu.VMEM((span, cout), F32), pltpu.VMEM((4, rows, cout), BF16), pltpu.VMEM((rows, cin), F32)],
        flops=flops,
        weights=kern_first,
    )
    outputs = call(
        functools.partial(output_rows_kernel, plan),
        [shape((length, length, slots, cout), BF16) for length in plan.sides],
        out_rows,
    )

    def mine(sums, row):
        value = sums[0][row : row + 1] + sums[1][row : row + 1]
        return lax.dynamic_slice(value, (0, me * owned), (1, owned))[0]

    def as_weight(value):
        return jnp.transpose(value.reshape(3, 3, owned, value.shape[2]), (0, 1, 3, 2))

    return (
        *[jnp.transpose(value, (2, 0, 1, 3)) for value in (*outputs, *input_grads)],
        as_weight(dw_first),
        mine(sums_y, 1),
        mine(sums_y, 0),
        as_weight(dw_second),
        mine(sums_z, 1),
        mine(sums_z, 0),
        jnp.transpose(dw_side),
        mine(sums_z, 2),
        mine(sums_z, 3),
    )


def solution(mesh):
    split = ("batch", "fsdp")
    image = P(split, None, None, None)
    kernel = P(None, None, None, "fsdp")
    vector = P("fsdp")
    in_specs = (image,) * 6 + (
        P(split, None),
        kernel,
        vector,
        vector,
        kernel,
        vector,
        vector,
        P(None, "fsdp"),
        vector,
        vector,
    )
    out_specs = (image,) * 6 + (
        kernel,
        vector,
        vector,
        kernel,
        vector,
        vector,
        P(None, "fsdp"),
        vector,
        vector,
    )
    body = functools.partial(local, batch=mesh.shape["batch"], fsdp=mesh.shape["fsdp"])
    return jax.shard_map(body, mesh=mesh, in_specs=in_specs, out_specs=out_specs, check_vma=False)
```

```python
import functools

import jax
import jax.numpy as jnp
import numpy as np
from jax import lax
from jax.experimental import pallas as pl
from jax.experimental.pallas import tpu as pltpu
from jax.sharding import PartitionSpec as P

EPSILON = 1e-05
F32 = jnp.float32
BF16 = jnp.bfloat16
ROWS = 16
VMEM_LIMIT = 20 * 2**20


def up(value, step):
    return -(-value // step) * step


class Plan:
    def __init__(self, sides, slots):
        self.sides, self.slots = sides, slots
        self.starts, self.sizes, row = [], [], 0
        for index, side in enumerate(sides):
            width = side + 1
            after = sides[index + 1] + 1 if index + 1 < len(sides) else 0
            size = up(slots * (width * width + max(0, width + 1 - after)), ROWS)
            self.starts.append(row)
            self.sizes.append(size)
            row += size
        self.rows = row
        self.margin = up(slots * (max(sides) + 2), ROWS)
        self.span = self.rows + 2 * self.margin

    def segments(self):
        return list(zip(self.starts, self.sizes, [side + 1 for side in self.sides]))


    def cells(self):
        for group, (start, side) in enumerate(zip(self.starts, self.sides)):
            for down in range(side):
                for right in range(side):
                    yield group, down, right, start + self.slots * ((down + 1) * (side + 1) + right + 1)


def nn(left, right):
    return lax.dot_general(left, right, (((1,), (0,)), ((), ())), preferred_element_type=F32)


def nt(left, right):
    return lax.dot_general(left, right, (((1,), (1,)), ((), ())), preferred_element_type=F32)


def column(value):
    return jnp.sum(value, axis=0, keepdims=True)


def wide(mask_ref, channels):
    return jnp.concatenate([mask_ref[...]] * (channels // mask_ref.shape[1]), axis=1)


def silu_slope(value):
    gate = jax.nn.sigmoid(value)
    return gate * (1.0 + value * (1.0 - gate))


def norm(value, sums, row, total):
    center = sums[row : row + 1] / total
    spread = sums[row + 1 : row + 2] / total - center * center
    factor = lax.rsqrt(spread + EPSILON)
    return (value - center) * factor, factor


def put_rows(ref, rows):
    for index, row in enumerate(rows):
        ref[index : index + 1, :] = row
    ref[len(rows) :, :] = jnp.zeros((ref.shape[0] - len(rows), ref.shape[1]), F32)


def offsets(plan, width):
    return [plan.slots * (dy * width + dx) for dy in (-1, 0, 1) for dx in (-1, 0, 1)]


def unfold(plan, padded_ref, out_ref, sign):
    channels = padded_ref.shape[1]
    for start, size, width in plan.segments():
        for tap, offset in enumerate(offsets(plan, width)):
            first = plan.margin + start + sign * offset
            out_ref[start : start + size, tap * channels : (tap + 1) * channels] = padded_ref[
                first : first + size, :
            ].astype(BF16)


def fill(plan, padded_ref, value):
    edge = jnp.zeros((plan.margin, padded_ref.shape[1]), F32)
    padded_ref[: plan.margin, :] = edge
    padded_ref[plan.margin : plan.margin + plan.rows, :] = value
    padded_ref[plan.margin + plan.rows :, :] = edge


def prepare_kernel(plan, owned, place_ref, counts_ref, *refs):
    fields, cots, vectors = refs[:3], refs[3:6], refs[6:12]
    patches_ref, cot_ref, mask_ref, vec_ref, held_ref = refs[12:]
    slots, channels = plan.slots, fields[0].shape[3]
    held_ref[...] = jnp.zeros(held_ref.shape, F32)
    cot_ref[...] = jnp.zeros(cot_ref.shape, F32)
    mask_ref[...] = jnp.zeros(mask_ref.shape, F32)
    cout = vec_ref.shape[1]
    first = (place_ref[2] * 2 + place_ref[0]) * owned
    spot = lax.broadcasted_iota(jnp.int32, (owned, cout), 1) - lax.broadcasted_iota(jnp.int32, (owned, cout), 0)
    own = ((spot == first) & (place_ref[1] == 0)).astype(BF16)
    held = [ref[...].astype(F32) for ref in vectors] + [jnp.zeros((vec_ref.shape[0] - 6, owned), F32)]
    vec_ref[...] = nn(jnp.concatenate(held, axis=0).astype(BF16), own)
    slot = lax.broadcasted_iota(jnp.int32, (slots, mask_ref.shape[1]), 0)
    live = [(slot < counts_ref[0, group]).astype(F32) for group in range(3)]
    for group, down, right, row in plan.cells():
        mask_ref[row : row + slots, :] = live[group]
        cot_ref[row : row + slots, :] = cots[group][down, right].astype(F32)
        for py in range(2):
            for px in range(2):
                first = plan.margin + row
                held_ref[2 * py + px, first : first + slots, :] = fields[group][2 * down + py, 2 * right + px].astype(F32)
    for start, size, width in plan.segments():
        for ky in range(3):
            for kx in range(3):
                tap = ky * 3 + kx
                shift = plan.slots * (width * (ky == 0) + (kx == 0))
                first = plan.margin + start - shift
                patches_ref[start : start + size, tap * channels : (tap + 1) * channels] = held_ref[
                    2 * (ky != 1) + (kx != 1), first : first + size, :
                ].astype(BF16)


def first_kernel(patches_ref, mask_ref, vec_ref, weights_ref, ready, first_ref, side_ref, sums_ref):
    ready()
    cin = weights_ref.shape[2]
    cout = weights_ref.shape[1]
    total = nt(patches_ref[:, :cin], weights_ref[0])
    for tap in range(1, 9):
        total += nt(patches_ref[:, tap * cin : (tap + 1) * cin], weights_ref[tap])
    side = nt(patches_ref[:, 4 * cin : 5 * cin], weights_ref[9])
    first_ref[...] = total
    side_ref[...] = side
    mask = wide(mask_ref, cout)
    put_rows(
        sums_ref,
        [
            column(mask * total),
            column(mask * total * total),
            column(mask * side),
            column(mask * side * side),
            column(mask),
            vec_ref[0:1],
            vec_ref[1:2],
        ],
    )


def second_kernel(
    plan, sums_ref, got_ref, first_ref, mask_ref, vec_ref, weights_ref, ready, second_ref, patches_ref, out_ref, held_ref
):
    cout = first_ref.shape[1]
    mask = wide(mask_ref, cout)
    sums = sums_ref[...] + got_ref[...]
    normed, _ = norm(first_ref[...], sums, 0, sums[4:5])
    pre = normed * sums[5:6] + sums[6:7]
    fill(plan, held_ref, jax.nn.silu(pre) * mask)
    unfold(plan, held_ref, patches_ref, 1)
    ready()
    total = nt(patches_ref[:, :cout], weights_ref[0])
    for tap in range(1, 9):
        total += nt(patches_ref[:, tap * cout : (tap + 1) * cout], weights_ref[tap])
    second_ref[...] = total
    put_rows(
        out_ref, [column(mask * total), column(mask * total * total)] + [vec_ref[row : row + 1] for row in range(2, 6)]
    )


def output_kernel(
    plan, sums_ref, got_ref, sums_two_ref, got_two_ref, second_ref, side_ref, cot_ref, mask_ref, *refs
):
    outs, (dz_ref, sums_out_ref) = refs[:3], refs[3:]
    cout = second_ref.shape[1]
    mask = wide(mask_ref, cout)
    sums, sums_two = sums_ref[...] + got_ref[...], sums_two_ref[...] + got_two_ref[...]
    total = sums[4:5]
    normed_two, _ = norm(second_ref[...], sums_two, 0, total)
    normed_side, _ = norm(side_ref[...], sums, 2, total)
    value = (normed_two * sums_two[2:3] + sums_two[3:4]) + (normed_side * sums_two[4:5] + sums_two[5:6])
    gate = jax.nn.sigmoid(value)
    out = (value * gate * mask).astype(BF16)
    for group, down, right, row in plan.cells():
        outs[group][down, right] = out[row : row + plan.slots, :]
    grad = cot_ref[...] * mask * (gate * (1.0 + value * (1.0 - gate)))
    dz_ref[...] = grad
    total = column(grad)
    put_rows(sums_out_ref, [total, column(grad * normed_two), column(grad * normed_side), total])


def back_second_kernel(
    plan, sums_ref, got_ref, sums_two_ref, got_two_ref, sums_z_ref, got_z_ref,
    first_ref, second_ref, side_ref, dz_ref, mask_ref, weights_ref, ready,
    grad_two_ref, grad_side_ref, dy_ref, out_ref, held_ref, patches_ref,
):
    cout = first_ref.shape[1]
    mask = wide(mask_ref, cout)
    sums, sums_two = sums_ref[...] + got_ref[...], sums_two_ref[...] + got_two_ref[...]
    sums_z = sums_z_ref[...] + got_z_ref[...]
    total = sums[4:5]
    grad = dz_ref[...]
    normed, factor = norm(second_ref[...], sums_two, 0, total)
    two = sums_two[2:3] * factor * (grad - mask * (sums_z[0:1] + normed * sums_z[1:2]) / total)
    normed, factor = norm(side_ref[...], sums, 2, total)
    side = sums_two[4:5] * factor * (grad - mask * (sums_z[0:1] + normed * sums_z[2:3]) / total)
    grad_side_ref[...] = side.astype(BF16)
    grad_two_ref[...] = two.astype(BF16)
    fill(plan, held_ref, two)
    unfold(plan, held_ref, patches_ref, -1)
    ready()
    back = nn(patches_ref[:, :cout], weights_ref[0])
    for tap in range(1, 9):
        back += nn(patches_ref[:, tap * cout : (tap + 1) * cout], weights_ref[tap])
    normed, _ = norm(first_ref[...], sums, 0, total)
    pre = normed * sums[5:6] + sums[6:7]
    grad = back * silu_slope(pre) * mask
    dy_ref[...] = grad
    put_rows(out_ref, [column(grad), column(grad * normed)])


def back_first(sums_ref, got_ref, sums_y_ref, got_y_ref, first_ref, dy_ref, mask_ref, grad_ref):
    cout = first_ref.shape[1]
    mask = wide(mask_ref, cout)
    sums, sums_y = sums_ref[...] + got_ref[...], sums_y_ref[...] + got_y_ref[...]
    total = sums[4:5]
    normed, factor = norm(first_ref[...], sums, 0, total)
    grad = sums[5:6] * factor * (dy_ref[...] - mask * (sums_y[0:1] + normed * sums_y[1:2]) / total)
    grad_ref[...] = grad.astype(BF16)


class Order:
    def __init__(self, batch, fsdp, owned):
        self.zs, self.quarter, self.owned = fsdp // 2, owned // batch, owned
        half = self.zs // 2
        self.parts = []
        for core in range(2):
            self.parts.append([(core, b, z) for b in (0, 2, 1, 3) for z in range(half)])
            self.parts.append([(core, b, z) for b in (0, 1, 2, 3) for z in range(half, self.zs)])

    def starts(self, place_ref):
        core, b, z = place_ref[0], place_ref[1], place_ref[2]
        for part in self.parts:
            for rel_core, rel_b, rel_z in part:
                row = ((z ^ rel_z) * 2 + (core ^ rel_core)) * self.owned + (b ^ rel_b) * self.quarter
                yield pl.multiple_of(row, self.quarter)


def correlate(order, place_ref, grads, patch_refs, out_refs, turned_ref, lhs_ref):
    quarter = order.quarter
    for index, grad in enumerate(grads):
        turned_ref[...] = grad.T
        for block, start in enumerate(order.starts(place_ref)):
            lhs_ref[block * quarter : (block + 1) * quarter, :] = turned_ref[pl.ds(start, quarter), :]
        left = lhs_ref[...]
        for tap, (ref, first, size) in patch_refs[index]:
            value = nn(left, ref[:, first : first + size]).astype(BF16)
            begin = 0
            for out_ref in out_refs:
                count = out_ref.shape[0]
                out_ref[:, tap] = value[begin : begin + count * quarter].reshape(count, quarter, size)
                begin += count * quarter


def weight_second_kernel(order, place_ref, grad_ref, patches_ref, *refs):
    outs, (turned_ref, lhs_ref) = refs[:-2], refs[-2:]
    cout = grad_ref.shape[1]
    taps = [(tap, (patches_ref, tap * cout, cout)) for tap in range(9)]
    correlate(order, place_ref, [grad_ref[...]], [taps], outs, turned_ref, lhs_ref)


def weight_first_kernel(
    order, place_ref, sums_ref, got_ref, sums_y_ref, got_y_ref, first_ref, dy_ref, mask_ref, side_ref, patches_ref, *refs
):
    grad_ref, outs, (turned_ref, lhs_ref) = refs[0], refs[1:-2], refs[-2:]
    back_first(sums_ref, got_ref, sums_y_ref, got_y_ref, first_ref, dy_ref, mask_ref, grad_ref)
    cin = patches_ref.shape[1] // 9
    taps = [(tap, (patches_ref, tap * cin, cin)) for tap in range(9)]
    center = [(9, (patches_ref, 4 * cin, cin))]
    correlate(order, place_ref, [grad_ref[...], side_ref[...]], [taps, center], outs, turned_ref, lhs_ref)


def plain_weight_kernel(taps, grad_ref, patches_ref, out_ref):
    turned = grad_ref[...].T
    channels = out_ref.shape[2]
    for index, tap in enumerate(taps):
        out_ref[index] = nn(turned, patches_ref[:, tap * channels : (tap + 1) * channels]).astype(BF16)


def input_kernel(
    plan, owned, place_ref, sums_z_ref, got_z_ref, sums_y_ref, got_y_ref, grad_ref, side_ref, weights_ref, ready, *refs
):
    outs, owns, (held_ref, moved_ref, total_ref) = refs[:3], refs[3:9], refs[9:]
    ready()
    sums = jnp.concatenate([sums_z_ref[...] + got_z_ref[...], sums_y_ref[...] + got_y_ref[...]], axis=0)
    first = (place_ref[2] * 2 + place_ref[0]) * owned
    spot = lax.broadcasted_iota(jnp.int32, sums.shape, 1)
    sums = jnp.where((spot >= first) & (spot < first + owned), sums, 0.0)
    sums = sum(sums[:, begin : begin + owned] for begin in range(0, sums.shape[1], owned))
    for row, ref in zip((8, 9, 1, 0, 2, 3), owns):
        ref[...] = sums[row : row + 1]
    rows = plan.rows
    fill(plan, held_ref, grad_ref[...].astype(F32))
    for index, (down, right) in enumerate(((0, 0), (0, 1), (1, 0), (1, 1))):
        for start, size, width in plan.segments():
            first = plan.margin + start + plan.slots * (down * width + right)
            moved_ref[index, start : start + size, :] = held_ref[first : first + size, :].astype(BF16)
    for py in range(2):
        for px in range(2):
            total = None
            for ky in (0, 2) if py else (1,):
                for kx in (0, 2) if px else (1,):
                    index = 2 * (ky == 0) + (kx == 0)
                    term = nn(moved_ref[index], weights_ref[ky * 3 + kx])
                    total = term if total is None else total + term
            if py + px == 0:
                total += nn(side_ref[...], weights_ref[9])
            total_ref[...] = total
            for group, down, right, row in plan.cells():
                outs[group][2 * down + py, 2 * right + px] = total_ref[row : row + plan.slots, :].astype(BF16)


def finish_kernel(order, place_ref, *refs):
    parts, outs = refs[:4], refs[4:]
    b, quarter = place_ref[1], order.quarter
    taps = outs[0].shape[0]
    for rel, ref in enumerate(parts):
        rows = pl.ds(pl.multiple_of((b ^ rel) * quarter, quarter), quarter)
        outs[0][:, rows, :] = ref[:taps].astype(F32)
        if len(outs) > 1:
            outs[1][rows, :] = ref[taps].astype(F32)


class Gathered:
    def __init__(self, arrays, place=None, order=None, labels=(), far=False):
        self.arrays, self.place, self.order, self.labels, self.far = arrays, place, order, labels, far

    def dims(self):
        if self.order is None:
            return self.arrays[0].shape
        taps, quarter, channels = self.arrays[0].shape[-3:]
        return taps, quarter * len(self.labels), channels

    def wrap(self, body, scalars, count):
        if self.order is None:
            return lambda *refs: body(*refs[: count + 1], lambda: None, *refs[count + 1 :])
        order, many, labels, far = self.order, len(self.arrays), self.labels, self.far

        def whole(place_ref, *refs):
            inputs, bundles, rest = refs[:count], refs[count : count + many], refs[count + many :]
            whole_ref, outs, semaphores = rest[0], rest[1:-1], rest[-1]
            if far:
                weights_ref, outs = outs[-1], outs[:-1]
                leave = pltpu.make_async_copy(weights_ref, whole_ref, semaphores.at[len(labels)])
            else:
                weights_ref = whole_ref
            core, b, z = place_ref[0], place_ref[1], place_ref[2]
            copies = []
            for index, at, rel_core, quarter, rel_z in labels:
                row = ((z ^ rel_z) * 2 + (core ^ rel_core)) * order.owned + quarter(b) * order.quarter
                rows = pl.ds(pl.multiple_of(row, order.quarter), order.quarter)
                copies.append(
                    pltpu.make_async_copy(bundles[index].at[at], weights_ref.at[:, rows, :], semaphores.at[len(copies)])
                )
            for copy in copies:
                copy.start()

            def ready():
                for copy in copies:
                    copy.wait()
                if far:
                    leave.start()

            body(*inputs, weights_ref, ready, *outs)
            if far:
                leave.wait()

        return whole


def call(body, out_shapes, *args, scratch=(), scalars=0, flops=0, weights=None, far=False, whole=True):
    vmem = pl.BlockSpec(memory_space=pltpu.VMEM)
    inner = vmem if whole else pl.BlockSpec(memory_space=pltpu.MemorySpace.HBM)
    if far:
        args = args[:scalars] + tuple(
            pltpu.with_memory_space_constraint(arg, pltpu.MemorySpace.HBM) for arg in args[scalars:]
        )
    first_out = vmem
    specs = [pl.BlockSpec(memory_space=pltpu.SMEM)] * scalars + [inner] * (len(args) - scalars)
    if weights is not None:
        body = weights.wrap(body, scalars, len(args))
        scratch = list(scratch)
        if weights.order is None:
            args = args + tuple(weights.arrays)
            specs = specs + [vmem]
        else:
            args = (weights.place,) + args + tuple(weights.arrays)
            specs = [pl.BlockSpec(memory_space=pltpu.SMEM)] + specs + [pl.BlockSpec(memory_space=pl.ANY)] * len(weights.arrays)
            out_shapes = [shape(weights.dims(), BF16)] + list(out_shapes)
            if weights.far:
                scratch += [pltpu.VMEM(weights.dims(), BF16)]
                first_out = pl.BlockSpec(memory_space=pltpu.MemorySpace.HBM)
            scratch += [pltpu.SemaphoreType.DMA((len(weights.labels) + weights.far,))]
    many = isinstance(out_shapes, (list, tuple))
    moved = sum(arg.size * arg.dtype.itemsize for arg in args)
    return pl.pallas_call(
        body,
        in_specs=specs,
        out_specs=[first_out] + [vmem] * (len(out_shapes) - 1) if many else vmem,
        out_shape=list(out_shapes) if many else out_shapes,
        scratch_shapes=list(scratch),
        compiler_params=pltpu.CompilerParams(vmem_limit_bytes=VMEM_LIMIT),
        cost_estimate=pl.CostEstimate(flops=flops, bytes_accessed=moved, transcendentals=0),
    )(*args)


def shape(dims, dtype=F32):
    return jax.ShapeDtypeStruct(tuple(dims), dtype)


def exchange(value, axis, count, bit):
    return lax.ppermute(value, axis, [(index, index ^ bit) for index in range(count)])


def bits(count):
    return [1 << index for index in range(count.bit_length() - 1)]


def after(value, *others):
    return lax.optimization_barrier((value, *others))[0]


def together(*values):
    return list(lax.optimization_barrier(values))


def steps_of(axes):
    return [(axis, count, bit) for axis, count in axes for bit in bits(count)]


def sum_over(value, steps, hooks=None):
    got = jnp.zeros_like(value)
    for index, (axis, count, bit) in enumerate(steps):
        if index:
            value = value + got
        if hooks and index in hooks:
            value = hooks[index](value)
        got = exchange(value, axis, count, bit)
    return value, got


def parity(b):
    return (b ^ (b // 2)) % 2


def rotated(rel):
    return lambda b: b ^ rel


def of_half(other, index):
    return lambda b: 2 * (parity(b) ^ other) + index


def share_kernel(order, place_ref, first_ref, side_ref, second_ref, first_out_ref, second_out_ref, semaphores):
    b, size, copies = place_ref[1], order.quarter, []

    def copy(source, target):
        copies.append(pltpu.make_async_copy(source, target, semaphores.at[len(copies)]))
        copies[-1].start()

    rows = pl.ds(pl.multiple_of(b * size, size), size)
    copy(first_ref.at[:, rows, :], first_out_ref.at[pl.ds(0, 9)])
    copy(side_ref.at[rows, :], first_out_ref.at[9])
    for index in range(2):
        rows = pl.ds(pl.multiple_of((2 * parity(b) + index) * size, size), size)
        copy(second_ref.at[:, rows, :], second_out_ref.at[index])
    for started in copies:
        started.wait()


def spread_line(order, share, fsdp):
    return [share] + [exchange(share, "fsdp", fsdp, 2 * rel) for rel in range(1, order.zs)]


def double_line(order, share, fsdp):
    held, rels = share[:, None], [0]
    for bit in reversed(bits(order.zs)):
        held = jnp.concatenate([held, exchange(held, "fsdp", fsdp, 2 * bit)], axis=1)
        rels = rels + [rel ^ bit for rel in rels]
    return held, rels


def both_cores(bundles, fsdp):
    return bundles + [exchange(value, "fsdp", fsdp, 1) for value in bundles]


def spread_quarters(line, batch):
    return [line] + [exchange(line, "batch", batch, rel) for rel in (1, 2, 3)]


def quarter_labels(order):
    return [
        (4 * core + rel, (z,), core, rotated(rel), z) for core in range(2) for rel in range(4) for z in range(order.zs)
    ]


def spread_halves(line, batch):
    return [exchange(line[0], "batch", batch, 1), exchange(line[1], "batch", batch, 2)]


def half_labels(rels):
    labels = []
    for core in range(2):
        for at, z in enumerate(rels):
            for index in range(2):
                labels.append((3 * core, (index, at), core, of_half(0, index), z))
                labels.append((3 * core + 1 + index, (at,), core, of_half(1, index), z))
    return labels


def reduce_cores(parts, fsdp):
    keep_p, keep_q, send_p, send_q = parts
    return keep_p + exchange(send_p, "fsdp", fsdp, 1), keep_q + exchange(send_q, "fsdp", fsdp, 1)


def reduce_line(pieces, fsdp):
    total = pieces[0].astype(F32)
    for rel in range(1, len(pieces)):
        total = total + exchange(pieces[rel], "fsdp", fsdp, 2 * rel).astype(F32)
    return total


def first_in_plane(halves, batch):
    half_p, half_q = halves
    n_p, n_q = half_p.shape[0] // 2, half_q.shape[0] // 2
    got_p = exchange(half_p[n_p:], "batch", batch, 1)
    got_q = exchange(half_q[n_q:], "batch", batch, 2)
    return [half_p[:n_p] + got_p, half_q[:n_q] + got_q]


def then_in_plane(halves, batch):
    half_p, half_q = halves
    n_p, n_q = half_p.shape[0] // 2, half_q.shape[0] // 2
    got_p = exchange(half_p[n_p:], "batch", batch, 2)
    got_q = exchange(half_q[n_q:], "batch", batch, 1)
    low, high = half_p[:n_p] + got_p, half_q[:n_q] + got_q
    return [low[index] for index in range(n_p)] + [high[index] for index in range(n_q)]


def finish_weights(order, place, quarter, batch, outs):
    quarter = quarter.astype(BF16)
    spread = [quarter] + [exchange(quarter, "batch", batch, rel) for rel in (1, 2, 3)]
    return call(functools.partial(finish_kernel, order), outs, place, *spread, scalars=1)


def local(
    x_small,
    x_mid,
    x_large,
    cot_small,
    cot_mid,
    cot_large,
    counts,
    w_first,
    gain_first,
    shift_first,
    w_second,
    gain_second,
    shift_second,
    w_short,
    gain_short,
    shift_short,
    *,
    batch,
    fsdp,
):
    fields = (x_small, x_mid, x_large)
    cots = (cot_small, cot_mid, cot_large)
    slots, cin, owned = x_small.shape[0], x_small.shape[3], gain_first.shape[0]
    cout = owned * fsdp
    plan = Plan([cot.shape[1] for cot in cots], slots)
    rows, span = plan.rows, plan.span
    everywhere = steps_of((("fsdp", fsdp), ("batch", batch)))
    me = lax.axis_index("fsdp")
    fast = batch == 4 and fsdp >= 4 and fsdp & (fsdp - 1) == 0 and owned % (ROWS * batch) == 0
    order = Order(batch, fsdp, owned) if fast else None
    if fast:
        everywhere = everywhere[:1] + everywhere[-2:] + everywhere[1:-2]
    place = jnp.stack([me % 2, lax.axis_index("batch"), me // 2]).astype(jnp.int32)

    own_first = jnp.transpose(w_first, (0, 1, 3, 2)).reshape(9, owned, cin)
    own_second = jnp.transpose(w_second, (0, 1, 3, 2)).reshape(9, owned, cout)
    own_side = jnp.transpose(w_short)
    vectors = [gain_first, shift_first, gain_second, shift_second, gain_short, shift_short]
    patches, cot_rows, mask, vec = call(
        functools.partial(prepare_kernel, plan, owned),
        [shape((rows, 9 * cin), BF16), shape((rows, cout)), shape((rows, 128)), shape((8, cout))],
        place,
        counts,
        *[jnp.transpose(value, (1, 2, 0, 3)) for value in fields + cots],
        *[value.reshape(1, owned) for value in vectors],
        scratch=[pltpu.VMEM((4, plan.margin + rows, cin), F32)],
        scalars=2,
        far=True,
    )
    if fast:
        share_first, share_second = call(
            functools.partial(share_kernel, order),
            [shape((10, order.quarter, cin), BF16), shape((2, 9, order.quarter, cout), BF16)],
            place,
            own_first,
            own_side,
            own_second,
            scratch=[pltpu.SemaphoreType.DMA((4,))],
            scalars=1,
            far=True,
            whole=False,
        )
        line_first = spread_line(order, share_first, fsdp)
        line_first = after(jnp.stack(line_first), patches, vec)
        line_second, rels = double_line(order, after(share_second, line_first), fsdp)
        kern_first = Gathered(both_cores(spread_quarters(line_first, batch), fsdp), place, order, quarter_labels(order), True)
    else:
        kern_first = Gathered([lax.all_gather(jnp.concatenate([own_first, own_side[None]]), "fsdp", axis=1, tiled=True)])
        kern_second = Gathered([lax.all_gather(own_second, "fsdp", axis=1, tiled=True)])
    flops = 2 * rows * cout * cin * 9
    *whole, first, side, sums = call(
        first_kernel,
        [shape((rows, cout)), shape((rows, cout)), shape((8, cout))],
        patches,
        mask,
        vec,
        flops=flops,
        weights=kern_first,
    )
    hooks = None
    if fast:
        kern_first = Gathered(whole)
        plane_second = []

        def spread_second(value):
            plane_second.extend(spread_halves(after(line_second, value), batch))
            return value

        hooks = {3: spread_second}
    sums = sum_over(sums, everywhere, hooks)
    if fast:
        bundles = [after(value, *sums) for value in plane_second]
        kern_second = Gathered(both_cores([line_second] + bundles, fsdp), place, order, half_labels(rels))
    *whole, second, patches_two, sums_two = call(
        functools.partial(second_kernel, plan),
        [shape((rows, cout)), shape((rows, 9 * cout), BF16), shape((8, cout))],
        *sums,
        first,
        mask,
        vec,
        scratch=[pltpu.VMEM((span, cout), F32)],
        flops=2 * flops,
        weights=kern_second,
    )
    if fast:
        kern_second = Gathered(whole)
    sums_two = sum_over(sums_two, everywhere)
    *outputs, dz, sums_z = call(
        functools.partial(output_kernel, plan),
        [shape((length, length, slots, cout), BF16) for length in plan.sides] + [shape((rows, cout)), shape((8, cout))],
        *sums,
        *sums_two,
        second,
        side,
        cot_rows,
        mask,
        flops=50 * rows * cout,
    )
    sums_z = sum_over(sums_z, everywhere)
    grad_two, grad_side, dy, sums_y = call(
        functools.partial(back_second_kernel, plan),
        [shape((rows, cout), BF16), shape((rows, cout), BF16), shape((rows, cout)), shape((8, cout))],
        *sums,
        *sums_two,
        *sums_z,
        first,
        second,
        side,
        dz,
        mask,
        scratch=[pltpu.VMEM((span, cout), F32), pltpu.VMEM((rows, 9 * cout), BF16)],
        flops=2 * flops,
        weights=kern_second,
    )
    hooks = None
    if fast:
        turned = [pltpu.VMEM((cout, rows), BF16), pltpu.VMEM((cout, rows), BF16)]
        parts_two, halves_two = [], []

        def weights_second(value):
            parts_two.extend(
                call(
                    functools.partial(weight_second_kernel, order),
                    [shape((len(part), 9, order.quarter, cout), BF16) for part in order.parts],
                    place,
                    after(grad_two, value),
                    patches_two,
                    scratch=turned,
                    scalars=1,
                    flops=2 * flops,
                )
            )
            halves_two.extend(reduce_cores(parts_two, fsdp))
            return value

        def over_plane(value):
            value, *halves_two[:] = together(value, *halves_two)
            return value

        hooks = {1: weights_second, 2: lambda value: after(value, *parts_two), 3: over_plane}
    sums_y = sum_over(sums_y, everywhere, hooks)
    if fast:
        grad_one, *parts_one = call(
            functools.partial(weight_first_kernel, order),
            [shape((rows, cout), BF16)] + [shape((len(part), 10, order.quarter, cin), BF16) for part in order.parts],
            place,
            *sums,
            *sums_y,
            first,
            dy,
            mask,
            grad_side,
            patches,
            scratch=turned,
            scalars=1,
            flops=flops,
        )
        halves_two = first_in_plane(halves_two, batch)
        halves_one = reduce_cores(parts_one, fsdp)
        grad_late = after(grad_one, *halves_one)
        *halves_one, last = together(*halves_one, halves_two[0])
        halves_two[0] = last
        halves_one = first_in_plane(halves_one, batch)
        quarter_two = reduce_line(then_in_plane(halves_two, batch), fsdp)
        quarter_one = reduce_line(then_in_plane(halves_one, batch), fsdp)
        dw_second = finish_weights(order, place, quarter_two, batch, [shape((9, owned, cout))])[0]
        dw_first, dw_side = finish_weights(
            order, place, quarter_one, batch, [shape((9, owned, cin)), shape((owned, cin))]
        )
    else:
        grad_one = call(back_first, shape((rows, cout), BF16), *sums, *sums_y, first, dy, mask)
        taps = tuple(range(9))
        whole = [
            call(functools.partial(plain_weight_kernel, taps), shape((9, cout, cout), BF16), grad_two, patches_two),
            call(functools.partial(plain_weight_kernel, taps), shape((9, cout, cin), BF16), grad_one, patches),
            call(functools.partial(plain_weight_kernel, (4,)), shape((1, cout, cin), BF16), grad_side, patches),
        ]
        dw_second, dw_first, dw_side = [
            lax.psum(lax.psum_scatter(value, "fsdp", scatter_dimension=1, tiled=True), "batch").astype(F32)
            for value in whole
        ]
        dw_side = dw_side[0]
        grad_late = grad_one
    *input_grads, shift_1, gain_1, gain_2, shift_2, gain_3, shift_3 = call(
        functools.partial(input_kernel, plan, owned),
        [shape((2 * length, 2 * length, slots, cin), BF16) for length in plan.sides] + [shape((1, owned))] * 6,
        place,
        *sums_z,
        *sums_y,
        grad_late,
        grad_side,
        scratch=[pltpu.VMEM((span, cout), F32), pltpu.VMEM((4, rows, cout), BF16), pltpu.VMEM((rows, cin), F32)],
        scalars=1,
        flops=flops,
        weights=kern_first,
    )
    def as_weight(value):
        return jnp.transpose(value.reshape(3, 3, owned, value.shape[2]), (0, 1, 3, 2))

    return (
        *[jnp.transpose(value, (2, 0, 1, 3)) for value in (*outputs, *input_grads)],
        as_weight(dw_first),
        gain_1[0],
        shift_1[0],
        as_weight(dw_second),
        gain_2[0],
        shift_2[0],
        jnp.transpose(dw_side),
        gain_3[0],
        shift_3[0],
    )


def solution(mesh):
    split = ("batch", "fsdp")
    image = P(split, None, None, None)
    kernel = P(None, None, None, "fsdp")
    vector = P("fsdp")
    in_specs = (image,) * 6 + (
        P(split, None),
        kernel,
        vector,
        vector,
        kernel,
        vector,
        vector,
        P(None, "fsdp"),
        vector,
        vector,
    )
    out_specs = (image,) * 6 + (
        kernel,
        vector,
        vector,
        kernel,
        vector,
        vector,
        P(None, "fsdp"),
        vector,
        vector,
    )
    body = functools.partial(local, batch=mesh.shape["batch"], fsdp=mesh.shape["fsdp"])
    return jax.shard_map(body, mesh=mesh, in_specs=in_specs, out_specs=out_specs, check_vma=False)
```

```python
import functools

import jax
import jax.numpy as jnp
import numpy as np
from jax import lax
from jax.experimental import pallas as pl
from jax.experimental.pallas import tpu as pltpu
from jax.sharding import PartitionSpec as P

EPSILON = 1e-05
F32 = jnp.float32
BF16 = jnp.bfloat16
ROWS = 16
KN = dict(vm=24, pq=0, z2=0, z1=0, ag2=0, ag1=0, gx2=0, gx1=0, k7=0, k7d=3, gate5=1, dl5=2, dlh=3, cost=1, fin=0, gcore=0)
VMEM_LIMIT = KN["vm"] * 2**20


def up(value, step):
    return -(-value // step) * step


class Plan:
    def __init__(self, sides, slots):
        self.sides, self.slots = sides, slots
        self.starts, self.sizes, row = [], [], 0
        for index, side in enumerate(sides):
            width = side + 1
            after = sides[index + 1] + 1 if index + 1 < len(sides) else 0
            size = up(slots * (width * width + max(0, width + 1 - after)), ROWS)
            self.starts.append(row)
            self.sizes.append(size)
            row += size
        self.rows = row
        self.margin = up(slots * (max(sides) + 2), ROWS)
        self.span = self.rows + 2 * self.margin

    def segments(self):
        return list(zip(self.starts, self.sizes, [side + 1 for side in self.sides]))


    def cells(self):
        for group, (start, side) in enumerate(zip(self.starts, self.sides)):
            for down in range(side):
                for right in range(side):
                    yield group, down, right, start + self.slots * ((down + 1) * (side + 1) + right + 1)


def nn(left, right):
    return lax.dot_general(left, right, (((1,), (0,)), ((), ())), preferred_element_type=F32)


def nt(left, right):
    return lax.dot_general(left, right, (((1,), (1,)), ((), ())), preferred_element_type=F32)


def column(value):
    return jnp.sum(value, axis=0, keepdims=True)


def wide(mask_ref, channels):
    return jnp.concatenate([mask_ref[...]] * (channels // mask_ref.shape[1]), axis=1)


def silu_slope(value):
    gate = jax.nn.sigmoid(value)
    return gate * (1.0 + value * (1.0 - gate))


def norm(value, sums, row, total):
    center = sums[row : row + 1] / total
    spread = sums[row + 1 : row + 2] / total - center * center
    factor = lax.rsqrt(spread + EPSILON)
    return (value - center) * factor, factor


def put_rows(ref, rows):
    for index, row in enumerate(rows):
        ref[index : index + 1, :] = row
    ref[len(rows) :, :] = jnp.zeros((ref.shape[0] - len(rows), ref.shape[1]), F32)


def offsets(plan, width):
    return [plan.slots * (dy * width + dx) for dy in (-1, 0, 1) for dx in (-1, 0, 1)]


def unfold(plan, padded_ref, out_ref, sign):
    channels = padded_ref.shape[1]
    for start, size, width in plan.segments():
        for tap, offset in enumerate(offsets(plan, width)):
            first = plan.margin + start + sign * offset
            out_ref[start : start + size, tap * channels : (tap + 1) * channels] = padded_ref[
                first : first + size, :
            ].astype(BF16)


def fill(plan, padded_ref, value):
    edge = jnp.zeros((plan.margin, padded_ref.shape[1]), F32)
    padded_ref[: plan.margin, :] = edge
    padded_ref[plan.margin : plan.margin + plan.rows, :] = value
    padded_ref[plan.margin + plan.rows :, :] = edge


def prepare_kernel(plan, owned, place_ref, counts_ref, *refs):
    fields, cots, vectors = refs[:3], refs[3:6], refs[6:12]
    patches_ref, cot_ref, mask_ref, vec_ref, held_ref = refs[12:]
    slots, channels = plan.slots, fields[0].shape[3]
    held_ref[...] = jnp.zeros(held_ref.shape, F32)
    cot_ref[...] = jnp.zeros(cot_ref.shape, F32)
    mask_ref[...] = jnp.zeros(mask_ref.shape, F32)
    cout = vec_ref.shape[1]
    first = (place_ref[2] * 2 + place_ref[0]) * owned
    spot = lax.broadcasted_iota(jnp.int32, (owned, cout), 1) - lax.broadcasted_iota(jnp.int32, (owned, cout), 0)
    own = ((spot == first) & (place_ref[1] == 0)).astype(BF16)
    held = [ref[...].astype(F32) for ref in vectors] + [jnp.zeros((vec_ref.shape[0] - 6, owned), F32)]
    vec_ref[...] = nn(jnp.concatenate(held, axis=0).astype(BF16), own)
    slot = lax.broadcasted_iota(jnp.int32, (slots, mask_ref.shape[1]), 0)
    live = [(slot < counts_ref[0, group]).astype(F32) for group in range(3)]
    for group, down, right, row in plan.cells():
        mask_ref[row : row + slots, :] = live[group]
        cot_ref[row : row + slots, :] = cots[group][down, right].astype(F32)
        for py in range(2):
            for px in range(2):
                first = plan.margin + row
                held_ref[2 * py + px, first : first + slots, :] = fields[group][2 * down + py, 2 * right + px].astype(F32)
    for start, size, width in plan.segments():
        for ky in range(3):
            for kx in range(3):
                tap = ky * 3 + kx
                shift = plan.slots * (width * (ky == 0) + (kx == 0))
                first = plan.margin + start - shift
                patches_ref[start : start + size, tap * channels : (tap + 1) * channels] = held_ref[
                    2 * (ky != 1) + (kx != 1), first : first + size, :
                ].astype(BF16)


def first_kernel(patches_ref, mask_ref, vec_ref, weights_ref, ready, first_ref, side_ref, sums_ref):
    ready()
    cin = weights_ref.shape[2]
    cout = weights_ref.shape[1]
    total = nt(patches_ref[:, :cin], weights_ref[0])
    for tap in range(1, 9):
        total += nt(patches_ref[:, tap * cin : (tap + 1) * cin], weights_ref[tap])
    side = nt(patches_ref[:, 4 * cin : 5 * cin], weights_ref[9])
    first_ref[...] = total
    side_ref[...] = side
    mask = wide(mask_ref, cout)
    put_rows(
        sums_ref,
        [
            column(mask * total),
            column(mask * total * total),
            column(mask * side),
            column(mask * side * side),
            column(mask),
            vec_ref[0:1],
            vec_ref[1:2],
        ],
    )


def second_kernel(
    plan, sums_ref, got_ref, first_ref, mask_ref, vec_ref, weights_ref, ready, second_ref, patches_ref, out_ref, held_ref
):
    cout = first_ref.shape[1]
    mask = wide(mask_ref, cout)
    sums = sums_ref[...] + got_ref[...]
    normed, _ = norm(first_ref[...], sums, 0, sums[4:5])
    pre = normed * sums[5:6] + sums[6:7]
    fill(plan, held_ref, jax.nn.silu(pre) * mask)
    unfold(plan, held_ref, patches_ref, 1)
    ready()
    total = nt(patches_ref[:, :cout], weights_ref[0])
    for tap in range(1, 9):
        total += nt(patches_ref[:, tap * cout : (tap + 1) * cout], weights_ref[tap])
    second_ref[...] = total
    put_rows(
        out_ref, [column(mask * total), column(mask * total * total)] + [vec_ref[row : row + 1] for row in range(2, 6)]
    )


def output_kernel(
    plan, sums_ref, got_ref, sums_two_ref, got_two_ref, second_ref, side_ref, cot_ref, mask_ref, *refs
):
    outs, (dz_ref, sums_out_ref) = refs[:3], refs[3:]
    cout = second_ref.shape[1]
    mask = wide(mask_ref, cout)
    sums, sums_two = sums_ref[...] + got_ref[...], sums_two_ref[...] + got_two_ref[...]
    total = sums[4:5]
    normed_two, _ = norm(second_ref[...], sums_two, 0, total)
    normed_side, _ = norm(side_ref[...], sums, 2, total)
    value = (normed_two * sums_two[2:3] + sums_two[3:4]) + (normed_side * sums_two[4:5] + sums_two[5:6])
    gate = jax.nn.sigmoid(value)
    out = (value * gate * mask).astype(BF16)
    for group, down, right, row in plan.cells():
        outs[group][down, right] = out[row : row + plan.slots, :]
    grad = cot_ref[...] * mask * (gate * (1.0 + value * (1.0 - gate)))
    dz_ref[...] = grad
    total = column(grad)
    put_rows(sums_out_ref, [total, column(grad * normed_two), column(grad * normed_side), total])


def back_second_kernel(
    plan, sums_ref, got_ref, sums_two_ref, got_two_ref, sums_z_ref, got_z_ref,
    first_ref, second_ref, side_ref, dz_ref, mask_ref, weights_ref, ready,
    grad_two_ref, grad_side_ref, dy_ref, out_ref, held_ref, patches_ref,
):
    cout = first_ref.shape[1]
    mask = wide(mask_ref, cout)
    sums, sums_two = sums_ref[...] + got_ref[...], sums_two_ref[...] + got_two_ref[...]
    sums_z = sums_z_ref[...] + got_z_ref[...]
    total = sums[4:5]
    grad = dz_ref[...]
    normed, factor = norm(second_ref[...], sums_two, 0, total)
    two = sums_two[2:3] * factor * (grad - mask * (sums_z[0:1] + normed * sums_z[1:2]) / total)
    normed, factor = norm(side_ref[...], sums, 2, total)
    side = sums_two[4:5] * factor * (grad - mask * (sums_z[0:1] + normed * sums_z[2:3]) / total)
    grad_side_ref[...] = side.astype(BF16)
    grad_two_ref[...] = two.astype(BF16)
    fill(plan, held_ref, two)
    unfold(plan, held_ref, patches_ref, -1)
    ready()
    back = nn(patches_ref[:, :cout], weights_ref[0])
    for tap in range(1, 9):
        back += nn(patches_ref[:, tap * cout : (tap + 1) * cout], weights_ref[tap])
    normed, _ = norm(first_ref[...], sums, 0, total)
    pre = normed * sums[5:6] + sums[6:7]
    grad = back * silu_slope(pre) * mask
    dy_ref[...] = grad
    put_rows(out_ref, [column(grad), column(grad * normed)])


def back_first(sums_ref, got_ref, sums_y_ref, got_y_ref, first_ref, dy_ref, mask_ref, grad_ref):
    cout = first_ref.shape[1]
    mask = wide(mask_ref, cout)
    sums, sums_y = sums_ref[...] + got_ref[...], sums_y_ref[...] + got_y_ref[...]
    total = sums[4:5]
    normed, factor = norm(first_ref[...], sums, 0, total)
    grad = sums[5:6] * factor * (dy_ref[...] - mask * (sums_y[0:1] + normed * sums_y[1:2]) / total)
    grad_ref[...] = grad.astype(BF16)


class Order:
    def __init__(self, batch, fsdp, owned):
        self.zs, self.quarter, self.owned = fsdp // 2, owned // batch, owned
        half = self.zs // 2
        self.parts = []
        for core in range(2):
            self.parts.append([(core, b, z) for b in (0, 2, 1, 3) for z in range(half)])
            self.parts.append([(core, b, z) for b in (0, 1, 2, 3) for z in range(half, self.zs)])

    def starts(self, place_ref):
        core, b, z = place_ref[0], place_ref[1], place_ref[2]
        for part in self.parts:
            for rel_core, rel_b, rel_z in part:
                row = ((z ^ rel_z) * 2 + (core ^ rel_core)) * self.owned + (b ^ rel_b) * self.quarter
                yield pl.multiple_of(row, self.quarter)


def correlate(order, place_ref, grads, patch_refs, out_refs, turned_ref, lhs_ref):
    quarter = order.quarter
    for index, grad in enumerate(grads):
        turned_ref[...] = grad.T
        for block, start in enumerate(order.starts(place_ref)):
            lhs_ref[block * quarter : (block + 1) * quarter, :] = turned_ref[pl.ds(start, quarter), :]
        left = lhs_ref[...]
        for tap, (ref, first, size) in patch_refs[index]:
            value = nn(left, ref[:, first : first + size]).astype(BF16)
            begin = 0
            for out_ref in out_refs:
                count = out_ref.shape[0]
                out_ref[:, tap] = value[begin : begin + count * quarter].reshape(count, quarter, size)
                begin += count * quarter


def weight_second_kernel(order, place_ref, grad_ref, patches_ref, *refs):
    outs, (turned_ref, lhs_ref) = refs[:-2], refs[-2:]
    cout = grad_ref.shape[1]
    taps = [(tap, (patches_ref, tap * cout, cout)) for tap in range(9)]
    correlate(order, place_ref, [grad_ref[...]], [taps], outs, turned_ref, lhs_ref)


def weight_first_kernel(
    order, place_ref, sums_ref, got_ref, sums_y_ref, got_y_ref, first_ref, dy_ref, mask_ref, side_ref, patches_ref, *refs
):
    grad_ref, outs, (turned_ref, lhs_ref) = refs[0], refs[1:-2], refs[-2:]
    back_first(sums_ref, got_ref, sums_y_ref, got_y_ref, first_ref, dy_ref, mask_ref, grad_ref)
    cin = patches_ref.shape[1] // 9
    taps = [(tap, (patches_ref, tap * cin, cin)) for tap in range(9)]
    center = [(9, (patches_ref, 4 * cin, cin))]
    correlate(order, place_ref, [grad_ref[...], side_ref[...]], [taps, center], outs, turned_ref, lhs_ref)


def plain_weight_kernel(taps, grad_ref, patches_ref, out_ref):
    turned = grad_ref[...].T
    channels = out_ref.shape[2]
    for index, tap in enumerate(taps):
        out_ref[index] = nn(turned, patches_ref[:, tap * channels : (tap + 1) * channels]).astype(BF16)


def input_kernel(
    plan, owned, place_ref, sums_z_ref, got_z_ref, sums_y_ref, got_y_ref, grad_ref, side_ref, weights_ref, ready, *refs
):
    outs, owns, (held_ref, moved_ref, total_ref) = refs[:3], refs[3:9], refs[9:]
    ready()
    sums = jnp.concatenate([sums_z_ref[...] + got_z_ref[...], sums_y_ref[...] + got_y_ref[...]], axis=0)
    first = (place_ref[2] * 2 + place_ref[0]) * owned
    spot = lax.broadcasted_iota(jnp.int32, sums.shape, 1)
    sums = jnp.where((spot >= first) & (spot < first + owned), sums, 0.0)
    sums = sum(sums[:, begin : begin + owned] for begin in range(0, sums.shape[1], owned))
    for row, ref in zip((8, 9, 1, 0, 2, 3), owns):
        ref[...] = sums[row : row + 1]
    rows = plan.rows
    fill(plan, held_ref, grad_ref[...].astype(F32))
    for index, (down, right) in enumerate(((0, 0), (0, 1), (1, 0), (1, 1))):
        for start, size, width in plan.segments():
            first = plan.margin + start + plan.slots * (down * width + right)
            moved_ref[index, start : start + size, :] = held_ref[first : first + size, :].astype(BF16)
    for py in range(2):
        for px in range(2):
            total = None
            for ky in (0, 2) if py else (1,):
                for kx in (0, 2) if px else (1,):
                    index = 2 * (ky == 0) + (kx == 0)
                    term = nn(moved_ref[index], weights_ref[ky * 3 + kx])
                    total = term if total is None else total + term
            if py + px == 0:
                total += nn(side_ref[...], weights_ref[9])
            total_ref[...] = total
            for group, down, right, row in plan.cells():
                outs[group][2 * down + py, 2 * right + px] = total_ref[row : row + plan.slots, :].astype(BF16)


def finish_kernel(order, place_ref, *refs):
    parts, outs = refs[:4], refs[4:]
    b, quarter = place_ref[1], order.quarter
    taps = outs[0].shape[0]
    for rel, ref in enumerate(parts):
        rows = pl.ds(pl.multiple_of((b ^ rel) * quarter, quarter), quarter)
        outs[0][:, rows, :] = ref[:taps].astype(F32)
        if len(outs) > 1:
            outs[1][rows, :] = ref[taps].astype(F32)


class Gathered:
    def __init__(self, arrays, place=None, order=None, labels=(), far=False):
        self.arrays, self.place, self.order, self.labels, self.far = arrays, place, order, labels, far
        self.taps = max((label[2] + label[3] for label in labels), default=0)

    def dims(self):
        if self.order is None:
            return self.arrays[0].shape
        return self.taps, 2 * self.order.zs * self.order.owned, self.arrays[0].shape[-1]

    def wrap(self, body, scalars, count):
        if self.order is None:
            return lambda *refs: body(*refs[: count + 1], lambda: None, *refs[count + 1 :])
        order, many, labels, far = self.order, len(self.arrays), self.labels, self.far

        def whole(place_ref, *refs):
            inputs, bundles, rest = refs[:count], refs[count : count + many], refs[count + many :]
            whole_ref, outs, semaphores = rest[0], rest[1:-1], rest[-1]
            if far:
                weights_ref, outs = outs[-1], outs[:-1]
                leave = pltpu.make_async_copy(weights_ref, whole_ref, semaphores.at[len(labels)])
            else:
                weights_ref = whole_ref
            core, b, z = place_ref[0], place_ref[1], place_ref[2]
            copies = []
            for index, at, tap, taps, rel_core, owner, quarter in labels:
                row = (owner(z) * 2 + (core ^ rel_core)) * order.owned + quarter(b) * order.quarter
                rows = pl.ds(pl.multiple_of(row, order.quarter), order.quarter)
                target = weights_ref.at[pl.ds(tap, taps), rows, :]
                copies.append(pltpu.make_async_copy(bundles[index].at[at], target, semaphores.at[len(copies)]))
            for copy in copies:
                copy.start()

            def ready():
                for copy in copies:
                    copy.wait()
                if far:
                    leave.start()

            body(*inputs, weights_ref, ready, *outs)
            if far:
                leave.wait()

        return whole


def call(body, out_shapes, *args, scratch=(), scalars=0, flops=0, weights=None, far=False, whole=True):
    vmem = pl.BlockSpec(memory_space=pltpu.VMEM)
    inner = vmem if whole else pl.BlockSpec(memory_space=pltpu.MemorySpace.HBM)
    if far:
        args = args[:scalars] + tuple(
            pltpu.with_memory_space_constraint(arg, pltpu.MemorySpace.HBM) for arg in args[scalars:]
        )
    first_out = vmem
    specs = [pl.BlockSpec(memory_space=pltpu.SMEM)] * scalars + [inner] * (len(args) - scalars)
    if weights is not None:
        body = weights.wrap(body, scalars, len(args))
        scratch = list(scratch)
        if weights.order is None:
            args = args + tuple(weights.arrays)
            specs = specs + [vmem]
        else:
            args = (weights.place,) + args + tuple(weights.arrays)
            specs = [pl.BlockSpec(memory_space=pltpu.SMEM)] + specs + [pl.BlockSpec(memory_space=pl.ANY)] * len(weights.arrays)
            out_shapes = [shape(weights.dims(), BF16)] + list(out_shapes)
            if weights.far:
                scratch += [pltpu.VMEM(weights.dims(), BF16)]
                first_out = pl.BlockSpec(memory_space=pltpu.MemorySpace.HBM)
            scratch += [pltpu.SemaphoreType.DMA((len(weights.labels) + weights.far,))]
    many = isinstance(out_shapes, (list, tuple))
    moved = sum(arg.size * arg.dtype.itemsize for arg in args)
    return pl.pallas_call(
        body,
        in_specs=specs,
        out_specs=[first_out] + [vmem] * (len(out_shapes) - 1) if many else vmem,
        out_shape=list(out_shapes) if many else out_shapes,
        scratch_shapes=list(scratch),
        compiler_params=pltpu.CompilerParams(vmem_limit_bytes=VMEM_LIMIT),
        cost_estimate=pl.CostEstimate(flops=int(flops * KN["cost"]), bytes_accessed=moved, transcendentals=0),
    )(*args)


def shape(dims, dtype=F32):
    return jax.ShapeDtypeStruct(tuple(dims), dtype)


def exchange(value, axis, count, bit):
    return lax.ppermute(value, axis, [(index, index ^ bit) for index in range(count)])


def bits(count):
    return [1 << index for index in range(count.bit_length() - 1)]


def after(value, *others):
    return lax.optimization_barrier((value, *others))[0]


def together(*values):
    return list(lax.optimization_barrier(values))


def steps_of(axes):
    return [(axis, count, bit) for axis, count in axes for bit in bits(count)]


def sum_over(value, steps, hooks=None):
    got = jnp.zeros_like(value)
    for index, (axis, count, bit) in enumerate(steps):
        if index:
            value = value + got
        if hooks and index in hooks:
            value = hooks[index](value)
        got = exchange(value, axis, count, bit)
    return value, got


def parity(b):
    return (b ^ (b // 2)) % 2


def rotated(rel):
    return lambda own: own ^ rel


def of_half(other, index):
    return lambda b: 2 * (parity(b) ^ other) + index


def share_kernel(order, place_ref, first_ref, side_ref, second_ref, first_out_ref, second_out_ref, semaphores):
    b, size, copies = place_ref[1], order.quarter, []

    def copy(source, target):
        copies.append(pltpu.make_async_copy(source, target, semaphores.at[len(copies)]))
        copies[-1].start()

    rows = pl.ds(pl.multiple_of(b * size, size), size)
    copy(first_ref.at[:, rows, :], first_out_ref.at[pl.ds(0, 9)])
    copy(side_ref.at[rows, :], first_out_ref.at[9])
    for index in range(2):
        rows = pl.ds(pl.multiple_of((2 * parity(b) + index) * size, size), size)
        copy(second_ref.at[:, rows, :], second_out_ref.at[index])
    for started in copies:
        started.wait()


def spread_line(order, share, fsdp):
    return jnp.stack([share] + [exchange(share, "fsdp", fsdp, 2 * rel) for rel in range(1, order.zs)])


def both_cores(bundles, fsdp):
    return bundles + [exchange(value, "fsdp", fsdp, 1) for value in bundles]


def spread_quarters(line, batch):
    return [line] + [exchange(line, "batch", batch, rel) for rel in (1, 2, 3)]


def quarter_labels(order, taps):
    labels = []
    for core in range(2):
        for rel in range(4):
            for step in range(order.zs):
                labels.append((4 * core + rel, step, 0, taps, core, rotated(step), rotated(rel)))
    return labels


def to_plane(halves, batch):
    return jnp.stack([exchange(halves[0], "batch", batch, 1), exchange(halves[1], "batch", batch, 2)])


def half_labels():
    labels = []
    for core in range(2):
        for rel in range(4):
            for index in range(2):
                own, other = of_half(0, index), of_half(1, index)
                labels.append((3 * core, (index, rel), 0, 9, core, rotated(rel), own))
                bundle, at = (1, (index, rel)) if rel < 3 else (2, index)
                labels.append((3 * core + bundle, at, 0, 9, core, rotated(rel), other))
    return labels


def assemble_kernel(weights_ref, ready):
    ready()


def reduce_cores(parts, fsdp):
    keep_p, keep_q, send_p, send_q = parts
    return keep_p + exchange(send_p, "fsdp", fsdp, 1), keep_q + exchange(send_q, "fsdp", fsdp, 1)


def reduce_line(pieces, fsdp):
    total = pieces[0].astype(F32)
    for rel in range(1, len(pieces)):
        total = total + exchange(pieces[rel], "fsdp", fsdp, 2 * rel).astype(F32)
    return total


def first_in_plane(halves, batch):
    half_p, half_q = halves
    n_p, n_q = half_p.shape[0] // 2, half_q.shape[0] // 2
    got_p = exchange(half_p[n_p:], "batch", batch, 1)
    got_q = exchange(half_q[n_q:], "batch", batch, 2)
    return [half_p[:n_p] + got_p, half_q[:n_q] + got_q]


def then_in_plane(halves, batch):
    half_p, half_q = halves
    n_p, n_q = half_p.shape[0] // 2, half_q.shape[0] // 2
    got_p = exchange(half_p[n_p:], "batch", batch, 2)
    got_q = exchange(half_q[n_q:], "batch", batch, 1)
    low, high = half_p[:n_p] + got_p, half_q[:n_q] + got_q
    return [low[index] for index in range(n_p)] + [high[index] for index in range(n_q)]


def halve_line(pieces, fsdp):
    low, high = jnp.stack(pieces[0::2]), jnp.stack(pieces[1::2])
    low = low + exchange(high, "fsdp", fsdp, 2)
    return low[0].astype(F32) + exchange(low[1], "fsdp", fsdp, 4).astype(F32)


def finish_weights(order, place, quarter, batch, outs, doubling=0):
    quarter = quarter.astype(BF16)
    if doubling:
        one = exchange(quarter, "batch", batch, 1)
        two = exchange(jnp.stack([quarter, one]), "batch", batch, 2)
        spread = [quarter, one, two[0], two[1]]
    else:
        spread = [quarter] + [exchange(quarter, "batch", batch, rel) for rel in (1, 2, 3)]
    return call(functools.partial(finish_kernel, order), outs, place, *spread, scalars=1)


def local(
    x_small,
    x_mid,
    x_large,
    cot_small,
    cot_mid,
    cot_large,
    counts,
    w_first,
    gain_first,
    shift_first,
    w_second,
    gain_second,
    shift_second,
    w_short,
    gain_short,
    shift_short,
    *,
    batch,
    fsdp,
):
    fields = (x_small, x_mid, x_large)
    cots = (cot_small, cot_mid, cot_large)
    slots, cin, owned = x_small.shape[0], x_small.shape[3], gain_first.shape[0]
    cout = owned * fsdp
    plan = Plan([cot.shape[1] for cot in cots], slots)
    rows, span = plan.rows, plan.span
    everywhere = steps_of((("fsdp", fsdp), ("batch", batch)))
    me = lax.axis_index("fsdp")
    fast = batch == 4 and fsdp == 8 and owned % (ROWS * batch) == 0
    order = Order(batch, fsdp, owned) if fast else None
    place = jnp.stack([me % 2, lax.axis_index("batch"), me // 2]).astype(jnp.int32)

    own_first = jnp.transpose(w_first, (0, 1, 3, 2)).reshape(9, owned, cin)
    own_second = jnp.transpose(w_second, (0, 1, 3, 2)).reshape(9, owned, cout)
    own_side = jnp.transpose(w_short)
    vectors = [gain_first, shift_first, gain_second, shift_second, gain_short, shift_short]
    patches, cot_rows, mask, vec = call(
        functools.partial(prepare_kernel, plan, owned),
        [shape((rows, 9 * cin), BF16), shape((rows, cout)), shape((rows, 128)), shape((8, cout))],
        place,
        counts,
        *[jnp.transpose(value, (1, 2, 0, 3)) for value in fields + cots],
        *[value.reshape(1, owned) for value in vectors],
        scratch=[pltpu.VMEM((4, plan.margin + rows, cin), F32)],
        scalars=2,
        far=True,
    )
    if fast:
        share_first, share_second = call(
            functools.partial(share_kernel, order),
            [shape((10, order.quarter, cin), BF16), shape((2, 9, order.quarter, cout), BF16)],
            place,
            own_first,
            own_side,
            own_second,
            scratch=[pltpu.SemaphoreType.DMA((4,))],
            scalars=1,
            far=True,
            whole=False,
        )
        line_first = after(spread_line(order, share_first, fsdp), patches, vec)
        plane_first = spread_quarters(line_first, batch)
        kern_first = Gathered(both_cores(plane_first, fsdp), place, order, quarter_labels(order, 10), True)
        share_second = after(share_second, line_first)
        near, far = [exchange(share_second, "fsdp", fsdp, bit) for bit in (2, 4)]
        last = exchange(far, "fsdp", fsdp, 2)
        front = jnp.stack(together(share_second, near, far, *plane_first[1:])[:3], axis=1)
        front_plane = to_plane(front, batch)
    else:
        kern_first = Gathered([lax.all_gather(jnp.concatenate([own_first, own_side[None]]), "fsdp", axis=1, tiled=True)])
        kern_second = Gathered([lax.all_gather(own_second, "fsdp", axis=1, tiled=True)])
    flops = 2 * rows * cout * cin * 9
    *whole, first, side, sums = call(
        first_kernel,
        [shape((rows, cout)), shape((rows, cout)), shape((8, cout))],
        patches,
        mask,
        vec,
        flops=flops,
        weights=kern_first,
    )
    if fast:
        kern_first = Gathered(whole)
        held, whole = [last], []

        def over_last(value):
            value, held[0] = together(value, last)
            held.append(to_plane(held[0], batch))
            return value

        def assemble(value):
            value, *planes = together(value, front_plane, held[1])
            line = jnp.concatenate([front, held[0][:, None]], axis=1)
            bundles = both_cores([line, *planes], fsdp)
            whole.extend(call(assemble_kernel, [], weights=Gathered(bundles, place, order, half_labels())))
            return value

        hooks = {2: over_last, 3: assemble, 4: lambda value: after(value, *whole)}
        sums = sum_over(sums, everywhere, hooks)
        kern_second = Gathered(whole)
        everywhere = everywhere[:1] + everywhere[-2:] + everywhere[1:-2]
    else:
        sums = sum_over(sums, everywhere)
    second, patches_two, sums_two = call(
        functools.partial(second_kernel, plan),
        [shape((rows, cout)), shape((rows, 9 * cout), BF16), shape((8, cout))],
        *sums,
        first,
        mask,
        vec,
        scratch=[pltpu.VMEM((span, cout), F32)],
        flops=2 * flops,
        weights=kern_second,
    )
    sums_two = sum_over(sums_two, everywhere)
    *outputs, dz, sums_z = call(
        functools.partial(output_kernel, plan),
        [shape((length, length, slots, cout), BF16) for length in plan.sides] + [shape((rows, cout)), shape((8, cout))],
        *sums,
        *sums_two,
        second,
        side,
        cot_rows,
        mask,
        flops=50 * rows * cout,
    )
    sums_z = sum_over(sums_z, everywhere)
    grad_two, grad_side, dy, sums_y = call(
        functools.partial(back_second_kernel, plan),
        [shape((rows, cout), BF16), shape((rows, cout), BF16), shape((rows, cout)), shape((8, cout))],
        *sums,
        *sums_two,
        *sums_z,
        first,
        second,
        side,
        dz,
        mask,
        scratch=[pltpu.VMEM((span, cout), F32), pltpu.VMEM((rows, 9 * cout), BF16)],
        flops=2 * flops,
        weights=kern_second,
    )
    hooks = None
    if fast:
        turned = [pltpu.VMEM((cout, rows), BF16), pltpu.VMEM((cout, rows), BF16)]
        parts_two, halves_two = [], []

        def weights_second(value):
            parts_two.extend(
                call(
                    functools.partial(weight_second_kernel, order),
                    [shape((len(part), 9, order.quarter, cout), BF16) for part in order.parts],
                    place,
                    after(grad_two, value) if KN["gate5"] else grad_two,
                    patches_two,
                    scratch=turned,
                    scalars=1,
                    flops=2 * flops,
                )
            )
            halves_two.extend(reduce_cores(parts_two, fsdp))
            return value

        def over_plane(value):
            value, *halves_two[:] = together(value, *halves_two)
            return value

        def over_x(value):
            if KN["pq"] == 1:
                value, halves_two[0] = together(value, halves_two[0], *parts_two)[:2]
            elif KN["pq"] == 2:
                halves_two[0] = after(halves_two[0], value)
                value = after(value, *parts_two)
            else:
                value = after(value, *parts_two)
            return value

        def over_y(value):
            if KN["pq"]:
                value, halves_two[1] = together(value, halves_two[1])
            else:
                value, *halves_two[:] = together(value, *halves_two)
            return value

        hooks = {1: weights_second, KN["dl5"]: over_x, KN["dlh"]: over_y}
    sums_y = sum_over(sums_y, everywhere, hooks)
    def input_part(grad_late):
        return call(
            functools.partial(input_kernel, plan, owned),
            [shape((2 * length, 2 * length, slots, cin), BF16) for length in plan.sides] + [shape((1, owned))] * 6,
            place,
            *sums_z,
            *sums_y,
            grad_late,
            grad_side,
            scratch=[pltpu.VMEM((span, cout), F32), pltpu.VMEM((4, rows, cout), BF16), pltpu.VMEM((rows, cin), F32)],
            scalars=1,
            flops=flops,
            weights=kern_first,
        )
    if fast:
        grad_one, *parts_one = call(
            functools.partial(weight_first_kernel, order),
            [shape((rows, cout), BF16)] + [shape((len(part), 10, order.quarter, cin), BF16) for part in order.parts],
            place,
            *sums,
            *sums_y,
            first,
            dy,
            mask,
            grad_side,
            patches,
            scratch=turned,
            scalars=1,
            flops=flops,
        )
        halves_two = first_in_plane(halves_two, batch)
        halves_one = reduce_cores(parts_one, fsdp)
        if KN["k7"] == 0:
            grad_late = after(grad_one, *halves_one)
        elif KN["k7"] == 1:
            grad_late = after(grad_one, *parts_one)
        if KN["gx1"]:
            *halves_one, last = together(*halves_one, halves_two[0])
            halves_two[0] = last
        if KN["gx2"] == 1:
            halves_two[:] = together(*halves_two, *halves_one)[:2]
        halves_one = first_in_plane(halves_one, batch)
        if KN["gx2"] == 2:
            halves_two[:] = together(*halves_two, *halves_one)[:2]
        if KN["k7"] == 2:
            grad_late = after(grad_one, *halves_one)
        reduce_two = halve_line if KN["z2"] else reduce_line
        reduce_one = halve_line if KN["z1"] else reduce_line
        quarter_two = reduce_two(then_in_plane(halves_two, batch), fsdp)
        early_grads = input_part(grad_late)
        if KN["k7d"] == 1:
            halves_one = together(*halves_one, early_grads[3])[:2]
        pieces_one = then_in_plane(halves_one, batch)
        if KN["k7d"] == 2:
            pieces_one = together(*pieces_one, early_grads[3])[:-1]
        quarter_one = reduce_one(pieces_one, fsdp)
        if KN["k7d"] == 3:
            quarter_one = after(quarter_one, early_grads[3])
        dw_second = finish_weights(order, place, quarter_two, batch, [shape((9, owned, cout))], KN["ag2"])[0]
        dw_first, dw_side = finish_weights(
            order, place, quarter_one, batch, [shape((9, owned, cin)), shape((owned, cin))], KN["ag1"]
        )
    else:
        grad_one = call(back_first, shape((rows, cout), BF16), *sums, *sums_y, first, dy, mask)
        taps = tuple(range(9))
        whole = [
            call(functools.partial(plain_weight_kernel, taps), shape((9, cout, cout), BF16), grad_two, patches_two),
            call(functools.partial(plain_weight_kernel, taps), shape((9, cout, cin), BF16), grad_one, patches),
            call(functools.partial(plain_weight_kernel, (4,)), shape((1, cout, cin), BF16), grad_side, patches),
        ]
        dw_second, dw_first, dw_side = [
            lax.psum(lax.psum_scatter(value, "fsdp", scatter_dimension=1, tiled=True), "batch").astype(F32)
            for value in whole
        ]
        dw_side = dw_side[0]
        grad_late = grad_one
    *input_grads, shift_1, gain_1, gain_2, shift_2, gain_3, shift_3 = early_grads if fast else input_part(grad_late)

    def as_weight(value):
        return jnp.transpose(value.reshape(3, 3, owned, value.shape[2]), (0, 1, 3, 2))

    return (
        *[jnp.transpose(value, (2, 0, 1, 3)) for value in (*outputs, *input_grads)],
        as_weight(dw_first),
        gain_1[0],
        shift_1[0],
        as_weight(dw_second),
        gain_2[0],
        shift_2[0],
        jnp.transpose(dw_side),
        gain_3[0],
        shift_3[0],
    )


def solution(mesh):
    split = ("batch", "fsdp")
    image = P(split, None, None, None)
    kernel = P(None, None, None, "fsdp")
    vector = P("fsdp")
    in_specs = (image,) * 6 + (
        P(split, None),
        kernel,
        vector,
        vector,
        kernel,
        vector,
        vector,
        P(None, "fsdp"),
        vector,
        vector,
    )
    out_specs = (image,) * 6 + (
        kernel,
        vector,
        vector,
        kernel,
        vector,
        vector,
        P(None, "fsdp"),
        vector,
        vector,
    )
    body = functools.partial(local, batch=mesh.shape["batch"], fsdp=mesh.shape["fsdp"])
    return jax.shard_map(body, mesh=mesh, in_specs=in_specs, out_specs=out_specs, check_vma=False)
```

```python
import functools

import jax
import jax.numpy as jnp
import numpy as np
from jax import lax
from jax.experimental import pallas as pl
from jax.experimental.pallas import tpu as pltpu
from jax.sharding import PartitionSpec as P

EPSILON = 1e-05
F32 = jnp.float32
BF16 = jnp.bfloat16
ROWS = 16
VMEM_LIMIT = 30 * 2**20


def up(value, step):
    return -(-value // step) * step


class Plan:
    def __init__(self, sides, slots):
        self.sides, self.slots = sides, slots
        self.starts, self.sizes, row = [], [], 0
        for index, side in enumerate(sides):
            width = side + 1
            after = sides[index + 1] + 1 if index + 1 < len(sides) else 0
            size = up(slots * (width * width + max(0, width + 1 - after)), ROWS)
            self.starts.append(row)
            self.sizes.append(size)
            row += size
        self.rows = row
        self.margin = up(slots * (max(sides) + 2), ROWS)
        self.span = self.rows + 2 * self.margin

    def segments(self):
        return list(zip(self.starts, self.sizes, [side + 1 for side in self.sides]))


    def cells(self):
        for group, (start, side) in enumerate(zip(self.starts, self.sides)):
            for down in range(side):
                for right in range(side):
                    yield group, down, right, start + self.slots * ((down + 1) * (side + 1) + right + 1)


def nn(left, right):
    return lax.dot_general(left, right, (((1,), (0,)), ((), ())), preferred_element_type=F32)


def nt(left, right):
    return lax.dot_general(left, right, (((1,), (1,)), ((), ())), preferred_element_type=F32)


def column(value):
    return jnp.sum(value, axis=0, keepdims=True)


def wide(mask_ref, channels):
    return jnp.concatenate([mask_ref[...]] * (channels // mask_ref.shape[1]), axis=1)


def silu_slope(value):
    gate = jax.nn.sigmoid(value)
    return gate * (1.0 + value * (1.0 - gate))


def norm(value, sums, row, total):
    center = sums[row : row + 1] / total
    spread = sums[row + 1 : row + 2] / total - center * center
    factor = lax.rsqrt(spread + EPSILON)
    return (value - center) * factor, factor


def put_rows(ref, rows):
    for index, row in enumerate(rows):
        ref[index : index + 1, :] = row
    ref[len(rows) :, :] = jnp.zeros((ref.shape[0] - len(rows), ref.shape[1]), F32)


def offsets(plan, width):
    return [plan.slots * (dy * width + dx) for dy in (-1, 0, 1) for dx in (-1, 0, 1)]


def unfold(plan, padded_ref, out_ref, sign):
    channels = padded_ref.shape[1]
    for start, size, width in plan.segments():
        for tap, offset in enumerate(offsets(plan, width)):
            first = plan.margin + start + sign * offset
            out_ref[start : start + size, tap * channels : (tap + 1) * channels] = padded_ref[
                first : first + size, :
            ].astype(BF16)


def fill(plan, padded_ref, value):
    edge = jnp.zeros((plan.margin, padded_ref.shape[1]), F32)
    padded_ref[: plan.margin, :] = edge
    padded_ref[plan.margin : plan.margin + plan.rows, :] = value
    padded_ref[plan.margin + plan.rows :, :] = edge


def prepare_kernel(plan, owned, place_ref, counts_ref, *refs):
    fields, cots, vectors = refs[:3], refs[3:6], refs[6:12]
    patches_ref, cot_ref, mask_ref, vec_ref, held_ref = refs[12:]
    slots, channels = plan.slots, fields[0].shape[3]
    held_ref[...] = jnp.zeros(held_ref.shape, F32)
    cot_ref[...] = jnp.zeros(cot_ref.shape, F32)
    mask_ref[...] = jnp.zeros(mask_ref.shape, F32)
    cout = vec_ref.shape[1]
    first = (place_ref[2] * 2 + place_ref[0]) * owned
    spot = lax.broadcasted_iota(jnp.int32, (owned, cout), 1) - lax.broadcasted_iota(jnp.int32, (owned, cout), 0)
    own = ((spot == first) & (place_ref[1] == 0)).astype(BF16)
    held = [ref[...].astype(F32) for ref in vectors] + [jnp.zeros((vec_ref.shape[0] - 6, owned), F32)]
    vec_ref[...] = nn(jnp.concatenate(held, axis=0).astype(BF16), own)
    slot = lax.broadcasted_iota(jnp.int32, (slots, mask_ref.shape[1]), 0)
    live = [(slot < counts_ref[0, group]).astype(F32) for group in range(3)]
    for group, down, right, row in plan.cells():
        mask_ref[row : row + slots, :] = live[group]
        cot_ref[row : row + slots, :] = cots[group][down, right].astype(F32)
        for py in range(2):
            for px in range(2):
                first = plan.margin + row
                held_ref[2 * py + px, first : first + slots, :] = fields[group][2 * down + py, 2 * right + px].astype(F32)
    for start, size, width in plan.segments():
        for ky in range(3):
            for kx in range(3):
                tap = ky * 3 + kx
                shift = plan.slots * (width * (ky == 0) + (kx == 0))
                first = plan.margin + start - shift
                patches_ref[start : start + size, tap * channels : (tap + 1) * channels] = held_ref[
                    2 * (ky != 1) + (kx != 1), first : first + size, :
                ].astype(BF16)


def first_kernel(patches_ref, mask_ref, vec_ref, weights_ref, ready, first_ref, side_ref, sums_ref):
    ready()
    cin = weights_ref.shape[2]
    cout = weights_ref.shape[1]
    total = nt(patches_ref[:, :cin], weights_ref[0])
    for tap in range(1, 9):
        total += nt(patches_ref[:, tap * cin : (tap + 1) * cin], weights_ref[tap])
    side = nt(patches_ref[:, 4 * cin : 5 * cin], weights_ref[9])
    first_ref[...] = total
    side_ref[...] = side
    mask = wide(mask_ref, cout)
    put_rows(
        sums_ref,
        [
            column(mask * total),
            column(mask * total * total),
            column(mask * side),
            column(mask * side * side),
            column(mask),
            vec_ref[0:1],
            vec_ref[1:2],
        ],
    )


def second_kernel(
    plan, sums_ref, got_ref, first_ref, mask_ref, vec_ref, weights_ref, ready, second_ref, patches_ref, out_ref, held_ref
):
    cout = first_ref.shape[1]
    mask = wide(mask_ref, cout)
    sums = sums_ref[...] + got_ref[...]
    normed, _ = norm(first_ref[...], sums, 0, sums[4:5])
    pre = normed * sums[5:6] + sums[6:7]
    fill(plan, held_ref, jax.nn.silu(pre) * mask)
    unfold(plan, held_ref, patches_ref, 1)
    ready()
    total = nt(patches_ref[:, :cout], weights_ref[0])
    for tap in range(1, 9):
        total += nt(patches_ref[:, tap * cout : (tap + 1) * cout], weights_ref[tap])
    second_ref[...] = total
    put_rows(
        out_ref, [column(mask * total), column(mask * total * total)] + [vec_ref[row : row + 1] for row in range(2, 6)]
    )


def output_kernel(
    plan, sums_ref, got_ref, sums_two_ref, got_two_ref, second_ref, side_ref, cot_ref, mask_ref, *refs
):
    outs, (dz_ref, sums_out_ref) = refs[:3], refs[3:]
    cout = second_ref.shape[1]
    mask = wide(mask_ref, cout)
    sums, sums_two = sums_ref[...] + got_ref[...], sums_two_ref[...] + got_two_ref[...]
    total = sums[4:5]
    normed_two, _ = norm(second_ref[...], sums_two, 0, total)
    normed_side, _ = norm(side_ref[...], sums, 2, total)
    value = (normed_two * sums_two[2:3] + sums_two[3:4]) + (normed_side * sums_two[4:5] + sums_two[5:6])
    gate = jax.nn.sigmoid(value)
    out = (value * gate * mask).astype(BF16)
    for group, down, right, row in plan.cells():
        outs[group][down, right] = out[row : row + plan.slots, :]
    grad = cot_ref[...] * mask * (gate * (1.0 + value * (1.0 - gate)))
    dz_ref[...] = grad
    total = column(grad)
    put_rows(sums_out_ref, [total, column(grad * normed_two), column(grad * normed_side), total])


def back_second_kernel(
    plan, sums_ref, got_ref, sums_two_ref, got_two_ref, sums_z_ref, got_z_ref,
    first_ref, second_ref, side_ref, dz_ref, mask_ref, weights_ref, ready,
    grad_two_ref, grad_side_ref, dy_ref, out_ref, held_ref, patches_ref,
):
    cout = first_ref.shape[1]
    mask = wide(mask_ref, cout)
    sums, sums_two = sums_ref[...] + got_ref[...], sums_two_ref[...] + got_two_ref[...]
    sums_z = sums_z_ref[...] + got_z_ref[...]
    total = sums[4:5]
    grad = dz_ref[...]
    normed, factor = norm(second_ref[...], sums_two, 0, total)
    two = sums_two[2:3] * factor * (grad - mask * (sums_z[0:1] + normed * sums_z[1:2]) / total)
    normed, factor = norm(side_ref[...], sums, 2, total)
    side = sums_two[4:5] * factor * (grad - mask * (sums_z[0:1] + normed * sums_z[2:3]) / total)
    grad_side_ref[...] = side.astype(BF16)
    grad_two_ref[...] = two.astype(BF16)
    fill(plan, held_ref, two)
    unfold(plan, held_ref, patches_ref, -1)
    ready()
    back = nn(patches_ref[:, :cout], weights_ref[0])
    for tap in range(1, 9):
        back += nn(patches_ref[:, tap * cout : (tap + 1) * cout], weights_ref[tap])
    normed, _ = norm(first_ref[...], sums, 0, total)
    pre = normed * sums[5:6] + sums[6:7]
    grad = back * silu_slope(pre) * mask
    dy_ref[...] = grad
    put_rows(out_ref, [column(grad), column(grad * normed)])


def back_first(sums_ref, got_ref, sums_y_ref, got_y_ref, first_ref, dy_ref, mask_ref, grad_ref):
    cout = first_ref.shape[1]
    mask = wide(mask_ref, cout)
    sums, sums_y = sums_ref[...] + got_ref[...], sums_y_ref[...] + got_y_ref[...]
    total = sums[4:5]
    normed, factor = norm(first_ref[...], sums, 0, total)
    grad = sums[5:6] * factor * (dy_ref[...] - mask * (sums_y[0:1] + normed * sums_y[1:2]) / total)
    grad_ref[...] = grad.astype(BF16)


class Order:
    def __init__(self, batch, fsdp, owned):
        self.zs, self.quarter, self.owned = fsdp // 2, owned // batch, owned
        half = self.zs // 2
        self.blocks = [(b, z) for b in (0, 2, 1, 3) for z in range(half)]
        self.blocks += [(b, z) for b in (0, 1, 2, 3) for z in range(half, self.zs)]

    def share(self, place_ref, grad_refs, keep_ref, send_ref, turned_ref):
        core, b, z = place_ref[0], place_ref[1], place_ref[2]
        for index, grad_ref in enumerate(grad_refs):
            turned_ref[...] = grad_ref[...].T
            for rel_core, out_ref in enumerate((keep_ref, send_ref)):
                for block, (rel_b, rel_z) in enumerate(self.blocks):
                    row = ((z ^ rel_z) * 2 + (core ^ rel_core)) * self.owned + (b ^ rel_b) * self.quarter
                    rows = pl.ds(pl.multiple_of(row, self.quarter), self.quarter)
                    first = (index * len(self.blocks) + block) * self.quarter
                    out_ref[first : first + self.quarter, :] = turned_ref[rows, :]

    def correlate(self, grads, patch_refs, first, size, tap, out_refs):
        value = sum(nn(grad, ref[:, first : first + size]) for grad, ref in zip(grads, patch_refs)).astype(BF16)
        begin = 0
        for out_ref in out_refs:
            count = out_ref.shape[0]
            out_ref[:, tap] = value[begin : begin + count * self.quarter].reshape(count, self.quarter, size)
            begin += count * self.quarter


def back_second_share_kernel(plan, order, place_ref, *refs):
    inputs, (grad_side_ref, dy_ref, out_ref, keep_ref, send_ref) = refs[:13], refs[13:18]
    held_ref, patches_ref, turned_ref, grad_two_ref = refs[18:]
    back_second_kernel(plan, *inputs, grad_two_ref, grad_side_ref, dy_ref, out_ref, held_ref, patches_ref)
    order.share(place_ref, [grad_two_ref], keep_ref, send_ref, turned_ref)


def share_kernel_of(order, place_ref, grad_ref, keep_ref, send_ref, turned_ref):
    order.share(place_ref, [grad_ref], keep_ref, send_ref, turned_ref)


def back_first_share_kernel(order, place_ref, *refs):
    back_first(*refs[:8])
    order.share(place_ref, refs[7:8], refs[8], refs[9], refs[10])


def weight_second_kernel(order, part, keep_ref, got_ref, patches_ref, other_ref, out_ref):
    cout = patches_ref.shape[1] // 9
    grads = [ref[part * cout // 4 : (part + 1) * cout // 4] for ref in (keep_ref, got_ref)]
    for tap in range(9):
        order.correlate(grads, (patches_ref, other_ref), tap * cout, cout, tap, [out_ref])


def weight_first_kernel(order, keep_ref, got_ref, side_keep_ref, side_got_ref, patches_ref, other_ref, *outs):
    cin = patches_ref.shape[1] // 9
    grads = [keep_ref[...], got_ref[...]]
    for tap in range(9):
        order.correlate(grads, (patches_ref, other_ref), tap * cin, cin, tap, outs)
    grads = [side_keep_ref[...], side_got_ref[...]]
    order.correlate(grads, (patches_ref, other_ref), 4 * cin, cin, 9, outs)


def plain_weight_kernel(taps, grad_ref, patches_ref, out_ref):
    turned = grad_ref[...].T
    channels = out_ref.shape[2]
    for index, tap in enumerate(taps):
        out_ref[index] = nn(turned, patches_ref[:, tap * channels : (tap + 1) * channels]).astype(BF16)


def input_kernel(
    plan, owned, place_ref, sums_z_ref, got_z_ref, sums_y_ref, got_y_ref, grad_ref, side_ref, weights_ref, ready, *refs
):
    outs, owns, (held_ref, moved_ref, total_ref) = refs[:3], refs[3:9], refs[9:]
    ready()
    sums = jnp.concatenate([sums_z_ref[...] + got_z_ref[...], sums_y_ref[...] + got_y_ref[...]], axis=0)
    first = (place_ref[2] * 2 + place_ref[0]) * owned
    spot = lax.broadcasted_iota(jnp.int32, sums.shape, 1)
    sums = jnp.where((spot >= first) & (spot < first + owned), sums, 0.0)
    sums = sum(sums[:, begin : begin + owned] for begin in range(0, sums.shape[1], owned))
    for row, ref in zip((8, 9, 1, 0, 2, 3), owns):
        ref[...] = sums[row : row + 1]
    rows = plan.rows
    fill(plan, held_ref, grad_ref[...].astype(F32))
    for index, (down, right) in enumerate(((0, 0), (0, 1), (1, 0), (1, 1))):
        for start, size, width in plan.segments():
            first = plan.margin + start + plan.slots * (down * width + right)
            moved_ref[index, start : start + size, :] = held_ref[first : first + size, :].astype(BF16)
    for py in range(2):
        for px in range(2):
            total = None
            for ky in (0, 2) if py else (1,):
                for kx in (0, 2) if px else (1,):
                    index = 2 * (ky == 0) + (kx == 0)
                    term = nn(moved_ref[index], weights_ref[ky * 3 + kx])
                    total = term if total is None else total + term
            if py + px == 0:
                total += nn(side_ref[...], weights_ref[9])
            total_ref[...] = total
            for group, down, right, row in plan.cells():
                outs[group][2 * down + py, 2 * right + px] = total_ref[row : row + plan.slots, :].astype(BF16)


def finish_kernel(order, place_ref, *refs):
    parts, outs = refs[:4], refs[4:]
    b, quarter = place_ref[1], order.quarter
    taps = outs[0].shape[0]
    for rel, ref in enumerate(parts):
        rows = pl.ds(pl.multiple_of((b ^ rel) * quarter, quarter), quarter)
        outs[0][:, rows, :] = ref[:taps].astype(F32)
        if len(outs) > 1:
            outs[1][rows, :] = ref[taps].astype(F32)


class Gathered:
    def __init__(self, arrays, place=None, order=None, labels=()):
        self.arrays, self.place, self.order, self.labels = arrays, place, order, labels
        self.taps = max((label[2] + label[3] for label in labels), default=0)

    def dims(self):
        if self.order is None:
            return self.arrays[0].shape
        return self.taps, 2 * self.order.zs * self.order.owned, self.arrays[0].shape[-1]

    def wrap(self, body, scalars, count):
        if self.order is None:
            return lambda *refs: body(*refs[: count + 1], lambda: None, *refs[count + 1 :])
        order, many, labels = self.order, len(self.arrays), self.labels

        def whole(place_ref, *refs):
            inputs, bundles, rest = refs[:count], refs[count : count + many], refs[count + many :]
            weights_ref, outs, semaphores = rest[0], rest[1:-1], rest[-1]
            core, b, z = place_ref[0], place_ref[1], place_ref[2]
            copies = []
            for index, at, tap, taps, rel_core, owner, quarter in labels:
                row = (owner(z) * 2 + (core ^ rel_core)) * order.owned + quarter(b) * order.quarter
                rows = pl.ds(pl.multiple_of(row, order.quarter), order.quarter)
                target = weights_ref.at[pl.ds(tap, taps), rows, :]
                copies.append(pltpu.make_async_copy(bundles[index].at[at], target, semaphores.at[len(copies)]))
            for copy in copies:
                copy.start()

            def ready():
                for copy in copies:
                    copy.wait()

            body(*inputs, weights_ref, ready, *outs)

        return whole


def call(body, out_shapes, *args, scratch=(), scalars=0, weights=None, far=False, whole=True):
    vmem = pl.BlockSpec(memory_space=pltpu.VMEM)
    inner = vmem if whole else pl.BlockSpec(memory_space=pltpu.MemorySpace.HBM)
    if far:
        args = args[:scalars] + tuple(
            pltpu.with_memory_space_constraint(arg, pltpu.MemorySpace.HBM) for arg in args[scalars:]
        )
    specs = [pl.BlockSpec(memory_space=pltpu.SMEM)] * scalars + [inner] * (len(args) - scalars)
    if weights is not None:
        body = weights.wrap(body, scalars, len(args))
        scratch = list(scratch)
        if weights.order is None:
            args = args + tuple(weights.arrays)
            specs = specs + [vmem]
        else:
            args = (weights.place,) + args + tuple(weights.arrays)
            specs = [pl.BlockSpec(memory_space=pltpu.SMEM)] + specs + [pl.BlockSpec(memory_space=pl.ANY)] * len(weights.arrays)
            out_shapes = [shape(weights.dims(), BF16)] + list(out_shapes)
            scratch += [pltpu.SemaphoreType.DMA((len(weights.labels),))]
    many = isinstance(out_shapes, (list, tuple))
    return pl.pallas_call(
        body,
        in_specs=specs,
        out_specs=[vmem] * len(out_shapes) if many else vmem,
        out_shape=list(out_shapes) if many else out_shapes,
        scratch_shapes=list(scratch),
        compiler_params=pltpu.CompilerParams(vmem_limit_bytes=VMEM_LIMIT),
        cost_estimate=pl.CostEstimate(flops=0, bytes_accessed=0, transcendentals=0),
    )(*args)


def shape(dims, dtype=F32):
    return jax.ShapeDtypeStruct(tuple(dims), dtype)


def exchange(value, axis, count, bit):
    return lax.ppermute(value, axis, [(index, index ^ bit) for index in range(count)])


def bits(count):
    return [1 << index for index in range(count.bit_length() - 1)]


def after(value, *others):
    return lax.optimization_barrier((value, *others))[0]


def together(*values):
    return list(lax.optimization_barrier(values))


def steps_of(axes):
    return [(axis, count, bit) for axis, count in axes for bit in bits(count)]


def sum_over(value, steps, hooks=None):
    got = jnp.zeros_like(value)
    for index, (axis, count, bit) in enumerate(steps):
        if index:
            value = value + got
        if hooks and index in hooks:
            value = hooks[index](value)
        got = exchange(value, axis, count, bit)
    return value, got


def parity(b):
    return (b ^ (b // 2)) % 2


def rotated(rel):
    return lambda own: own ^ rel


def of_half(other, index):
    return lambda b: 2 * (parity(b) ^ other) + index


def share_kernel(order, place_ref, first_ref, side_ref, second_ref, first_out_ref, second_out_ref, semaphores):
    b, size, copies = place_ref[1], order.quarter, []

    def copy(source, target):
        copies.append(pltpu.make_async_copy(source, target, semaphores.at[len(copies)]))
        copies[-1].start()

    rows = pl.ds(pl.multiple_of(b * size, size), size)
    copy(first_ref.at[:, rows, :], first_out_ref.at[pl.ds(0, 9)])
    copy(side_ref.at[rows, :], first_out_ref.at[9])
    for index in range(2):
        rows = pl.ds(pl.multiple_of((2 * parity(b) + index) * size, size), size)
        copy(second_ref.at[:, rows, :], second_out_ref.at[index])
    for started in copies:
        started.wait()


def spread_line(order, share, fsdp):
    return jnp.stack([share] + [exchange(share, "fsdp", fsdp, 2 * rel) for rel in range(1, order.zs)])


def both_cores(bundles, fsdp):
    return bundles + [exchange(value, "fsdp", fsdp, 1) for value in bundles]


def spread_quarters(line, batch):
    return [line] + [exchange(line, "batch", batch, rel) for rel in (1, 2, 3)]


def quarter_labels(order, taps):
    labels = []
    for core in range(2):
        for rel in range(4):
            for step in range(order.zs):
                labels.append((4 * core + rel, step, 0, taps, core, rotated(step), rotated(rel)))
    return labels


def to_plane(halves, batch):
    return [exchange(halves[0], "batch", batch, 1), exchange(halves[1], "batch", batch, 2)]


def half_labels():
    labels = []
    for core in range(2):
        for rel in range(4):
            for index in range(2):
                own, other = of_half(0, index), of_half(1, index)
                labels.append((3 * core, (index, rel), 0, 9, core, rotated(rel), own))
                bundle, at = (1, (index, rel)) if rel < 3 else (2, index)
                labels.append((3 * core + bundle, at, 0, 9, core, rotated(rel), other))
    return labels


def assemble_kernel(weights_ref, ready):
    ready()


def reduce_line(pieces, fsdp):
    total = pieces[0].astype(F32)
    for rel in range(1, len(pieces)):
        total = total + exchange(pieces[rel], "fsdp", fsdp, 2 * rel).astype(F32)
    return total


def first_in_plane(halves, batch):
    half_p, half_q = halves
    n_p, n_q = half_p.shape[0] // 2, half_q.shape[0] // 2
    got_p = exchange(half_p[n_p:], "batch", batch, 1)
    got_q = exchange(half_q[n_q:], "batch", batch, 2)
    return [half_p[:n_p] + got_p, half_q[:n_q] + got_q]


def then_in_plane(halves, batch):
    half_p, half_q = halves
    n_p, n_q = half_p.shape[0] // 2, half_q.shape[0] // 2
    got_p = exchange(half_p[n_p:], "batch", batch, 2)
    got_q = exchange(half_q[n_q:], "batch", batch, 1)
    low, high = half_p[:n_p] + got_p, half_q[:n_q] + got_q
    return [low[index] for index in range(n_p)] + [high[index] for index in range(n_q)]


def finish_weights(order, place, quarter, batch, outs):
    quarter = quarter.astype(BF16)
    spread = [quarter] + [exchange(quarter, "batch", batch, rel) for rel in (1, 2, 3)]
    return call(functools.partial(finish_kernel, order), outs, place, *spread, scalars=1)


def local(
    x_small,
    x_mid,
    x_large,
    cot_small,
    cot_mid,
    cot_large,
    counts,
    w_first,
    gain_first,
    shift_first,
    w_second,
    gain_second,
    shift_second,
    w_short,
    gain_short,
    shift_short,
    *,
    batch,
    fsdp,
):
    fields = (x_small, x_mid, x_large)
    cots = (cot_small, cot_mid, cot_large)
    slots, cin, owned = x_small.shape[0], x_small.shape[3], gain_first.shape[0]
    cout = owned * fsdp
    plan = Plan([cot.shape[1] for cot in cots], slots)
    rows, span = plan.rows, plan.span
    everywhere = steps_of((("fsdp", fsdp), ("batch", batch)))
    me = lax.axis_index("fsdp")
    fast = batch == 4 and fsdp == 8 and owned % (ROWS * batch) == 0
    order = Order(batch, fsdp, owned) if fast else None
    place = jnp.stack([me % 2, lax.axis_index("batch"), me // 2]).astype(jnp.int32)

    own_first = jnp.transpose(w_first, (0, 1, 3, 2)).reshape(9, owned, cin)
    own_second = jnp.transpose(w_second, (0, 1, 3, 2)).reshape(9, owned, cout)
    own_side = jnp.transpose(w_short)
    vectors = [gain_first, shift_first, gain_second, shift_second, gain_short, shift_short]
    patches, cot_rows, mask, vec = call(
        functools.partial(prepare_kernel, plan, owned),
        [shape((rows, 9 * cin), BF16), shape((rows, cout)), shape((rows, 128)), shape((8, cout))],
        place,
        counts,
        *[jnp.transpose(value, (1, 2, 0, 3)) for value in fields + cots],
        *[value.reshape(1, owned) for value in vectors],
        scratch=[pltpu.VMEM((4, plan.margin + rows, cin), F32)],
        scalars=2,
        far=True,
    )
    if fast:
        share_first, share_second = call(
            functools.partial(share_kernel, order),
            [shape((10, order.quarter, cin), BF16), shape((2, 9, order.quarter, cout), BF16)],
            place,
            own_first,
            own_side,
            own_second,
            scratch=[pltpu.SemaphoreType.DMA((4,))],
            scalars=1,
            far=True,
            whole=False,
        )
        line_first = after(spread_line(order, share_first, fsdp), patches, vec)
        plane_first = spread_quarters(line_first, batch)
        kern_first = Gathered(both_cores(plane_first, fsdp), place, order, quarter_labels(order, 10))
        share_second = after(share_second, line_first)
        near, far = [exchange(share_second, "fsdp", fsdp, bit) for bit in (2, 4)]
        last = exchange(far, "fsdp", fsdp, 2)
        front = jnp.stack(together(share_second, near, far, *plane_first[1:])[:3], axis=1)
        front_plane = to_plane(front, batch)
    else:
        kern_first = Gathered([lax.all_gather(jnp.concatenate([own_first, own_side[None]]), "fsdp", axis=1, tiled=True)])
        kern_second = Gathered([lax.all_gather(own_second, "fsdp", axis=1, tiled=True)])
    if fast:
        kern_first = Gathered(call(assemble_kernel, [], weights=kern_first))
    first, side, sums = call(
        first_kernel,
        [shape((rows, cout)), shape((rows, cout)), shape((8, cout))],
        patches,
        mask,
        vec,
        weights=kern_first,
    )
    if fast:
        held, whole = [last], []

        def over_last(value):
            value, held[0] = together(value, last)
            held.append(to_plane(held[0], batch))
            return value

        def assemble(value):
            value, piece, *planes = together(value, held[0], *front_plane, *held[1])
            line = jnp.concatenate([front, piece[:, None]], axis=1)
            bundles = both_cores([line, jnp.stack(planes[:2]), jnp.stack(planes[2:])], fsdp)
            whole.extend(call(assemble_kernel, [], weights=Gathered(bundles, place, order, half_labels())))
            return value

        hooks = {2: over_last, 3: assemble}
        sums = sum_over(sums, everywhere, hooks)
        kern_second = Gathered(whole)
        everywhere = everywhere[:1] + everywhere[-2:] + everywhere[1:-2]
    else:
        sums = sum_over(sums, everywhere)
    second, patches_two, sums_two = call(
        functools.partial(second_kernel, plan),
        [shape((rows, cout)), shape((rows, 9 * cout), BF16), shape((8, cout))],
        *sums,
        first,
        mask,
        vec,
        scratch=[pltpu.VMEM((span, cout), F32)],
        weights=kern_second,
    )
    def to_other_core(array, into):
        def begin(value):
            into.append(exchange(after(array, value), "fsdp", fsdp, 1))
            return value

        def end(value):
            value, into[0] = together(value, into[0])
            return value

        return {1: begin, 4: end} if fast else None

    other_two, other_one = [], []
    sums_two = sum_over(sums_two, everywhere, to_other_core(patches_two, other_two))
    *outputs, dz, sums_z = call(
        functools.partial(output_kernel, plan),
        [shape((length, length, slots, cout), BF16) for length in plan.sides] + [shape((rows, cout)), shape((8, cout))],
        *sums,
        *sums_two,
        second,
        side,
        cot_rows,
        mask,
    )
    sums_z = sum_over(sums_z, everywhere, to_other_core(patches, other_one))
    shared = []
    if fast:
        turned = pltpu.VMEM((cout, rows), BF16)
        shared = [shape((cout // 2, rows), BF16)] * 2
    results = call(
        functools.partial(back_second_share_kernel, plan, order) if fast else functools.partial(back_second_kernel, plan),
        ([] if fast else [shape((rows, cout), BF16)])
        + [shape((rows, cout), BF16), shape((rows, cout)), shape((8, cout))]
        + shared,
        *([place] if fast else []),
        *sums,
        *sums_two,
        *sums_z,
        first,
        second,
        side,
        dz,
        mask,
        scratch=[pltpu.VMEM((span, cout), F32), pltpu.VMEM((rows, 9 * cout), BF16)] + ([turned, pltpu.VMEM((rows, cout), BF16)] if fast else []),
        scalars=int(fast),
        weights=kern_second,
    )
    hooks = None
    if fast:
        grad_side, dy, sums_y, keep, send = results
        got, halves_two, sides = [], [], []

        def begin_second(value):
            got.append(exchange(after(send, value), "fsdp", fsdp, 1))
            return value

        def weights_second(value, part):
            half = (len(order.blocks) // 2, 9, order.quarter, cout)
            halves_two.append(
                call(
                    functools.partial(weight_second_kernel, order, part),
                    shape(half, BF16),
                    after(keep, value),
                    got[0],
                    patches_two,
                    other_two[0],
                )
            )
            return value

        def over_x(value):
            value, halves_two[0] = together(value, halves_two[0])
            return value

        def over_y(value):
            value, halves_two[1] = together(value, halves_two[1])
            return value

        def begin(value):
            return weights_second(begin_second(value), 0)

        def between(value):
            return weights_second(over_x(value), 1)

        def share_side(value):
            value = over_y(value)
            shares = call(
                functools.partial(share_kernel_of, order),
                [shape((cout // 2, rows), BF16)] * 2,
                place,
                after(grad_side, value),
                scratch=[turned],
                scalars=1,
            )
            sides.extend([shares[0], exchange(shares[1], "fsdp", fsdp, 1)])
            return value

        hooks = {1: begin, 2: between, 3: share_side, 4: lambda value: after(value, *sides)}
    else:
        grad_two, grad_side, dy, sums_y = results
    sums_y = sum_over(sums_y, everywhere, hooks)
    def input_part(grad_late):
        return call(
            functools.partial(input_kernel, plan, owned),
            [shape((2 * length, 2 * length, slots, cin), BF16) for length in plan.sides] + [shape((1, owned))] * 6,
            place,
            *sums_z,
            *sums_y,
            grad_late,
            grad_side,
            scratch=[pltpu.VMEM((span, cout), F32), pltpu.VMEM((4, rows, cout), BF16), pltpu.VMEM((rows, cin), F32)],
            scalars=1,
            weights=kern_first,
        )
    if fast:
        grad_one, keep_one, send_one = call(
            functools.partial(back_first_share_kernel, order),
            [shape((rows, cout), BF16)] + [shape((cout // 2, rows), BF16)] * 2,
            place,
            *sums,
            *sums_y,
            first,
            dy,
            mask,
            scratch=[turned],
            scalars=1,
        )
        halves_two = first_in_plane(halves_two, batch)
        got_one = exchange(send_one, "fsdp", fsdp, 1)
        keep_one, halves_two[0] = together(keep_one, halves_two[0])
        half = (len(order.blocks) // 2, 10, order.quarter, cin)
        halves_one = call(
            functools.partial(weight_first_kernel, order),
            [shape(half, BF16)] * 2,
            keep_one,
            got_one,
            *sides,
            patches,
            other_one[0],
        )
        *halves_one, halves_two[1] = together(*halves_one, halves_two[1])
        halves_one = first_in_plane(halves_one, batch)
        early_grads = input_part(after(grad_one, *halves_one))
        quarter_two = reduce_line(then_in_plane(halves_two, batch), fsdp)
        pieces_one = together(*then_in_plane(halves_one, batch), early_grads[3])[:-1]
        quarter_one = reduce_line(pieces_one, fsdp)
        dw_second = finish_weights(order, place, quarter_two, batch, [shape((9, owned, cout))])[0]
        dw_first, dw_side = finish_weights(
            order, place, quarter_one, batch, [shape((9, owned, cin)), shape((owned, cin))]
        )
    else:
        grad_one = call(back_first, shape((rows, cout), BF16), *sums, *sums_y, first, dy, mask)
        taps = tuple(range(9))
        whole = [
            call(functools.partial(plain_weight_kernel, taps), shape((9, cout, cout), BF16), grad_two, patches_two),
            call(functools.partial(plain_weight_kernel, taps), shape((9, cout, cin), BF16), grad_one, patches),
            call(functools.partial(plain_weight_kernel, (4,)), shape((1, cout, cin), BF16), grad_side, patches),
        ]
        dw_second, dw_first, dw_side = [
            lax.psum(lax.psum_scatter(value, "fsdp", scatter_dimension=1, tiled=True), "batch").astype(F32)
            for value in whole
        ]
        dw_side = dw_side[0]
        grad_late = grad_one
    *input_grads, shift_1, gain_1, gain_2, shift_2, gain_3, shift_3 = early_grads if fast else input_part(grad_late)

    def as_weight(value):
        return jnp.transpose(value.reshape(3, 3, owned, value.shape[2]), (0, 1, 3, 2))

    return (
        *[jnp.transpose(value, (2, 0, 1, 3)) for value in (*outputs, *input_grads)],
        as_weight(dw_first),
        gain_1[0],
        shift_1[0],
        as_weight(dw_second),
        gain_2[0],
        shift_2[0],
        jnp.transpose(dw_side),
        gain_3[0],
        shift_3[0],
    )


def solution(mesh):
    split = ("batch", "fsdp")
    image = P(split, None, None, None)
    kernel = P(None, None, None, "fsdp")
    vector = P("fsdp")
    in_specs = (image,) * 6 + (
        P(split, None),
        kernel,
        vector,
        vector,
        kernel,
        vector,
        vector,
        P(None, "fsdp"),
        vector,
        vector,
    )
    out_specs = (image,) * 6 + (
        kernel,
        vector,
        vector,
        kernel,
        vector,
        vector,
        P(None, "fsdp"),
        vector,
        vector,
    )
    body = functools.partial(local, batch=mesh.shape["batch"], fsdp=mesh.shape["fsdp"])
    return jax.shard_map(body, mesh=mesh, in_specs=in_specs, out_specs=out_specs, check_vma=False)
```

```python
import functools

import jax
import jax.numpy as jnp
import numpy as np
from jax import lax
from jax.experimental import pallas as pl
from jax.experimental.pallas import tpu as pltpu
from jax.sharding import PartitionSpec as P

EPSILON = 1e-05
F32 = jnp.float32
BF16 = jnp.bfloat16
ROWS = 16
VMEM_LIMIT = 30 * 2**20


def up(value, step):
    return -(-value // step) * step


class Plan:
    def __init__(self, sides, slots):
        self.sides, self.slots = sides, slots
        self.starts, self.sizes, row = [], [], 0
        for index, side in enumerate(sides):
            width = side + 1
            after = sides[index + 1] + 1 if index + 1 < len(sides) else 0
            size = up(slots * (width * width + max(0, width + 1 - after)), ROWS)
            self.starts.append(row)
            self.sizes.append(size)
            row += size
        self.rows = row
        self.margin = up(slots * (max(sides) + 2), ROWS)
        self.span = self.rows + 2 * self.margin

    def segments(self):
        return list(zip(self.starts, self.sizes, [side + 1 for side in self.sides]))


    def cells(self):
        for group, (start, side) in enumerate(zip(self.starts, self.sides)):
            for down in range(side):
                for right in range(side):
                    yield group, down, right, start + self.slots * ((down + 1) * (side + 1) + right + 1)


def nn(left, right):
    return lax.dot_general(left, right, (((1,), (0,)), ((), ())), preferred_element_type=F32)


def nt(left, right):
    return lax.dot_general(left, right, (((1,), (1,)), ((), ())), preferred_element_type=F32)


def column(value):
    return jnp.sum(value, axis=0, keepdims=True)


def wide(mask_ref, channels):
    return jnp.concatenate([mask_ref[...]] * (channels // mask_ref.shape[1]), axis=1)


def silu_slope(value):
    gate = jax.nn.sigmoid(value)
    return gate * (1.0 + value * (1.0 - gate))


def norm(value, sums, row, total):
    center = sums[row : row + 1] / total
    spread = sums[row + 1 : row + 2] / total - center * center
    factor = lax.rsqrt(spread + EPSILON)
    return (value - center) * factor, factor


def put_rows(ref, rows):
    for index, row in enumerate(rows):
        ref[index : index + 1, :] = row
    if len(rows) < ref.shape[0]:
        ref[len(rows) :, :] = jnp.zeros((ref.shape[0] - len(rows), ref.shape[1]), F32)


def offsets(plan, width):
    return [plan.slots * (dy * width + dx) for dy in (-1, 0, 1) for dx in (-1, 0, 1)]


def unfold(plan, padded_ref, out_ref, sign):
    channels = padded_ref.shape[1]
    for start, size, width in plan.segments():
        for tap, offset in enumerate(offsets(plan, width)):
            first = plan.margin + start + sign * offset
            out_ref[start : start + size, tap * channels : (tap + 1) * channels] = padded_ref[
                first : first + size, :
            ].astype(BF16)


def fill(plan, padded_ref, value):
    edge = jnp.zeros((plan.margin, padded_ref.shape[1]), F32)
    padded_ref[: plan.margin, :] = edge
    padded_ref[plan.margin : plan.margin + plan.rows, :] = value
    padded_ref[plan.margin + plan.rows :, :] = edge


def prepare_kernel(plan, owned, place_ref, counts_ref, *refs):
    fields, cots, vectors = refs[:3], refs[3:6], refs[6:12]
    patches_ref, cot_ref, mask_ref, vec_ref, held_ref = refs[12:]
    slots, channels = plan.slots, fields[0].shape[3]
    held_ref[...] = jnp.zeros(held_ref.shape, F32)
    cot_ref[...] = jnp.zeros(cot_ref.shape, F32)
    mask_ref[...] = jnp.zeros(mask_ref.shape, F32)
    cout = vec_ref.shape[1]
    first = (place_ref[2] * 2 + place_ref[0]) * owned
    spot = lax.broadcasted_iota(jnp.int32, (owned, cout), 1) - lax.broadcasted_iota(jnp.int32, (owned, cout), 0)
    own = ((spot == first) & (place_ref[1] == 0)).astype(BF16)
    held = [ref[...].astype(F32) for ref in vectors] + [jnp.zeros((vec_ref.shape[0] - 6, owned), F32)]
    vec_ref[...] = nn(jnp.concatenate(held, axis=0).astype(BF16), own)
    slot = lax.broadcasted_iota(jnp.int32, (slots, mask_ref.shape[1]), 0)
    live = [(slot < counts_ref[0, group]).astype(F32) for group in range(3)]
    for group, down, right, row in plan.cells():
        mask_ref[row : row + slots, :] = live[group]
        cot_ref[row : row + slots, :] = cots[group][down, right].astype(F32)
        for py in range(2):
            for px in range(2):
                first = plan.margin + row
                held_ref[2 * py + px, first : first + slots, :] = fields[group][2 * down + py, 2 * right + px].astype(F32)
    for start, size, width in plan.segments():
        for ky in range(3):
            for kx in range(3):
                tap = ky * 3 + kx
                shift = plan.slots * (width * (ky == 0) + (kx == 0))
                first = plan.margin + start - shift
                patches_ref[start : start + size, tap * channels : (tap + 1) * channels] = held_ref[
                    2 * (ky != 1) + (kx != 1), first : first + size, :
                ].astype(BF16)


def first_kernel(patches_ref, mask_ref, vec_ref, weights_ref, ready, first_ref, side_ref, sums_ref):
    ready()
    cin = weights_ref.shape[2]
    cout = weights_ref.shape[1]
    total = nt(patches_ref[:, :cin], weights_ref[0])
    for tap in range(1, 9):
        total += nt(patches_ref[:, tap * cin : (tap + 1) * cin], weights_ref[tap])
    side = nt(patches_ref[:, 4 * cin : 5 * cin], weights_ref[9])
    first_ref[...] = total
    side_ref[...] = side
    mask = wide(mask_ref, cout)
    put_rows(
        sums_ref,
        [
            column(mask * total),
            column(mask * total * total),
            column(mask * side),
            column(mask * side * side),
            column(mask),
            vec_ref[0:1],
            vec_ref[1:2],
        ],
    )


def second_kernel(
    plan, sums_ref, got_ref, first_ref, mask_ref, vec_ref, weights_ref, ready, second_ref, patches_ref, out_ref, held_ref
):
    cout = first_ref.shape[1]
    mask = wide(mask_ref, cout)
    sums = sums_ref[...] + got_ref[...]
    normed, _ = norm(first_ref[...], sums, 0, sums[4:5])
    pre = normed * sums[5:6] + sums[6:7]
    fill(plan, held_ref, jax.nn.silu(pre) * mask)
    unfold(plan, held_ref, patches_ref, 1)
    ready()
    total = nt(patches_ref[:, :cout], weights_ref[0])
    for tap in range(1, 9):
        total += nt(patches_ref[:, tap * cout : (tap + 1) * cout], weights_ref[tap])
    second_ref[...] = total
    put_rows(
        out_ref, [column(mask * total), column(mask * total * total)] + [vec_ref[row : row + 1] for row in range(2, 6)]
    )


def output_kernel(
    plan, sums_ref, got_ref, sums_two_ref, got_two_ref, second_ref, side_ref, cot_ref, mask_ref, *refs
):
    outs, (dz_ref, sums_out_ref) = refs[:3], refs[3:]
    cout = second_ref.shape[1]
    mask = wide(mask_ref, cout)
    sums, sums_two = sums_ref[...] + got_ref[...], sums_two_ref[...] + got_two_ref[...]
    total = sums[4:5]
    normed_two, _ = norm(second_ref[...], sums_two, 0, total)
    normed_side, _ = norm(side_ref[...], sums, 2, total)
    value = (normed_two * sums_two[2:3] + sums_two[3:4]) + (normed_side * sums_two[4:5] + sums_two[5:6])
    gate = jax.nn.sigmoid(value)
    out = (value * gate * mask).astype(BF16)
    for group, down, right, row in plan.cells():
        outs[group][down, right] = out[row : row + plan.slots, :]
    grad = cot_ref[...] * mask * (gate * (1.0 + value * (1.0 - gate)))
    dz_ref[...] = grad
    total = column(grad)
    put_rows(sums_out_ref, [total, column(grad * normed_two), column(grad * normed_side), total])


def back_second_kernel(
    plan, sums_ref, got_ref, sums_two_ref, got_two_ref, sums_z_ref, got_z_ref,
    first_ref, second_ref, side_ref, dz_ref, mask_ref, weights_ref, ready,
    grad_two_ref, grad_side_ref, dy_ref, out_ref, held_ref, patches_ref,
):
    cout = first_ref.shape[1]
    mask = wide(mask_ref, cout)
    sums, sums_two = sums_ref[...] + got_ref[...], sums_two_ref[...] + got_two_ref[...]
    sums_z = sums_z_ref[...] + got_z_ref[...]
    total = sums[4:5]
    grad = dz_ref[...]
    normed, factor = norm(second_ref[...], sums_two, 0, total)
    two = sums_two[2:3] * factor * (grad - mask * (sums_z[0:1] + normed * sums_z[1:2]) / total)
    normed, factor = norm(side_ref[...], sums, 2, total)
    side = sums_two[4:5] * factor * (grad - mask * (sums_z[0:1] + normed * sums_z[2:3]) / total)
    grad_side_ref[...] = side.astype(BF16)
    grad_two_ref[...] = two.astype(BF16)
    fill(plan, held_ref, two)
    unfold(plan, held_ref, patches_ref, -1)
    ready()
    back = nn(patches_ref[:, :cout], weights_ref[0])
    for tap in range(1, 9):
        back += nn(patches_ref[:, tap * cout : (tap + 1) * cout], weights_ref[tap])
    normed, _ = norm(first_ref[...], sums, 0, total)
    pre = normed * sums[5:6] + sums[6:7]
    grad = back * silu_slope(pre) * mask
    dy_ref[...] = grad
    put_rows(out_ref, [column(grad), column(grad * normed)])


def back_first(sums_ref, got_ref, sums_y_ref, got_y_ref, first_ref, dy_ref, mask_ref, grad_ref):
    cout = first_ref.shape[1]
    mask = wide(mask_ref, cout)
    sums, sums_y = sums_ref[...] + got_ref[...], sums_y_ref[...] + got_y_ref[...]
    total = sums[4:5]
    normed, factor = norm(first_ref[...], sums, 0, total)
    grad = sums[5:6] * factor * (dy_ref[...] - mask * (sums_y[0:1] + normed * sums_y[1:2]) / total)
    grad_ref[...] = grad.astype(BF16)


class Order:
    def __init__(self, batch, fsdp, owned):
        self.zs, self.quarter, self.owned = fsdp // 2, owned // batch, owned
        half = self.zs // 2
        self.blocks = [(b, z) for b in (0, 2, 1, 3) for z in range(half)]
        self.blocks += [(b, z) for b in (0, 1, 2, 3) for z in range(half, self.zs)]

    def share(self, place_ref, grad_refs, keep_ref, send_ref, turned_ref):
        core, b, z = place_ref[0], place_ref[1], place_ref[2]
        for index, grad_ref in enumerate(grad_refs):
            turned_ref[...] = grad_ref[...].T
            for rel_core, out_ref in enumerate((keep_ref, send_ref)):
                for block, (rel_b, rel_z) in enumerate(self.blocks):
                    row = ((z ^ rel_z) * 2 + (core ^ rel_core)) * self.owned + (b ^ rel_b) * self.quarter
                    rows = pl.ds(pl.multiple_of(row, self.quarter), self.quarter)
                    first = (index * len(self.blocks) + block) * self.quarter
                    out_ref[first : first + self.quarter, :] = turned_ref[rows, :]

    def correlate(self, grads, patch_refs, first, size, tap, out_refs):
        value = sum(nn(grad, ref[:, first : first + size]) for grad, ref in zip(grads, patch_refs)).astype(BF16)
        begin = 0
        for out_ref in out_refs:
            count = out_ref.shape[0]
            out_ref[:, tap] = value[begin : begin + count * self.quarter].reshape(count, self.quarter, size)
            begin += count * self.quarter


def back_second_share_kernel(plan, order, place_ref, *refs):
    inputs, (grad_side_ref, dy_ref, out_ref, keep_ref, send_ref) = refs[:13], refs[13:18]
    held_ref, patches_ref, turned_ref, grad_two_ref = refs[18:]
    back_second_kernel(plan, *inputs, grad_two_ref, grad_side_ref, dy_ref, out_ref, held_ref, patches_ref)
    order.share(place_ref, [grad_two_ref], keep_ref, send_ref, turned_ref)


def share_kernel_of(order, place_ref, grad_ref, keep_ref, send_ref, turned_ref):
    order.share(place_ref, [grad_ref], keep_ref, send_ref, turned_ref)


def back_first_share_kernel(order, place_ref, *refs):
    back_first(*refs[:8])
    order.share(place_ref, refs[7:8], refs[8], refs[9], refs[10])


def weight_second_kernel(order, part, keep_ref, got_ref, patches_ref, other_ref, out_ref):
    cout = patches_ref.shape[1] // 9
    grads = [ref[part * cout // 4 : (part + 1) * cout // 4] for ref in (keep_ref, got_ref)]
    for tap in range(9):
        order.correlate(grads, (patches_ref, other_ref), tap * cout, cout, tap, [out_ref])


def weight_first_kernel(order, keep_ref, got_ref, side_keep_ref, side_got_ref, patches_ref, other_ref, *outs):
    cin = patches_ref.shape[1] // 9
    grads = [keep_ref[...], got_ref[...]]
    for tap in range(9):
        order.correlate(grads, (patches_ref, other_ref), tap * cin, cin, tap, outs)
    grads = [side_keep_ref[...], side_got_ref[...]]
    order.correlate(grads, (patches_ref, other_ref), 4 * cin, cin, 9, outs)


def plain_weight_kernel(taps, grad_ref, patches_ref, out_ref):
    turned = grad_ref[...].T
    channels = out_ref.shape[2]
    for index, tap in enumerate(taps):
        out_ref[index] = nn(turned, patches_ref[:, tap * channels : (tap + 1) * channels]).astype(BF16)


def input_kernel(
    plan, owned, place_ref, sums_z_ref, got_z_ref, sums_y_ref, got_y_ref, grad_ref, side_ref, weights_ref, ready, *refs
):
    outs, owns, (held_ref, moved_ref, total_ref) = refs[:3], refs[3:9], refs[9:]
    ready()
    sums = jnp.concatenate([sums_z_ref[...] + got_z_ref[...], sums_y_ref[...] + got_y_ref[...]], axis=0)
    first = (place_ref[2] * 2 + place_ref[0]) * owned
    spot = lax.broadcasted_iota(jnp.int32, sums.shape, 1)
    sums = jnp.where((spot >= first) & (spot < first + owned), sums, 0.0)
    sums = sum(sums[:, begin : begin + owned] for begin in range(0, sums.shape[1], owned))
    for row, ref in zip((4, 5, 1, 0, 2, 3), owns):
        ref[...] = sums[row : row + 1]
    rows = plan.rows
    fill(plan, held_ref, grad_ref[...].astype(F32))
    for index, (down, right) in enumerate(((0, 0), (0, 1), (1, 0), (1, 1))):
        for start, size, width in plan.segments():
            first = plan.margin + start + plan.slots * (down * width + right)
            moved_ref[index, start : start + size, :] = held_ref[first : first + size, :].astype(BF16)
    for py in range(2):
        for px in range(2):
            total = None
            for ky in (0, 2) if py else (1,):
                for kx in (0, 2) if px else (1,):
                    index = 2 * (ky == 0) + (kx == 0)
                    term = nn(moved_ref[index], weights_ref[ky * 3 + kx])
                    total = term if total is None else total + term
            if py + px == 0:
                total += nn(side_ref[...], weights_ref[9])
            total_ref[...] = total
            for group, down, right, row in plan.cells():
                outs[group][2 * down + py, 2 * right + px] = total_ref[row : row + plan.slots, :].astype(BF16)


def finish_kernel(order, place_ref, *refs):
    parts, outs = refs[:4], refs[4:]
    b, quarter = place_ref[1], order.quarter
    taps = outs[0].shape[0]
    for rel, ref in enumerate(parts):
        rows = pl.ds(pl.multiple_of((b ^ rel) * quarter, quarter), quarter)
        outs[0][:, rows, :] = ref[:taps].astype(F32)
        if len(outs) > 1:
            outs[1][rows, :] = ref[taps].astype(F32)


class Gathered:
    def __init__(self, arrays, place=None, order=None, labels=()):
        self.arrays, self.place, self.order, self.labels = arrays, place, order, labels
        self.taps = max((label[2] + label[3] for label in labels), default=0)

    def dims(self):
        if self.order is None:
            return self.arrays[0].shape
        return self.taps, 2 * self.order.zs * self.order.owned, self.arrays[0].shape[-1]

    def wrap(self, body, scalars, count):
        if self.order is None:
            return lambda *refs: body(*refs[: count + 1], lambda: None, *refs[count + 1 :])
        order, many, labels = self.order, len(self.arrays), self.labels

        def whole(place_ref, *refs):
            inputs, bundles, rest = refs[:count], refs[count : count + many], refs[count + many :]
            weights_ref, outs, semaphores = rest[0], rest[1:-1], rest[-1]
            core, b, z = place_ref[0], place_ref[1], place_ref[2]
            copies = []
            for index, at, tap, taps, rel_core, owner, quarter in labels:
                row = (owner(z) * 2 + (core ^ rel_core)) * order.owned + quarter(b) * order.quarter
                rows = pl.ds(pl.multiple_of(row, order.quarter), order.quarter)
                target = weights_ref.at[pl.ds(tap, taps), rows, :]
                copies.append(pltpu.make_async_copy(bundles[index].at[at], target, semaphores.at[len(copies)]))
            for copy in copies:
                copy.start()

            def ready():
                for copy in copies:
                    copy.wait()

            body(*inputs, weights_ref, ready, *outs)

        return whole


def call(body, out_shapes, *args, scratch=(), scalars=0, weights=None, far=False, whole=True):
    vmem = pl.BlockSpec(memory_space=pltpu.VMEM)
    inner = vmem if whole else pl.BlockSpec(memory_space=pltpu.MemorySpace.HBM)
    if far:
        args = args[:scalars] + tuple(
            pltpu.with_memory_space_constraint(arg, pltpu.MemorySpace.HBM) for arg in args[scalars:]
        )
    specs = [pl.BlockSpec(memory_space=pltpu.SMEM)] * scalars + [inner] * (len(args) - scalars)
    if weights is not None:
        body = weights.wrap(body, scalars, len(args))
        scratch = list(scratch)
        if weights.order is None:
            args = args + tuple(weights.arrays)
            specs = specs + [vmem]
        else:
            args = (weights.place,) + args + tuple(weights.arrays)
            specs = [pl.BlockSpec(memory_space=pltpu.SMEM)] + specs + [pl.BlockSpec(memory_space=pl.ANY)] * len(weights.arrays)
            out_shapes = [shape(weights.dims(), BF16)] + list(out_shapes)
            scratch += [pltpu.SemaphoreType.DMA((len(weights.labels),))]
    many = isinstance(out_shapes, (list, tuple))
    return pl.pallas_call(
        body,
        in_specs=specs,
        out_specs=[vmem] * len(out_shapes) if many else vmem,
        out_shape=list(out_shapes) if many else out_shapes,
        scratch_shapes=list(scratch),
        compiler_params=pltpu.CompilerParams(vmem_limit_bytes=VMEM_LIMIT),
        cost_estimate=pl.CostEstimate(flops=0, bytes_accessed=0, transcendentals=0),
    )(*args)


def shape(dims, dtype=F32):
    return jax.ShapeDtypeStruct(tuple(dims), dtype)


def exchange(value, axis, count, bit):
    return lax.ppermute(value, axis, [(index, index ^ bit) for index in range(count)])


def bits(count):
    return [1 << index for index in range(count.bit_length() - 1)]


def after(value, *others):
    return lax.optimization_barrier((value, *others))[0]


def together(*values):
    return list(lax.optimization_barrier(values))


def steps_of(axes):
    return [(axis, count, bit) for axis, count in axes for bit in bits(count)]


def sum_over(value, steps, hooks=None):
    got = jnp.zeros_like(value)
    for index, (axis, count, bit) in enumerate(steps):
        if index:
            value = value + got
        if hooks and index in hooks:
            value = hooks[index](value)
        got = exchange(value, axis, count, bit)
    return value, got


def parity(b):
    return (b ^ (b // 2)) % 2


def rotated(rel):
    return lambda own: own ^ rel


def of_half(other, index):
    return lambda b: 2 * (parity(b) ^ other) + index


def share_kernel(order, place_ref, first_ref, side_ref, second_ref, first_out_ref, second_out_ref, semaphores):
    b, size, copies = place_ref[1], order.quarter, []

    def copy(source, target):
        copies.append(pltpu.make_async_copy(source, target, semaphores.at[len(copies)]))
        copies[-1].start()

    rows = pl.ds(pl.multiple_of(b * size, size), size)
    copy(first_ref.at[:, rows, :], first_out_ref.at[pl.ds(0, 9)])
    copy(side_ref.at[rows, :], first_out_ref.at[9])
    for index in range(2):
        rows = pl.ds(pl.multiple_of((2 * parity(b) + index) * size, size), size)
        copy(second_ref.at[:, rows, :], second_out_ref.at[index])
    for started in copies:
        started.wait()


def spread_line(order, share, fsdp):
    return jnp.stack([share] + [exchange(share, "fsdp", fsdp, 2 * rel) for rel in range(1, order.zs)])


def both_cores(bundles, fsdp):
    return bundles + [exchange(value, "fsdp", fsdp, 1) for value in bundles]


def spread_quarters(line, batch):
    return [line] + [exchange(line, "batch", batch, rel) for rel in (1, 2, 3)]


def quarter_labels(order, taps):
    labels = []
    for core in range(2):
        for rel in range(4):
            for step in range(order.zs):
                labels.append((4 * core + rel, step, 0, taps, core, rotated(step), rotated(rel)))
    return labels


def to_plane(halves, batch):
    return [exchange(halves[0], "batch", batch, 1), exchange(halves[1], "batch", batch, 2)]


def half_labels():
    labels = []
    for core in range(2):
        for rel in range(4):
            for index in range(2):
                own, other = of_half(0, index), of_half(1, index)
                labels.append((3 * core, (index, rel), 0, 9, core, rotated(rel), own))
                bundle, at = (1, (index, rel)) if rel < 3 else (2, index)
                labels.append((3 * core + bundle, at, 0, 9, core, rotated(rel), other))
    return labels


def assemble_kernel(weights_ref, ready):
    ready()


def reduce_line(pieces, fsdp):
    total = pieces[0].astype(F32)
    for rel in range(1, len(pieces)):
        total = total + exchange(pieces[rel], "fsdp", fsdp, 2 * rel).astype(F32)
    return total


def first_in_plane(halves, batch):
    half_p, half_q = halves
    n_p, n_q = half_p.shape[0] // 2, half_q.shape[0] // 2
    got_p = exchange(half_p[n_p:], "batch", batch, 1)
    got_q = exchange(half_q[n_q:], "batch", batch, 2)
    return [half_p[:n_p] + got_p, half_q[:n_q] + got_q]


def then_in_plane(halves, batch):
    half_p, half_q = halves
    n_p, n_q = half_p.shape[0] // 2, half_q.shape[0] // 2
    got_p = exchange(half_p[n_p:], "batch", batch, 2)
    got_q = exchange(half_q[n_q:], "batch", batch, 1)
    low, high = half_p[:n_p] + got_p, half_q[:n_q] + got_q
    return [low[index] for index in range(n_p)] + [high[index] for index in range(n_q)]


def finish_weights(order, place, quarter, batch, outs):
    quarter = quarter.astype(BF16)
    spread = [quarter] + [exchange(quarter, "batch", batch, rel) for rel in (1, 2, 3)]
    return call(functools.partial(finish_kernel, order), outs, place, *spread, scalars=1)


def local(
    x_small,
    x_mid,
    x_large,
    cot_small,
    cot_mid,
    cot_large,
    counts,
    w_first,
    gain_first,
    shift_first,
    w_second,
    gain_second,
    shift_second,
    w_short,
    gain_short,
    shift_short,
    *,
    batch,
    fsdp,
):
    fields = (x_small, x_mid, x_large)
    cots = (cot_small, cot_mid, cot_large)
    slots, cin, owned = x_small.shape[0], x_small.shape[3], gain_first.shape[0]
    cout = owned * fsdp
    plan = Plan([cot.shape[1] for cot in cots], slots)
    rows, span = plan.rows, plan.span
    everywhere = steps_of((("fsdp", fsdp), ("batch", batch)))
    me = lax.axis_index("fsdp")
    fast = batch == 4 and fsdp == 8 and owned % (ROWS * batch) == 0
    order = Order(batch, fsdp, owned) if fast else None
    place = jnp.stack([me % 2, lax.axis_index("batch"), me // 2]).astype(jnp.int32)

    own_first = jnp.transpose(w_first, (0, 1, 3, 2)).reshape(9, owned, cin)
    own_second = jnp.transpose(w_second, (0, 1, 3, 2)).reshape(9, owned, cout)
    own_side = jnp.transpose(w_short)
    vectors = [gain_first, shift_first, gain_second, shift_second, gain_short, shift_short]
    patches, cot_rows, mask, vec = call(
        functools.partial(prepare_kernel, plan, owned),
        [shape((rows, 9 * cin), BF16), shape((rows, cout)), shape((rows, 128)), shape((8, cout))],
        place,
        counts,
        *[jnp.transpose(value, (1, 2, 0, 3)) for value in fields + cots],
        *[value.reshape(1, owned) for value in vectors],
        scratch=[pltpu.VMEM((4, plan.margin + rows, cin), F32)],
        scalars=2,
        far=True,
    )
    if fast:
        share_first, share_second = call(
            functools.partial(share_kernel, order),
            [shape((10, order.quarter, cin), BF16), shape((2, 9, order.quarter, cout), BF16)],
            place,
            own_first,
            own_side,
            own_second,
            scratch=[pltpu.SemaphoreType.DMA((4,))],
            scalars=1,
            far=True,
            whole=False,
        )
        line_first = after(spread_line(order, share_first, fsdp), patches, vec)
        plane_first = spread_quarters(line_first, batch)
        kern_first = Gathered(both_cores(plane_first, fsdp), place, order, quarter_labels(order, 10))
        share_second = after(share_second, line_first)
        near, far = [exchange(share_second, "fsdp", fsdp, bit) for bit in (2, 4)]
        last = exchange(far, "fsdp", fsdp, 2)
        front = jnp.stack(together(share_second, near, far, *plane_first[1:])[:3], axis=1)
        front_plane = to_plane(front, batch)
    else:
        kern_first = Gathered([lax.all_gather(jnp.concatenate([own_first, own_side[None]]), "fsdp", axis=1, tiled=True)])
        kern_second = Gathered([lax.all_gather(own_second, "fsdp", axis=1, tiled=True)])
    if fast:
        kern_first = Gathered(call(assemble_kernel, [], weights=kern_first))
    first, side, sums = call(
        first_kernel,
        [shape((rows, cout)), shape((rows, cout)), shape((8, cout))],
        patches,
        mask,
        vec,
        weights=kern_first,
    )
    if fast:
        held, whole = [last], []

        def over_last(value):
            value, held[0] = together(value, last)
            held.append(to_plane(held[0], batch))
            return value

        def assemble(value):
            value, piece, *planes = together(value, held[0], *front_plane, *held[1])
            line = jnp.concatenate([front, piece[:, None]], axis=1)
            bundles = both_cores([line, jnp.stack(planes[:2]), jnp.stack(planes[2:])], fsdp)
            whole.extend(call(assemble_kernel, [], weights=Gathered(bundles, place, order, half_labels())))
            return value

        hooks = {2: over_last, 3: assemble}
        sums = sum_over(sums, everywhere, hooks)
        kern_second = Gathered(whole)
        everywhere = everywhere[:1] + everywhere[-2:] + everywhere[1:-2]
    else:
        sums = sum_over(sums, everywhere)
    second, patches_two, sums_two = call(
        functools.partial(second_kernel, plan),
        [shape((rows, cout)), shape((rows, 9 * cout), BF16), shape((8, cout))],
        *sums,
        first,
        mask,
        vec,
        scratch=[pltpu.VMEM((span, cout), F32)],
        weights=kern_second,
    )
    def to_other_core(array, into):
        def begin(value):
            into.append(exchange(after(array, value), "fsdp", fsdp, 1))
            return value

        def end(value):
            value, into[0] = together(value, into[0])
            return value

        return {1: begin, 4: end} if fast else None

    other_two, other_one = [], []
    sums_two = sum_over(sums_two, everywhere, to_other_core(patches_two, other_two))
    *outputs, dz, sums_z = call(
        functools.partial(output_kernel, plan),
        [shape((length, length, slots, cout), BF16) for length in plan.sides] + [shape((rows, cout)), shape((4, cout))],
        *sums,
        *sums_two,
        second,
        side,
        cot_rows,
        mask,
    )
    sums_z = sum_over(sums_z, everywhere, to_other_core(patches, other_one))
    shared = []
    if fast:
        turned = pltpu.VMEM((cout, rows), BF16)
        shared = [shape((cout // 2, rows), BF16)] * 2
    results = call(
        functools.partial(back_second_share_kernel, plan, order) if fast else functools.partial(back_second_kernel, plan),
        ([] if fast else [shape((rows, cout), BF16)])
        + [shape((rows, cout), BF16), shape((rows, cout)), shape((4, cout))]
        + shared,
        *([place] if fast else []),
        *sums,
        *sums_two,
        *sums_z,
        first,
        second,
        side,
        dz,
        mask,
        scratch=[pltpu.VMEM((span, cout), F32), pltpu.VMEM((rows, 9 * cout), BF16)] + ([turned, pltpu.VMEM((rows, cout), BF16)] if fast else []),
        scalars=int(fast),
        weights=kern_second,
    )
    hooks = None
    if fast:
        grad_side, dy, sums_y, keep, send = results
        got, halves_two, sides = [], [], []

        def begin_second(value):
            got.append(exchange(after(send, value), "fsdp", fsdp, 1))
            return value

        def weights_second(value, part):
            half = (len(order.blocks) // 2, 9, order.quarter, cout)
            halves_two.append(
                call(
                    functools.partial(weight_second_kernel, order, part),
                    shape(half, BF16),
                    after(keep, value),
                    got[0],
                    patches_two,
                    other_two[0],
                )
            )
            return value

        def over_x(value):
            value, halves_two[0] = together(value, halves_two[0])
            return value

        def over_y(value):
            value, halves_two[1] = together(value, halves_two[1])
            return value

        def begin(value):
            return weights_second(begin_second(value), 0)

        def between(value):
            return weights_second(over_x(value), 1)

        def share_side(value):
            value = over_y(value)
            shares = call(
                functools.partial(share_kernel_of, order),
                [shape((cout // 2, rows), BF16)] * 2,
                place,
                after(grad_side, value),
                scratch=[turned],
                scalars=1,
            )
            sides.extend([shares[0], exchange(shares[1], "fsdp", fsdp, 1)])
            return value

        hooks = {1: begin, 2: between, 3: share_side, 4: lambda value: after(value, *sides)}
    else:
        grad_two, grad_side, dy, sums_y = results
    sums_y = sum_over(sums_y, everywhere, hooks)
    def input_part(grad_late):
        return call(
            functools.partial(input_kernel, plan, owned),
            [shape((2 * length, 2 * length, slots, cin), BF16) for length in plan.sides] + [shape((1, owned))] * 6,
            place,
            *sums_z,
            *sums_y,
            grad_late,
            grad_side,
            scratch=[pltpu.VMEM((span, cout), F32), pltpu.VMEM((4, rows, cout), BF16), pltpu.VMEM((rows, cin), F32)],
            scalars=1,
            weights=kern_first,
        )
    if fast:
        grad_one, keep_one, send_one = call(
            functools.partial(back_first_share_kernel, order),
            [shape((rows, cout), BF16)] + [shape((cout // 2, rows), BF16)] * 2,
            place,
            *sums,
            *sums_y,
            first,
            dy,
            mask,
            scratch=[turned],
            scalars=1,
        )
        halves_two = first_in_plane(halves_two, batch)
        got_one = exchange(send_one, "fsdp", fsdp, 1)
        keep_one, halves_two[0] = together(keep_one, halves_two[0])
        half = (len(order.blocks) // 2, 10, order.quarter, cin)
        halves_one = call(
            functools.partial(weight_first_kernel, order),
            [shape(half, BF16)] * 2,
            keep_one,
            got_one,
            *sides,
            patches,
            other_one[0],
        )
        *halves_one, halves_two[1] = together(*halves_one, halves_two[1])
        halves_one = first_in_plane(halves_one, batch)
        early_grads = input_part(after(grad_one, *halves_one))
        quarter_two = reduce_line(then_in_plane(halves_two, batch), fsdp)
        pieces_one = together(*then_in_plane(halves_one, batch), early_grads[3])[:-1]
        quarter_one = reduce_line(pieces_one, fsdp)
        dw_second = finish_weights(order, place, quarter_two, batch, [shape((9, owned, cout))])[0]
        dw_first, dw_side = finish_weights(
            order, place, quarter_one, batch, [shape((9, owned, cin)), shape((owned, cin))]
        )
    else:
        grad_one = call(back_first, shape((rows, cout), BF16), *sums, *sums_y, first, dy, mask)
        taps = tuple(range(9))
        whole = [
            call(functools.partial(plain_weight_kernel, taps), shape((9, cout, cout), BF16), grad_two, patches_two),
            call(functools.partial(plain_weight_kernel, taps), shape((9, cout, cin), BF16), grad_one, patches),
            call(functools.partial(plain_weight_kernel, (4,)), shape((1, cout, cin), BF16), grad_side, patches),
        ]
        dw_second, dw_first, dw_side = [
            lax.psum(lax.psum_scatter(value, "fsdp", scatter_dimension=1, tiled=True), "batch").astype(F32)
            for value in whole
        ]
        dw_side = dw_side[0]
        grad_late = grad_one
    *input_grads, shift_1, gain_1, gain_2, shift_2, gain_3, shift_3 = early_grads if fast else input_part(grad_late)

    def as_weight(value):
        return jnp.transpose(value.reshape(3, 3, owned, value.shape[2]), (0, 1, 3, 2))

    return (
        *[jnp.transpose(value, (2, 0, 1, 3)) for value in (*outputs, *input_grads)],
        as_weight(dw_first),
        gain_1[0],
        shift_1[0],
        as_weight(dw_second),
        gain_2[0],
        shift_2[0],
        jnp.transpose(dw_side),
        gain_3[0],
        shift_3[0],
    )


def solution(mesh):
    split = ("batch", "fsdp")
    image = P(split, None, None, None)
    kernel = P(None, None, None, "fsdp")
    vector = P("fsdp")
    in_specs = (image,) * 6 + (
        P(split, None),
        kernel,
        vector,
        vector,
        kernel,
        vector,
        vector,
        P(None, "fsdp"),
        vector,
        vector,
    )
    out_specs = (image,) * 6 + (
        kernel,
        vector,
        vector,
        kernel,
        vector,
        vector,
        P(None, "fsdp"),
        vector,
        vector,
    )
    body = functools.partial(local, batch=mesh.shape["batch"], fsdp=mesh.shape["fsdp"])
    return jax.shard_map(body, mesh=mesh, in_specs=in_specs, out_specs=out_specs, check_vma=False)
```
